32 devices in a mesh: kp: 4 (over y, x), ga: 8 (over z, core).
Axes of the slice: x: 2, y: 2, z: 4, core: 2. Of those that a mesh axis runs over, the one named last changes fastest.
Arguments:
- densities: bfloat16 [8, 2, 3072, 256], P('kp', None, 'ga'), may hold values from -6 to 6
- screened: bfloat16 [8, 2, 3072, 3072], P('kp', None, 'ga'), may hold values from -3 to 3, as said below
- coulomb: float32 [3072], P('ga'), may hold values from 0.05 to 1
- block_rows: int32 [4, 2], P('kp'), may hold values from 0 to 6, as said below
Outputs:
- kernel: float32 [8, 2, 2, 256, 256], P('kp', None, None, 'ga')
- mirror: float32 [8, 2, 2, 256, 256], P('kp', None, None, 'ga')
The draws below stay inside these ranges and needn't reach their ends.
Inputs may be any that keep to these rules, and one draw needn't show every extreme that they name: block_rows[o, j] + 2 o + 1 <= 7, so every column k-point exists. Each panel screened[q] is Hermitian: its real part symmetric, its imaginary part antisymmetric.
All inputs are finite; a program needn't handle non-finite values.
Results may differ from the reference program's by a relative error of at most 0.0032.
Values may be sent and summed in bfloat16 or wider, within the bound.
No kernel may reach another device: no remote copies, remote signals or barrier semaphores. Data moves between devices by JAX's collectives and lax.ppermute only.
A program may use at most 64 MiB of HBM per device.

```python
import math
import jax
import jax.numpy as jnp
from jax import lax

G = 3072
NT = 256
KD = 2
KB = 2
NK = 8
N_KP = 4


def draw_screened(key, part):
    key = jax.random.fold_in(key, 5)
    first, second = jax.random.split(key)
    noise = jax.random.normal(first, (NK, 2, G, G), jnp.float32)
    noise = noise * G ** (-0.5)
    sym_part = (noise[:, 0] + jnp.swapaxes(noise[:, 0], 1, 2)) * 0.7071
    anti_part = (noise[:, 1] - jnp.swapaxes(noise[:, 1], 1, 2)) * 0.7071
    diag_values = jax.random.uniform(second, (NK, G), jnp.float32, 0.5, 2.0)
    identity = jnp.eye(G, dtype=jnp.float32)
    sym_part = sym_part + diag_values[:, :, None] * identity[None]
    return jnp.stack([sym_part, anti_part], 1).astype(jnp.bfloat16)


def draw_block_rows(key, part):
    key = jax.random.fold_in(key, 9)
    owners = jnp.arange(N_KP, dtype=jnp.int32)[:, None]
    upper = NK - KD * (owners + 1) + 1
    upper = jnp.broadcast_to(upper, (N_KP, KB))
    values = jax.random.randint(key, (N_KP, KB), 0, upper, dtype=jnp.int32)
    return values.at[0, KB - 1].set(NK - KD)


def block_scale(stream_key, shape, shards, least, top_value):
    gain, own = 1.0, jax.random.fold_in(stream_key, 6)
    for dim, blocks in shards:
        steps = jnp.exp(jax.random.uniform(jax.random.fold_in(own, dim), (blocks,), jnp.float32, least / len(shards), top_value / len(shards)))
        gain = gain * jnp.repeat(steps, shape[dim] // blocks).reshape([-1 if axis == dim else 1 for axis in range(len(shape))])
    return gain


def bell_draw(key, extent, scale, most, pieces=(), kind=jnp.bfloat16):
    level = block_scale(key, extent, pieces, -0.22, 0.18) if pieces else 1.0
    values = jax.random.normal(key, extent, jnp.float32) * scale * level
    return jnp.minimum(jnp.maximum(values, -most), most).astype(kind)


def setup_inputs(seed: int = 0) -> dict:
    seeds = jax.random.split(jax.random.key(seed), 5)
    densities = bell_draw(seeds[0], (NK, 2, G, NT), 1.0, 6.0, ((0, 4), (2, 8)))
    screened = draw_screened(jax.random.fold_in(seeds[4], 71), 0)
    coulomb = jnp.clip(jnp.exp(math.log(1.0) - 2.9957323 * jax.random.uniform(seeds[2], (G,), jnp.float32) ** block_scale(seeds[2], (G,), ((0, 8),), -0.2, 0.2)), 0.05, 1.0)
    block_rows = draw_block_rows(jax.random.fold_in(seeds[4], 71), 0)
    return dict(densities=densities, screened=screened, coulomb=coulomb, block_rows=block_rows)


def reference(densities, screened, coulomb, block_rows):
    inverse = 1.0 / math.sqrt(G)
    diagonal = jnp.diag(2.0 * coulomb.astype(jnp.float32))
    high = lax.Precision.HIGHEST

    def one_owner(owner):
        rows = block_rows[owner]
        transfers = owner * KD + jnp.arange(KD, dtype=jnp.int32)
        panel = lax.dynamic_slice_in_dim(screened, (owner * KD).astype(jnp.int32), KD, 0).astype(jnp.float32)
        screen_real = (diagonal[None] - panel[:, 0]).astype(jnp.bfloat16).astype(jnp.float32)
        screen_imag = (-panel[:, 1]).astype(jnp.bfloat16).astype(jnp.float32)
        near = densities[rows].astype(jnp.float32)
        far = densities[rows[:, None] + transfers[None, :]].astype(jnp.float32)
        near_real, near_imag = (near[:, 0], near[:, 1])
        image_real = jnp.einsum('sgh,jht->jsgt', screen_real, near_real, precision=high) - jnp.einsum('sgh,jht->jsgt', screen_imag, near_imag, precision=high)
        image_imag = jnp.einsum('sgh,jht->jsgt', screen_real, near_imag, precision=high) + jnp.einsum('sgh,jht->jsgt', screen_imag, near_real, precision=high)
        image_real = lax.optimization_barrier(image_real.astype(jnp.bfloat16)).astype(jnp.float32)
        image_imag = lax.optimization_barrier(image_imag.astype(jnp.bfloat16)).astype(jnp.float32)
        far_real, far_imag = (far[:, :, 0], far[:, :, 1])
        lower_real = jnp.einsum('jsga,jsgb->jsab', far_real, image_real, precision=high) + jnp.einsum('jsga,jsgb->jsab', far_imag, image_imag, precision=high)
        lower_imag = jnp.einsum('jsga,jsgb->jsab', far_real, image_imag, precision=high) - jnp.einsum('jsga,jsgb->jsab', far_imag, image_real, precision=high)
        mirror = jnp.stack([lower_real, lower_imag], 2) * inverse
        kernel = jnp.stack([jnp.swapaxes(mirror[:, :, 0], 2, 3), -jnp.swapaxes(mirror[:, :, 1], 2, 3)], 2)
        return (kernel, mirror)
    kernel, mirror = lax.map(one_owner, jnp.arange(N_KP, dtype=jnp.int32))
    shape = (N_KP * KB, KD, 2, NT, NT)
    return (kernel.reshape(shape), mirror.reshape(shape))
```

```python
import functools
import math

import jax
import jax.numpy as jnp
from jax import lax
from jax.experimental import pallas as pl
from jax.experimental.pallas import tpu as pltpu
from jax.sharding import PartitionSpec as P

F32 = jnp.float32
BF16 = jnp.bfloat16
LABELS = 16
VMEM = pl.BlockSpec(memory_space=pltpu.VMEM)
SMEM = pl.BlockSpec(memory_space=pltpu.SMEM)
HBM = pl.BlockSpec(memory_space=pltpu.HBM)


def dot(a, b):
    return jnp.dot(a, b, preferred_element_type=F32)


def tdot(a, b):
    return lax.dot_general(a, b, (((0,), (0,)), ((), ())), preferred_element_type=F32)


def run(body, out, *args, specs=None, scratch=(), name=None, aliases=None, mib=16):
    outs = out if isinstance(out, (list, tuple)) else [out]
    result = pl.pallas_call(
        body,
        in_specs=specs or [VMEM] * len(args),
        out_specs=[VMEM] * len(outs),
        out_shape=list(outs),
        scratch_shapes=list(scratch),
        input_output_aliases=aliases or {},
        compiler_params=pltpu.CompilerParams(vmem_limit_bytes=mib * 2**20),
        cost_estimate=pl.CostEstimate(flops=0, bytes_accessed=0, transcendentals=0),
        name=name,
    )(*args)
    return list(result) if isinstance(out, (list, tuple)) else result[0]


BITS = ((1, 2), (2, 1))


def pack_kernel(rows, densities, *sends):
    held, _, g_local, t = densities.shape
    half = g_local // 2
    for h in range(2):
        for k in range(held):
            for part in range(2):
                at = (2 * k + part) * half
                sends[h][at : at + half] = densities[k, part, h * half : (h + 1) * half]
        line = lax.broadcasted_iota(jnp.int32, (LABELS, t), 0)
        tile = jnp.zeros((LABELS, t), F32)
        for j in range(rows.shape[1]):
            tile = jnp.where(line == j, rows[0, j].astype(F32), tile)
        sends[h][2 * held * half :] = tile.astype(BF16)


def label_of(message, held, half, j):
    tail = message[2 * held * half :].astype(F32)
    return jnp.max(tail[j : j + 1]).astype(jnp.int32)


def entries(message, owner, held, half):
    return [(owner * held + k, message, 2 * k * half, (2 * k + 1) * half) for k in range(held)]


def copy_if(label, found, out):
    half = out.shape[1]
    hit = None
    for name, message, real, imag in found:
        match = label == name
        hit = match if hit is None else hit | match

        @pl.when(match)
        def _(message=message, real=real, imag=imag):
            out[0] = message[real : real + half]
            out[1] = message[imag : imag + half]

    return hit


def pick_kernel(held, packed_0, packed_1, came_0, came_1, *sends):
    owner = lax.axis_index("kp")
    packed, came = (packed_0, packed_1), (came_0, came_1)
    half = sends[0].shape[2]
    for j in range(sends[0].shape[0]):
        for h in range(2):
            found = entries(packed[h], owner, held, half)
            found += entries(came[h], owner ^ BITS[h][0], held, half)
            copy_if(label_of(came[1 - h], held, half, j), found, sends[h].at[j])


def near_kernel(held, packed_0, packed_1, came_0, came_1, picked_0, picked_1, near, *each):
    owner = lax.axis_index("kp")
    packed, came, picked = (packed_0, packed_1), (came_0, came_1), (picked_0, picked_1)
    half = picked_0.shape[2]
    for j in range(near.shape[0]):
        label = label_of(packed_0, held, half, j)
        for h in range(2):
            out = near.at[j, :, h * half : (h + 1) * half]
            found = entries(packed[h], owner, held, half)
            found += entries(came[h], owner ^ BITS[h][0], held, half)
            hit = copy_if(label, found, out)

            @pl.when(jnp.logical_not(hit))
            def _(h=h, j=j, out=out):
                out[...] = picked[h][j]

    for j, out in enumerate(each):
        out[...] = near[j]


def stack_kernel(*refs):
    for i, ref in enumerate(refs[:-1]):
        refs[-1][i] = ref[...]


def rest_kernel(held, packed_0, packed_1, came_0, came_1, *sends):
    owner = lax.axis_index("kp")
    packed, came = (packed_0, packed_1), (came_0, came_1)
    transfers, _, half, _ = sends[0].shape
    for j in range(len(sends) // 2):
        for h in range(2):
            first, second = BITS[h]
            found = entries(packed[h], owner, held, half)
            found += entries(came[h], owner ^ first, held, half)
            row = label_of(came[1 - h], held, half, j)
            for s in range(transfers):
                label = row + (owner ^ second) * transfers + s
                copy_if(label, found, sends[2 * j + h].at[s])


def far_kernel(held, j, packed_0, packed_1, came_0, came_1, rest_0, rest_1, far):
    owner = lax.axis_index("kp")
    packed, came, rest = (packed_0, packed_1), (came_0, came_1), (rest_0, rest_1)
    transfers, _, half, _ = rest_0.shape
    row = label_of(packed_0, held, half, j)
    for h in range(2):
        found = entries(packed[h], owner, held, half)
        found += entries(came[h], owner ^ BITS[h][0], held, half)
        for s in range(transfers):
            out = far.at[s, :, h * half : (h + 1) * half]
            hit = copy_if(row + owner * transfers + s, found, out)

            @pl.when(jnp.logical_not(hit))
            def _(h=h, s=s, out=out):
                out[...] = rest[h][s]


def load_kernel(source, panels, sems):
    copies = []
    for s in range(source.shape[0]):
        for part in range(2):
            copy = pltpu.make_async_copy(source.at[s, part], panels.at[s, part], sems.at[2 * s + part])
            copy.start()
            copies.append(copy)
    for copy in copies:
        copy.wait()


FORTH = (1, 3, 0, 2)
BACK = (2, 0, 3, 1)


def chip_at(z, steps):
    if steps == 1:
        return jnp.where(z < 2, 2 * z + 1, 2 * z - 4)
    if steps == -1:
        return jnp.where(lax.rem(z, 2) == 0, 2 + z // 2, z // 2)
    return z if steps == 0 else 3 - z


def lay(terms, upper, lower):
    for ref, first in terms:
        *count, _, g_local, t = ref.shape
        rows = pl.ds(first if isinstance(first, int) else pl.multiple_of(first, 128), g_local)
        for j, panel in enumerate([ref.at[j] for j in range(count[0])] if count else [ref]):
            real, imag = slice(2 * j * t, (2 * j + 1) * t), slice((2 * j + 1) * t, (2 * j + 2) * t)
            upper[rows, real] = panel[0]
            upper[rows, imag] = panel[1]
            lower[rows, real] = -panel[1]
            lower[rows, imag] = panel[0]


def place():
    slot = lax.axis_index("ga")
    return slot // 2, lax.rem(slot, 2)


def multiply(screened, s, span, width, upper, lower, first=0):
    span = pl.ds(pl.multiple_of(span, 128), width)
    rows = slice(first, first + width)
    return dot(screened[s, 0, :, span], upper[rows]) + dot(screened[s, 1, :, span], lower[rows])


def first_kernel(screened, own, coulomb, total, upper, lower):
    z, core = place()
    g = screened.shape[2]
    lay([(own, 0)], upper, lower)
    span = pl.ds(pl.multiple_of((2 * z + core) * g, 128), g)
    line = lax.broadcasted_iota(jnp.int32, (g, g), 0)
    on = line == lax.broadcasted_iota(jnp.int32, (g, g), 1)
    for s in range(screened.shape[0]):
        real = screened[s, 0, :, span]
        real = jnp.where(on, (real.astype(F32) - 2.0 * coulomb[...]).astype(BF16), real)
        total[s] = dot(real, upper[...]) + dot(screened[s, 1, :, span], lower[...])


def step_kernel(steps, screened, own, pair, before, total, upper, lower):
    z, core = place()
    g = screened.shape[2]
    lay([(own, core * g), (pair, (1 - core) * g)], upper, lower)
    span = 2 * chip_at(z, steps) * g
    for s in range(screened.shape[0]):
        total[s] = before[s] + multiply(screened, s, span, 2 * g, upper, lower)


def second_kernel(steps, screened, own, pairs, before, total, upper, lower):
    z, core = place()
    g = screened.shape[2]
    lay([(own, core * g), (pairs.at[1], (1 - core) * g), (pairs.at[0], 2 * g)], upper, lower)
    span = 2 * chip_at(z, steps) * g
    left = (2 * z + 1 - core) * g
    for s in range(screened.shape[0]):
        value = before[s] + multiply(screened, s, span, 2 * g, upper, lower)
        total[s] = value + multiply(screened, s, left, g, upper, lower, 2 * g)


def last_kernel(chips, steps, j, screened, own, pair, before, far, keep, give_0, give_1, upper, lower):
    z, core = place()
    g = screened.shape[2]
    t = far.shape[-1]
    lay([(own, core * g), (pair, (1 - core) * g)], upper, lower)
    span = 2 * chip_at(z, steps) * g
    first = core == 0
    for s in range(screened.shape[0]):
        value = before[s, :, 2 * j * t : 2 * (j + 1) * t]
        image = (value + multiply(screened, s, span, 2 * g, upper, lower)).astype(BF16)
        by_real, by_imag = tdot(far[s, 0], image), tdot(far[s, 1], image)
        real = by_real[:, :t] + by_imag[:, t:]
        imag = by_real[:, t:] - by_imag[:, :t]
        parts = ((real, imag), (real.T, -imag.T))
        for which in range(2):
            for part in range(2):
                block = parts[which][part]
                block = block.reshape(chips, 2, t // (2 * chips), t)
                keep[:, s, which, part] = jnp.where(first, block[:, 0], block[:, 1])
                give = (give_0, give_1)[which]
                give[:, s, part] = jnp.where(first, block[:, 1], block[:, 0]).astype(BF16)


def split_kernel(keep, came_0, came_1, own, cross, sends):
    z = lax.axis_index("ga") // 2
    for which, came in enumerate((came_0, came_1)):

        def chip(at):
            return keep[at, :, which] + came[at].astype(F32)

        own[:, which] = chip(z)
        cross[:, which] = chip(z ^ 2)
        for i, at in enumerate((z ^ 1, z ^ 3)):
            sends[i, :, which] = chip(at).astype(BF16)


def merge_kernel(own, cross, came, total, sends):
    total[...] = own[...] + came[0].astype(F32)
    sends[...] = (cross[...] + came[1].astype(F32)).astype(BF16)


def finish_kernel(count, chips, scale, *refs):
    kernel, mirror = refs[-2:]
    for j in range(count):
        terms = refs[j * chips : (j + 1) * chips]
        total = terms[0][...]
        for term in terms[1:]:
            total = total + term[...].astype(F32)
        mirror[j] = total[:, 0] * scale
        kernel[j] = total[:, 1] * scale


def quick(n_kp, n_ga, densities, screened, coulomb, block_rows):
    held, _, g_local, t = densities.shape
    transfers, g_total = screened.shape[0], screened.shape[3]
    count = block_rows.shape[1]
    chips = n_ga // 2
    half = g_local // 2
    shape = jax.ShapeDtypeStruct
    tie = lax.optimization_barrier

    def across(x, bit):
        return lax.ppermute(x, "kp", [(i, i ^ bit) for i in range(n_kp)])

    def other_core(x):
        return lax.ppermute(x, "ga", [(i, i ^ 1) for i in range(n_ga)])

    def along(x, chips_on):
        return lax.ppermute(x, "ga", [(i, 2 * chips_on[i // 2] + i % 2) for i in range(n_ga)])

    message = shape((2 * held * half + LABELS, t), BF16)

    def pack(panels):
        return run(pack_kernel, [message] * 2, block_rows, panels, specs=[SMEM, VMEM], name="pack")

    sums = shape((transfers, g_local, 2 * count * t), F32)

    def product(body, terms, *args):
        return run(
            body,
            sums,
            screened,
            *args,
            scratch=[pltpu.VMEM((terms * g_local, 2 * count * t), BF16)] * 2,
            aliases={} if terms == 1 else {3: 0},
            name="product",
            mib=24,
        )

    def pick(packed, came):
        sends = run(
            functools.partial(pick_kernel, held),
            [shape((count, 2, half, t), BF16)] * 2,
            *packed,
            *came,
            name="pick",
        )
        return [across(sends[h], BITS[h][1]) for h in range(2)]

    slices = shape((count, 2, g_local, t), BF16)

    def near_of(packed, came, picked, apart=False):
        kernel = functools.partial(near_kernel, held)
        outs = [slices] + [shape(slices.shape[1:], BF16)] * (count if apart else 0)
        near, *each = run(kernel, outs, *packed, *came, *picked, name="near")
        return (near, each) if apart else near

    packed = pack(densities)
    before = along(tie((densities, packed))[0], FORTH)
    came = [across(packed[h], BITS[h][0]) for h in range(2)]
    source, packed = tie((screened, packed))
    screened = run(
        load_kernel,
        shape(screened.shape, screened.dtype),
        source,
        specs=[HBM],
        scratch=[pltpu.SemaphoreType.DMA((2 * transfers,))],
        name="load",
        mib=40,
    )
    came, screened = tie((came, screened))
    picked = pick(packed, came)
    packed_before = pack(before)
    picked, _ = tie((picked, packed_before))
    near = near_of(packed, came, picked)
    ahead = along(near, BACK)
    total = product(first_kernel, 1, near, coulomb[None, :])

    came_before = [across(packed_before[h], BITS[h][0]) for h in range(2)]
    rest_sends = run(
        functools.partial(rest_kernel, held),
        [shape((transfers, 2, half, t), BF16)] * (2 * count),
        *packed,
        *came,
        name="rest",
    )
    came_before, total, rest_sends = tie((came_before, total, rest_sends))
    picked_before = pick(packed_before, came_before)
    near_before, before_each = near_of(packed_before, came_before, picked_before, True)

    behind = [along(x, FORTH) for x in before_each]
    rest_sends, ahead, _ = tie((rest_sends, ahead, near_before))
    rest = [across(x, BITS[i % 2][1]) for i, x in enumerate(rest_sends)]

    stack, _ = tie(((near, near_before), ahead))
    both = run(stack_kernel, shape((2, *slices.shape), BF16), *stack, name="stack")
    total = product(functools.partial(step_kernel, 1), 2, ahead, other_core(ahead), total)
    total = product(
        functools.partial(second_kernel, -1), 3, near_before, other_core(both), total
    )

    parts = shape((chips, transfers, 2, 2, t // n_ga, t), F32)
    part = parts.shape[1:]
    sums_of = []
    done = total
    for j in range(count):
        came_j = rest[2 * j : 2 * j + 2]
        if j:
            behind[j], came_j, _ = tie((behind[j], came_j, done))
        else:
            behind[j] = tie((behind[j], done))[0]
            came_j = [tie((x, done))[0] for x in came_j]
        far = run(
            functools.partial(far_kernel, held, j),
            shape((transfers, 2, g_local, t), BF16),
            *packed,
            *came,
            *came_j,
            name="far",
        )
        if j:
            far = tie((far, halves))[0]
        keep, *give = run(
            functools.partial(last_kernel, chips, -2, j),
            [parts] + [shape((chips, transfers, 2, t // n_ga, t), BF16)] * 2,
            screened,
            behind[j],
            other_core(behind[j]),
            total,
            far,
            scratch=[pltpu.VMEM((2 * g_local, 2 * t), BF16)] * 2,
            name="last",
            mib=24,
        )
        own, cross, sends = run(
            split_kernel,
            [shape(part, F32), shape(part, F32), shape((2, *part), BF16)],
            keep,
            *[other_core(x) for x in give],
            name="split",
        )
        done = sends
        halves = lax.ppermute(sends, "ga", [(i, i ^ 2) for i in range(n_ga)])
        sums_of.append((own, cross, halves))
    groups = []
    for own, cross, halves in sums_of:
        own, sends = run(
            merge_kernel, [shape(part, F32), shape(part, BF16)], own, cross, halves, name="merge"
        )
        groups += [own, lax.ppermute(sends, "ga", [(i, i ^ 4) for i in range(n_ga)])]
    result = shape((count, transfers, 2, t // n_ga, t), F32)
    return tuple(
        run(
            functools.partial(finish_kernel, count, 2, -1.0 / math.sqrt(g_total)),
            [result] * 2,
            *groups,
            name="finish",
        )
    )


def plain(densities, screened, coulomb, block_rows):
    owner = lax.axis_index("kp")
    g_slot = lax.axis_index("ga")
    k_held = densities.shape[0]
    g_local = densities.shape[2]
    g_total = screened.shape[3]
    rows = block_rows[0]
    transfers = owner * k_held + jnp.arange(k_held, dtype=jnp.int32)
    far_rows = rows[:, None] + transfers[None, :]
    piece = lax.all_gather(densities, "kp", axis=0, tiled=True)
    labels = jnp.arange(piece.shape[0], dtype=jnp.int32)
    pick_near = (rows[:, None] == labels[None, :]).astype(jnp.bfloat16)
    pick_far = (far_rows[:, :, None] == labels[None, None, :]).astype(jnp.bfloat16)
    near_acc = jnp.einsum(
        "jp,pcgt->jcgt", pick_near, piece, preferred_element_type=jnp.float32
    ).astype(jnp.bfloat16)
    far_acc = jnp.einsum(
        "jsp,pcgt->jscgt", pick_far, piece, preferred_element_type=jnp.float32
    ).astype(jnp.bfloat16)
    columns = jnp.arange(g_total, dtype=jnp.int32)
    own_rows = g_slot * g_local + jnp.arange(g_local, dtype=jnp.int32)
    diag_mask = own_rows[:, None] == columns[None, :]
    coulomb_diag = jnp.where(diag_mask, 2.0 * coulomb[:, None], 0.0)
    screen_real = (coulomb_diag[None] - screened[:, 0].astype(jnp.float32)).astype(jnp.bfloat16)
    screen_imag = -screened[:, 1]
    near_all = lax.all_gather(near_acc, "ga", axis=2, tiled=True)
    piece_real = near_all[:, 0]
    piece_imag = near_all[:, 1]
    real_term = jnp.einsum(
        "sgh,jht->jsgt", screen_real, piece_real, preferred_element_type=jnp.float32
    ) - jnp.einsum("sgh,jht->jsgt", screen_imag, piece_imag, preferred_element_type=jnp.float32)
    imag_term = jnp.einsum(
        "sgh,jht->jsgt", screen_real, piece_imag, preferred_element_type=jnp.float32
    ) + jnp.einsum("sgh,jht->jsgt", screen_imag, piece_real, preferred_element_type=jnp.float32)
    image = jnp.stack([real_term, imag_term], 2)
    image = image.astype(jnp.bfloat16)
    image_real = image[:, :, 0]
    image_imag = image[:, :, 1]
    far_real = far_acc[:, :, 0]
    far_imag = far_acc[:, :, 1]
    lower_real = jnp.einsum(
        "jsga,jsgb->jsab", far_real, image_real, preferred_element_type=jnp.float32
    ) + jnp.einsum("jsga,jsgb->jsab", far_imag, image_imag, preferred_element_type=jnp.float32)
    lower_imag = jnp.einsum(
        "jsga,jsgb->jsab", far_real, image_imag, preferred_element_type=jnp.float32
    ) - jnp.einsum("jsga,jsgb->jsab", far_imag, image_real, preferred_element_type=jnp.float32)
    partial_lower = jnp.stack([lower_real, lower_imag], 2)
    inverse = 1.0 / math.sqrt(g_total)
    mirror = lax.psum_scatter(partial_lower, "ga", scatter_dimension=3, tiled=True) * inverse
    partial_upper = jnp.stack([jnp.swapaxes(lower_real, 2, 3), -jnp.swapaxes(lower_imag, 2, 3)], 2)
    kernel = lax.psum_scatter(partial_upper, "ga", scatter_dimension=3, tiled=True) * inverse
    return (kernel, mirror)


def solution(mesh):
    placed = (P("kp", None, "ga", None), P("kp", None, "ga", None), P("ga"), P("kp", None))
    n_kp, n_ga = mesh.shape["kp"], mesh.shape["ga"]

    def shards(densities, screened, coulomb, block_rows):
        g_local, t = densities.shape[2], densities.shape[3]
        fits = n_kp == 2 * 2 and n_ga == 4 * 2
        fits = fits and g_local % 128 == 0 and t % (8 * n_ga) == 0
        fits = fits and n_kp * densities.shape[0] <= 256
        if fits:
            return quick(n_kp, n_ga, densities, screened, coulomb, block_rows)
        return plain(densities, screened, coulomb, block_rows)

    return jax.shard_map(
        shards,
        mesh=mesh,
        in_specs=placed,
        out_specs=(P("kp", None, None, "ga", None), P("kp", None, None, "ga", None)),
        check_vma=False,
    )
```

```python
import functools
import itertools
import math

import jax
import jax.numpy as jnp
from jax import lax
from jax.experimental import pallas as pl
from jax.experimental.pallas import tpu as pltpu
from jax.sharding import PartitionSpec as P

F32 = jnp.float32
BF16 = jnp.bfloat16
LABELS = 16
VMEM = pl.BlockSpec(memory_space=pltpu.VMEM)
SMEM = pl.BlockSpec(memory_space=pltpu.SMEM)
HBM = pl.BlockSpec(memory_space=pltpu.HBM)


def dot(a, b):
    return jnp.dot(a, b, preferred_element_type=F32)


def tdot(a, b):
    return lax.dot_general(a, b, (((0,), (0,)), ((), ())), preferred_element_type=F32)


def run(body, out, *args, specs=None, scratch=(), name=None, aliases=None, mib=16):
    outs = out if isinstance(out, (list, tuple)) else [out]
    result = pl.pallas_call(
        body,
        in_specs=specs or [VMEM] * len(args),
        out_specs=[VMEM] * len(outs),
        out_shape=list(outs),
        scratch_shapes=list(scratch),
        input_output_aliases=aliases or {},
        compiler_params=pltpu.CompilerParams(vmem_limit_bytes=mib * 2**20),
        cost_estimate=pl.CostEstimate(flops=0, bytes_accessed=0, transcendentals=0),
        name=name,
    )(*args)
    return list(result) if isinstance(out, (list, tuple)) else result[0]


BITS = ((1, 2), (2, 1))


def pack_kernel(rows, densities, *sends):
    held, _, g_local, t = densities.shape
    half = g_local // 2
    for h in range(2):
        for k in range(held):
            for part in range(2):
                at = (2 * k + part) * half
                sends[h][at : at + half] = densities[k, part, h * half : (h + 1) * half]
        line = lax.broadcasted_iota(jnp.int32, (LABELS, t), 0)
        tile = jnp.zeros((LABELS, t), F32)
        for j in range(rows.shape[1]):
            tile = jnp.where(line == j, rows[0, j].astype(F32), tile)
        sends[h][2 * held * half :] = tile.astype(BF16)


def label_of(message, held, half, j):
    tail = message[2 * held * half :].astype(F32)
    return jnp.max(tail[j : j + 1]).astype(jnp.int32)


def entries(message, owner, held, half):
    return [(owner * held + k, message, 2 * k * half, (2 * k + 1) * half) for k in range(held)]


def copy_if(label, found, out):
    half = out.shape[1]
    hit = None
    for name, message, real, imag in found:
        match = label == name
        hit = match if hit is None else hit | match

        @pl.when(match)
        def _(message=message, real=real, imag=imag):
            out[0] = message[real : real + half]
            out[1] = message[imag : imag + half]

    return hit


def pick_kernel(held, packed_0, packed_1, came_0, came_1, *sends):
    owner = lax.axis_index("kp")
    packed, came = (packed_0, packed_1), (came_0, came_1)
    half = sends[0].shape[2]
    for j in range(sends[0].shape[0]):
        for h in range(2):
            found = entries(packed[h], owner, held, half)
            found += entries(came[h], owner ^ BITS[h][0], held, half)
            copy_if(label_of(came[1 - h], held, half, j), found, sends[h].at[j])


def near_kernel(held, packed_0, packed_1, came_0, came_1, picked_0, picked_1, near):
    owner = lax.axis_index("kp")
    packed, came, picked = (packed_0, packed_1), (came_0, came_1), (picked_0, picked_1)
    half = picked_0.shape[2]
    for j in range(near.shape[0]):
        label = label_of(packed_0, held, half, j)
        for h in range(2):
            out = near.at[j, :, h * half : (h + 1) * half]
            found = entries(packed[h], owner, held, half)
            found += entries(came[h], owner ^ BITS[h][0], held, half)
            hit = copy_if(label, found, out)

            @pl.when(jnp.logical_not(hit))
            def _(h=h, j=j, out=out):
                out[...] = picked[h][j]


def stack_kernel(*refs):
    for i, ref in enumerate(refs[:-1]):
        refs[-1][i] = ref[...]


def left_over(n_kp, held, transfers, count):
    most = []
    for first, second in BITS:
        worst = 0
        for owner in range(n_kp):
            side = {who * held + k for who in (owner ^ second, owner ^ second ^ first) for k in range(held)}
            rows = range(n_kp * held - transfers * (owner + 1) + 1)
            for chosen in itertools.product(rows, repeat=count):
                need = {r + owner * transfers + s for r in chosen for s in range(transfers)}
                worst = max(worst, len((need & side) - set(chosen)))
        most.append(max(worst, 1))
    return most


def slots(labels, rows, owner, transfers):
    found, place = [], jnp.int32(0)
    for label in labels:
        need, sent = jnp.bool_(False), jnp.bool_(False)
        for row in rows:
            first = row + owner * transfers
            need = need | ((label >= first) & (label < first + transfers))
            sent = sent | (label == row)
        need = need & jnp.logical_not(sent)
        found.append((need, place))
        place = place + need.astype(jnp.int32)
    return found


def rest_kernel(held, transfers, count, packed_0, packed_1, came_0, came_1, *sends):
    owner = lax.axis_index("kp")
    packed, came = (packed_0, packed_1), (came_0, came_1)
    for h in range(2):
        first, second = BITS[h]
        room, _, half, _ = sends[h].shape
        found = entries(packed[h], owner, held, half)
        found += entries(came[h], owner ^ first, held, half)
        rows = [label_of(came[1 - h], held, half, j) for j in range(count)]
        places = slots([label for label, *_ in found], rows, owner ^ second, transfers)
        for (_, message, real, imag), (need, place) in zip(found, places):
            for i in range(room):

                @pl.when(need & (place == i))
                def _(h=h, i=i, message=message, real=real, imag=imag, half=half):
                    sends[h][i, 0] = message[real : real + half]
                    sends[h][i, 1] = message[imag : imag + half]


def far_kernel(
    held, packed_0, packed_1, came_0, came_1, picked_0, picked_1, rest_0, rest_1, far
):
    owner = lax.axis_index("kp")
    packed, came = (packed_0, packed_1), (came_0, came_1)
    picked, rest = (picked_0, picked_1), (rest_0, rest_1)
    count, transfers, _, g_local, _ = far.shape
    half = g_local // 2
    rows = [label_of(packed_0, held, half, j) for j in range(count)]
    for h in range(2):
        first, second = BITS[h]
        found = entries(packed[h], owner, held, half)
        found += entries(came[h], owner ^ first, held, half)
        side = [
            who * held + k for who in (owner ^ second, owner ^ second ^ first) for k in range(held)
        ]
        places = slots(side, rows, owner, transfers)
        for j in range(count):
            for s in range(transfers):
                label = rows[j] + owner * transfers + s
                out = far.at[j, s, :, h * half : (h + 1) * half]
                hit = copy_if(label, found, out)
                for i in range(count):
                    match = (label == rows[i]) & jnp.logical_not(hit)
                    hit = hit | match

                    @pl.when(match)
                    def _(h=h, i=i, out=out):
                        out[...] = picked[h][i]

                for name, (need, place) in zip(side, places):
                    for i in range(rest[h].shape[0]):

                        @pl.when((label == name) & need & (place == i))
                        def _(h=h, i=i, out=out):
                            out[...] = rest[h][i]


def load_kernel(source, panels, sems):
    copies = []
    for s in range(source.shape[0]):
        for part in range(2):
            copy = pltpu.make_async_copy(source.at[s, part], panels.at[s, part], sems.at[2 * s + part])
            copy.start()
            copies.append(copy)
    for copy in copies:
        copy.wait()


FORTH = (1, 3, 0, 2)
BACK = (2, 0, 3, 1)


def chip_at(z, steps):
    if steps == 1:
        return jnp.where(z < 2, 2 * z + 1, 2 * z - 4)
    if steps == -1:
        return jnp.where(lax.rem(z, 2) == 0, 2 + z // 2, z // 2)
    return z if steps == 0 else 3 - z


def lay(terms, upper, lower):
    for ref, first in terms:
        count, _, g_local, t = ref.shape
        rows = pl.ds(first if isinstance(first, int) else pl.multiple_of(first, 128), g_local)
        for j in range(count):
            real, imag = slice(2 * j * t, (2 * j + 1) * t), slice((2 * j + 1) * t, (2 * j + 2) * t)
            upper[rows, real] = ref[j, 0]
            upper[rows, imag] = ref[j, 1]
            lower[rows, real] = -ref[j, 1]
            lower[rows, imag] = ref[j, 0]


def place():
    slot = lax.axis_index("ga")
    return slot // 2, lax.rem(slot, 2)


def multiply(screened, s, span, width, upper, lower, first=0):
    span = pl.ds(pl.multiple_of(span, 128), width)
    rows = slice(first, first + width)
    return dot(screened[s, 0, :, span], upper[rows]) + dot(screened[s, 1, :, span], lower[rows])


def first_kernel(screened, own, coulomb, total, upper, lower):
    z, core = place()
    g = screened.shape[2]
    lay([(own, 0)], upper, lower)
    span = pl.ds(pl.multiple_of((2 * z + core) * g, 128), g)
    line = lax.broadcasted_iota(jnp.int32, (g, g), 0)
    on = line == lax.broadcasted_iota(jnp.int32, (g, g), 1)
    for s in range(screened.shape[0]):
        real = screened[s, 0, :, span]
        real = jnp.where(on, (real.astype(F32) - 2.0 * coulomb[...]).astype(BF16), real)
        total[s] = dot(real, upper[...]) + dot(screened[s, 1, :, span], lower[...])


def step_kernel(steps, screened, own, pair, before, total, upper, lower):
    z, core = place()
    g = screened.shape[2]
    lay([(own, core * g), (pair, (1 - core) * g)], upper, lower)
    span = 2 * chip_at(z, steps) * g
    for s in range(screened.shape[0]):
        total[s] = before[s] + multiply(screened, s, span, 2 * g, upper, lower)


def second_kernel(steps, screened, own, pairs, before, total, upper, lower):
    z, core = place()
    g = screened.shape[2]
    lay([(own, core * g), (pairs.at[1], (1 - core) * g), (pairs.at[0], 2 * g)], upper, lower)
    span = 2 * chip_at(z, steps) * g
    left = (2 * z + 1 - core) * g
    for s in range(screened.shape[0]):
        value = before[s] + multiply(screened, s, span, 2 * g, upper, lower)
        total[s] = value + multiply(screened, s, left, g, upper, lower, 2 * g)


def last_kernel(chips, steps, j, screened, own, pair, before, far, keep, give, upper, lower):
    z, core = place()
    g = screened.shape[2]
    t = far.shape[-1]
    lay([(own.at[j : j + 1], core * g), (pair.at[j : j + 1], (1 - core) * g)], upper, lower)
    span = 2 * chip_at(z, steps) * g
    first = core == 0
    for s in range(screened.shape[0]):
        value = before[s, :, 2 * j * t : 2 * (j + 1) * t]
        image = (value + multiply(screened, s, span, 2 * g, upper, lower)).astype(BF16)
        by_real, by_imag = tdot(far[j, s, 0], image), tdot(far[j, s, 1], image)
        real = by_real[:, :t] + by_imag[:, t:]
        imag = by_real[:, t:] - by_imag[:, :t]
        parts = ((real, imag), (real.T, -imag.T))
        for which in range(2):
            for part in range(2):
                block = parts[which][part]
                block = block.reshape(chips, 2, t // (2 * chips), t)
                keep[:, s, which, part] = jnp.where(first, block[:, 0], block[:, 1])
                give[:, s, which, part] = jnp.where(first, block[:, 1], block[:, 0]).astype(BF16)


def split_kernel(keep, came, own, cross, sends):
    z = lax.axis_index("ga") // 2
    own[...] = keep[z] + came[z].astype(F32)
    cross[...] = keep[z ^ 2] + came[z ^ 2].astype(F32)
    for i, at in enumerate((z ^ 1, z ^ 3)):
        sends[i] = (keep[at] + came[at].astype(F32)).astype(BF16)


def merge_kernel(own, cross, came, total, sends):
    total[...] = own[...] + came[0].astype(F32)
    sends[...] = (cross[...] + came[1].astype(F32)).astype(BF16)


def finish_kernel(count, chips, scale, *refs):
    kernel, mirror = refs[-2:]
    for j in range(count):
        terms = refs[j * chips : (j + 1) * chips]
        total = terms[0][...]
        for term in terms[1:]:
            total = total + term[...].astype(F32)
        mirror[j] = total[:, 0] * scale
        kernel[j] = total[:, 1] * scale


def quick(n_kp, n_ga, densities, screened, coulomb, block_rows):
    held, _, g_local, t = densities.shape
    transfers, g_total = screened.shape[0], screened.shape[3]
    count = block_rows.shape[1]
    chips = n_ga // 2
    half = g_local // 2
    shape = jax.ShapeDtypeStruct
    tie = lax.optimization_barrier

    def across(x, bit):
        return lax.ppermute(x, "kp", [(i, i ^ bit) for i in range(n_kp)])

    def other_core(x):
        return lax.ppermute(x, "ga", [(i, i ^ 1) for i in range(n_ga)])

    def along(x, chips_on):
        return lax.ppermute(x, "ga", [(i, 2 * chips_on[i // 2] + i % 2) for i in range(n_ga)])

    message = shape((2 * held * half + LABELS, t), BF16)

    def pack(panels):
        return run(pack_kernel, [message] * 2, block_rows, panels, specs=[SMEM, VMEM], name="pack")

    sums = shape((transfers, g_local, 2 * count * t), F32)

    def product(body, terms, *args):
        return run(
            body,
            sums,
            screened,
            *args,
            scratch=[pltpu.VMEM((terms * g_local, 2 * count * t), BF16)] * 2,
            aliases={} if terms == 1 else {3: 0},
            name="product",
            mib=24,
        )

    def pick(packed, came):
        sends = run(
            functools.partial(pick_kernel, held),
            [shape((count, 2, half, t), BF16)] * 2,
            *packed,
            *came,
            name="pick",
        )
        return [across(sends[h], BITS[h][1]) for h in range(2)]

    slices = shape((count, 2, g_local, t), BF16)

    def near_of(packed, came, picked):
        kernel = functools.partial(near_kernel, held)
        return run(kernel, slices, *packed, *came, *picked, name="near")

    before = along(densities, FORTH)
    packed = pack(densities)
    came = [across(packed[h], BITS[h][0]) for h in range(2)]
    source, packed = tie((screened, packed))
    screened = run(
        load_kernel,
        shape(screened.shape, screened.dtype),
        source,
        specs=[HBM],
        scratch=[pltpu.SemaphoreType.DMA((2 * transfers,))],
        name="load",
        mib=40,
    )
    came, screened = tie((came, screened))
    picked = pick(packed, came)
    packed_before = pack(before)
    rest_sends = run(
        functools.partial(rest_kernel, held, transfers, count),
        [shape((room, 2, half, t), BF16) for room in left_over(n_kp, held, transfers, count)],
        *packed,
        *came,
        name="rest",
    )
    picked = list(tie((picked, (packed_before, rest_sends)))[0])
    near = near_of(packed, came, picked)
    ahead = along(near, BACK)
    total = product(first_kernel, 1, near, coulomb[None, :])

    came_before = [across(packed_before[h], BITS[h][0]) for h in range(2)]
    came_before, total = tie((came_before, total))
    picked_before = pick(packed_before, came_before)
    near_before = near_of(packed_before, came_before, picked_before)
    behind = along(near_before, FORTH)

    rest_sends, ahead, _ = tie((rest_sends, ahead, near_before))
    rest = [across(rest_sends[h], BITS[h][1]) for h in range(2)]

    stack, _ = tie(((near, near_before), ahead))
    both = run(stack_kernel, shape((2, *slices.shape), BF16), *stack, name="stack")
    total = product(
        functools.partial(step_kernel, 1), 2, ahead, other_core(ahead), total
    )
    total = product(
        functools.partial(second_kernel, -1), 3, near_before, other_core(both), total
    )
    behind, rest, total = tie((behind, rest, total))
    far = run(
        functools.partial(far_kernel, held),
        shape((count, transfers, 2, g_local, t), BF16),
        *packed,
        *came,
        *picked,
        *rest,
        name="far",
    )

    parts = shape((chips, transfers, 2, 2, t // n_ga, t), F32)
    part = parts.shape[1:]
    pair = other_core(behind)
    swaps = []
    for j in range(count):
        keep, give = run(
            functools.partial(last_kernel, chips, -2, j),
            [parts, shape(parts.shape, BF16)],
            screened,
            behind,
            pair,
            total,
            far,
            scratch=[pltpu.VMEM((2 * g_local, 2 * t), BF16)] * 2,
            name="last",
            mib=24,
        )
        swaps.append((keep, other_core(give)))
    groups = []
    for keep, came_j in swaps:
        own, cross, sends = run(
            split_kernel,
            [shape(part, F32), shape(part, F32), shape((2, *part), BF16)],
            keep,
            came_j,
            name="split",
        )
        own, sends = run(
            merge_kernel,
            [shape(part, F32), shape(part, BF16)],
            own,
            cross,
            lax.ppermute(sends, "ga", [(i, i ^ 2) for i in range(n_ga)]),
            name="merge",
        )
        groups += [own, lax.ppermute(sends, "ga", [(i, i ^ 4) for i in range(n_ga)])]
    result = shape((count, transfers, 2, t // n_ga, t), F32)
    return tuple(
        run(
            functools.partial(finish_kernel, count, 2, -1.0 / math.sqrt(g_total)),
            [result] * 2,
            *groups,
            name="finish",
        )
    )


def plain(densities, screened, coulomb, block_rows):
    owner = lax.axis_index("kp")
    g_slot = lax.axis_index("ga")
    k_held = densities.shape[0]
    g_local = densities.shape[2]
    g_total = screened.shape[3]
    rows = block_rows[0]
    transfers = owner * k_held + jnp.arange(k_held, dtype=jnp.int32)
    far_rows = rows[:, None] + transfers[None, :]
    piece = lax.all_gather(densities, "kp", axis=0, tiled=True)
    labels = jnp.arange(piece.shape[0], dtype=jnp.int32)
    pick_near = (rows[:, None] == labels[None, :]).astype(jnp.bfloat16)
    pick_far = (far_rows[:, :, None] == labels[None, None, :]).astype(jnp.bfloat16)
    near_acc = jnp.einsum(
        "jp,pcgt->jcgt", pick_near, piece, preferred_element_type=jnp.float32
    ).astype(jnp.bfloat16)
    far_acc = jnp.einsum(
        "jsp,pcgt->jscgt", pick_far, piece, preferred_element_type=jnp.float32
    ).astype(jnp.bfloat16)
    columns = jnp.arange(g_total, dtype=jnp.int32)
    own_rows = g_slot * g_local + jnp.arange(g_local, dtype=jnp.int32)
    diag_mask = own_rows[:, None] == columns[None, :]
    coulomb_diag = jnp.where(diag_mask, 2.0 * coulomb[:, None], 0.0)
    screen_real = (coulomb_diag[None] - screened[:, 0].astype(jnp.float32)).astype(jnp.bfloat16)
    screen_imag = -screened[:, 1]
    near_all = lax.all_gather(near_acc, "ga", axis=2, tiled=True)
    piece_real = near_all[:, 0]
    piece_imag = near_all[:, 1]
    real_term = jnp.einsum(
        "sgh,jht->jsgt", screen_real, piece_real, preferred_element_type=jnp.float32
    ) - jnp.einsum("sgh,jht->jsgt", screen_imag, piece_imag, preferred_element_type=jnp.float32)
    imag_term = jnp.einsum(
        "sgh,jht->jsgt", screen_real, piece_imag, preferred_element_type=jnp.float32
    ) + jnp.einsum("sgh,jht->jsgt", screen_imag, piece_real, preferred_element_type=jnp.float32)
    image = jnp.stack([real_term, imag_term], 2)
    image = image.astype(jnp.bfloat16)
    image_real = image[:, :, 0]
    image_imag = image[:, :, 1]
    far_real = far_acc[:, :, 0]
    far_imag = far_acc[:, :, 1]
    lower_real = jnp.einsum(
        "jsga,jsgb->jsab", far_real, image_real, preferred_element_type=jnp.float32
    ) + jnp.einsum("jsga,jsgb->jsab", far_imag, image_imag, preferred_element_type=jnp.float32)
    lower_imag = jnp.einsum(
        "jsga,jsgb->jsab", far_real, image_imag, preferred_element_type=jnp.float32
    ) - jnp.einsum("jsga,jsgb->jsab", far_imag, image_real, preferred_element_type=jnp.float32)
    partial_lower = jnp.stack([lower_real, lower_imag], 2)
    inverse = 1.0 / math.sqrt(g_total)
    mirror = lax.psum_scatter(partial_lower, "ga", scatter_dimension=3, tiled=True) * inverse
    partial_upper = jnp.stack([jnp.swapaxes(lower_real, 2, 3), -jnp.swapaxes(lower_imag, 2, 3)], 2)
    kernel = lax.psum_scatter(partial_upper, "ga", scatter_dimension=3, tiled=True) * inverse
    return (kernel, mirror)


def solution(mesh):
    placed = (P("kp", None, "ga", None), P("kp", None, "ga", None), P("ga"), P("kp", None))
    n_kp, n_ga = mesh.shape["kp"], mesh.shape["ga"]

    def shards(densities, screened, coulomb, block_rows):
        g_local, t = densities.shape[2], densities.shape[3]
        fits = n_kp == 2 * 2 and n_ga == 4 * 2
        fits = fits and g_local % 128 == 0 and t % (8 * n_ga) == 0
        fits = fits and n_kp * densities.shape[0] <= 256
        if fits:
            return quick(n_kp, n_ga, densities, screened, coulomb, block_rows)
        return plain(densities, screened, coulomb, block_rows)

    return jax.shard_map(
        shards,
        mesh=mesh,
        in_specs=placed,
        out_specs=(P("kp", None, None, "ga", None), P("kp", None, None, "ga", None)),
        check_vma=False,
    )
```

```python
import functools
import itertools
import math

import jax
import jax.numpy as jnp
from jax import lax
from jax.experimental import pallas as pl
from jax.experimental.pallas import tpu as pltpu
from jax.sharding import PartitionSpec as P

F32 = jnp.float32
BF16 = jnp.bfloat16
LABELS = 16
VMEM = pl.BlockSpec(memory_space=pltpu.VMEM)
SMEM = pl.BlockSpec(memory_space=pltpu.SMEM)
HBM = pl.BlockSpec(memory_space=pltpu.HBM)


def dot(a, b):
    return jnp.dot(a, b, preferred_element_type=F32)


def tdot(a, b):
    return lax.dot_general(a, b, (((0,), (0,)), ((), ())), preferred_element_type=F32)


def run(body, out, *args, specs=None, scratch=(), name=None, aliases=None, mib=16):
    outs = out if isinstance(out, (list, tuple)) else [out]
    result = pl.pallas_call(
        body,
        in_specs=specs or [VMEM] * len(args),
        out_specs=[VMEM] * len(outs),
        out_shape=list(outs),
        scratch_shapes=list(scratch),
        input_output_aliases=aliases or {},
        compiler_params=pltpu.CompilerParams(vmem_limit_bytes=mib * 2**20),
        cost_estimate=pl.CostEstimate(flops=0, bytes_accessed=0, transcendentals=0),
        name=name,
    )(*args)
    return list(result) if isinstance(out, (list, tuple)) else result[0]


BITS = ((1, 2), (2, 1))


def pack_kernel(rows, densities, *sends):
    held, _, g_local, t = densities.shape
    half = g_local // 2
    for h in range(2):
        for k in range(held):
            for part in range(2):
                at = (2 * k + part) * half
                sends[h][at : at + half] = densities[k, part, h * half : (h + 1) * half]
        line = lax.broadcasted_iota(jnp.int32, (LABELS, t), 0)
        tile = jnp.zeros((LABELS, t), F32)
        for j in range(rows.shape[1]):
            tile = jnp.where(line == j, rows[0, j].astype(F32), tile)
        sends[h][2 * held * half :] = tile.astype(BF16)


def label_of(message, held, half, j):
    tail = message[2 * held * half :].astype(F32)
    return jnp.max(tail[j : j + 1]).astype(jnp.int32)


def entries(message, owner, held, half):
    return [(owner * held + k, message, 2 * k * half, (2 * k + 1) * half) for k in range(held)]


def copy_if(label, found, out):
    half = out.shape[1]
    hit = None
    for name, message, real, imag in found:
        match = label == name
        hit = match if hit is None else hit | match

        @pl.when(match)
        def _(message=message, real=real, imag=imag):
            out[0] = message[real : real + half]
            out[1] = message[imag : imag + half]

    return hit


def pick_kernel(held, packed_0, packed_1, came_0, came_1, *sends):
    owner = lax.axis_index("kp")
    packed, came = (packed_0, packed_1), (came_0, came_1)
    half = sends[0].shape[2]
    for j in range(sends[0].shape[0]):
        for h in range(2):
            found = entries(packed[h], owner, held, half)
            found += entries(came[h], owner ^ BITS[h][0], held, half)
            copy_if(label_of(came[1 - h], held, half, j), found, sends[h].at[j])


def near_kernel(held, packed_0, packed_1, came_0, came_1, picked_0, picked_1, near):
    owner = lax.axis_index("kp")
    packed, came, picked = (packed_0, packed_1), (came_0, came_1), (picked_0, picked_1)
    half = picked_0.shape[2]
    for j in range(near.shape[0]):
        label = label_of(packed_0, held, half, j)
        for h in range(2):
            out = near.at[j, :, h * half : (h + 1) * half]
            found = entries(packed[h], owner, held, half)
            found += entries(came[h], owner ^ BITS[h][0], held, half)
            hit = copy_if(label, found, out)

            @pl.when(jnp.logical_not(hit))
            def _(h=h, j=j, out=out):
                out[...] = picked[h][j]


def stack_kernel(*refs):
    for i, ref in enumerate(refs[:-1]):
        refs[-1][i] = ref[...]


def left_over(n_kp, held, transfers, count):
    most = []
    for first, second in BITS:
        worst = 0
        for owner in range(n_kp):
            side = {who * held + k for who in (owner ^ second, owner ^ second ^ first) for k in range(held)}
            rows = range(n_kp * held - transfers * (owner + 1) + 1)
            for chosen in itertools.product(rows, repeat=count):
                need = {r + owner * transfers + s for r in chosen for s in range(transfers)}
                worst = max(worst, len((need & side) - set(chosen)))
        most.append(max(worst, 1))
    return most


def slots(labels, rows, owner, transfers):
    found, place = [], jnp.int32(0)
    for label in labels:
        need, sent = jnp.bool_(False), jnp.bool_(False)
        for row in rows:
            first = row + owner * transfers
            need = need | ((label >= first) & (label < first + transfers))
            sent = sent | (label == row)
        need = need & jnp.logical_not(sent)
        found.append((need, place))
        place = place + need.astype(jnp.int32)
    return found


def rest_kernel(held, transfers, count, packed_0, packed_1, came_0, came_1, *sends):
    owner = lax.axis_index("kp")
    packed, came = (packed_0, packed_1), (came_0, came_1)
    for h in range(2):
        first, second = BITS[h]
        room, _, half, _ = sends[h].shape
        found = entries(packed[h], owner, held, half)
        found += entries(came[h], owner ^ first, held, half)
        rows = [label_of(came[1 - h], held, half, j) for j in range(count)]
        places = slots([label for label, *_ in found], rows, owner ^ second, transfers)
        for (_, message, real, imag), (need, place) in zip(found, places):
            for i in range(room):

                @pl.when(need & (place == i))
                def _(h=h, i=i, message=message, real=real, imag=imag, half=half):
                    sends[h][i, 0] = message[real : real + half]
                    sends[h][i, 1] = message[imag : imag + half]


def far_kernel(
    held, packed_0, packed_1, came_0, came_1, picked_0, picked_1, rest_0, rest_1, far
):
    owner = lax.axis_index("kp")
    packed, came = (packed_0, packed_1), (came_0, came_1)
    picked, rest = (picked_0, picked_1), (rest_0, rest_1)
    count, transfers, _, g_local, _ = far.shape
    half = g_local // 2
    rows = [label_of(packed_0, held, half, j) for j in range(count)]
    for h in range(2):
        first, second = BITS[h]
        found = entries(packed[h], owner, held, half)
        found += entries(came[h], owner ^ first, held, half)
        side = [
            who * held + k for who in (owner ^ second, owner ^ second ^ first) for k in range(held)
        ]
        places = slots(side, rows, owner, transfers)
        for j in range(count):
            for s in range(transfers):
                label = rows[j] + owner * transfers + s
                out = far.at[j, s, :, h * half : (h + 1) * half]
                hit = copy_if(label, found, out)
                for i in range(count):
                    match = (label == rows[i]) & jnp.logical_not(hit)
                    hit = hit | match

                    @pl.when(match)
                    def _(h=h, i=i, out=out):
                        out[...] = picked[h][i]

                for name, (need, place) in zip(side, places):
                    for i in range(rest[h].shape[0]):

                        @pl.when((label == name) & need & (place == i))
                        def _(h=h, i=i, out=out):
                            out[...] = rest[h][i]


def load_kernel(source, panels, sems):
    copies = []
    for s in range(source.shape[0]):
        for part in range(2):
            copy = pltpu.make_async_copy(source.at[s, part], panels.at[s, part], sems.at[2 * s + part])
            copy.start()
            copies.append(copy)
    for copy in copies:
        copy.wait()


FORTH = (1, 3, 0, 2)
BACK = (2, 0, 3, 1)


def chip_at(z, steps):
    if steps == 1:
        return jnp.where(z < 2, 2 * z + 1, 2 * z - 4)
    if steps == -1:
        return jnp.where(lax.rem(z, 2) == 0, 2 + z // 2, z // 2)
    return z if steps == 0 else 3 - z


def lay(terms, upper, lower):
    for ref, first in terms:
        count, _, g_local, t = ref.shape
        rows = pl.ds(first if isinstance(first, int) else pl.multiple_of(first, 128), g_local)
        for j in range(count):
            real, imag = slice(2 * j * t, (2 * j + 1) * t), slice((2 * j + 1) * t, (2 * j + 2) * t)
            upper[rows, real] = ref[j, 0]
            upper[rows, imag] = ref[j, 1]
            lower[rows, real] = -ref[j, 1]
            lower[rows, imag] = ref[j, 0]


def place():
    slot = lax.axis_index("ga")
    return slot // 2, lax.rem(slot, 2)


def multiply(screened, s, span, width, upper, lower, first=0):
    span = pl.ds(pl.multiple_of(span, 128), width)
    rows = slice(first, first + width)
    return dot(screened[s, 0, :, span], upper[rows]) + dot(screened[s, 1, :, span], lower[rows])


def first_kernel(screened, own, coulomb, total, upper, lower):
    z, core = place()
    g = screened.shape[2]
    lay([(own, 0)], upper, lower)
    span = pl.ds(pl.multiple_of((2 * z + core) * g, 128), g)
    line = lax.broadcasted_iota(jnp.int32, (g, g), 0)
    on = line == lax.broadcasted_iota(jnp.int32, (g, g), 1)
    for s in range(screened.shape[0]):
        real = screened[s, 0, :, span]
        real = jnp.where(on, (real.astype(F32) - 2.0 * coulomb[...]).astype(BF16), real)
        total[s] = dot(real, upper[...]) + dot(screened[s, 1, :, span], lower[...])


def step_kernel(steps, screened, own, pair, before, total, upper, lower):
    z, core = place()
    g = screened.shape[2]
    lay([(own, core * g), (pair, (1 - core) * g)], upper, lower)
    span = 2 * chip_at(z, steps) * g
    for s in range(screened.shape[0]):
        total[s] = before[s] + multiply(screened, s, span, 2 * g, upper, lower)


def second_kernel(steps, screened, own, pairs, before, total, upper, lower):
    z, core = place()
    g = screened.shape[2]
    lay([(own, core * g), (pairs.at[1], (1 - core) * g), (pairs.at[0], 2 * g)], upper, lower)
    span = 2 * chip_at(z, steps) * g
    left = (2 * z + 1 - core) * g
    for s in range(screened.shape[0]):
        value = before[s] + multiply(screened, s, span, 2 * g, upper, lower)
        total[s] = value + multiply(screened, s, left, g, upper, lower, 2 * g)


def last_kernel(chips, steps, j, screened, own, pair, before, far, keep, give, upper, lower):
    z, core = place()
    g = screened.shape[2]
    t = far.shape[-1]
    lay([(own.at[j : j + 1], core * g), (pair.at[j : j + 1], (1 - core) * g)], upper, lower)
    span = 2 * chip_at(z, steps) * g
    first = core == 0
    for s in range(screened.shape[0]):
        value = before[s, :, 2 * j * t : 2 * (j + 1) * t]
        image = (value + multiply(screened, s, span, 2 * g, upper, lower)).astype(BF16)
        by_real, by_imag = tdot(far[j, s, 0], image), tdot(far[j, s, 1], image)
        real = by_real[:, :t] + by_imag[:, t:]
        imag = by_real[:, t:] - by_imag[:, :t]
        parts = ((real, imag), (real.T, -imag.T))
        for which in range(2):
            for part in range(2):
                block = parts[which][part]
                block = block.reshape(chips, 2, t // (2 * chips), t)
                keep[:, s, which, part] = jnp.where(first, block[:, 0], block[:, 1])
                give[:, s, which, part] = jnp.where(first, block[:, 1], block[:, 0]).astype(BF16)


def split_kernel(near, far, keep, came, own, cross, sends):
    z = lax.axis_index("ga") // 2
    own[...] = keep[z] + came[z].astype(F32)
    cross[...] = keep[z ^ far] + came[z ^ far].astype(F32)
    for i, at in enumerate((z ^ near, z ^ 3)):
        sends[i] = (keep[at] + came[at].astype(F32)).astype(BF16)


def merge_kernel(own, cross, came, total, sends):
    total[...] = own[...] + came[0].astype(F32)
    sends[...] = (cross[...] + came[1].astype(F32)).astype(BF16)


def finish_kernel(count, chips, scale, *refs):
    kernel, mirror = refs[-2:]
    for j in range(count):
        terms = refs[j * chips : (j + 1) * chips]
        total = terms[0][...]
        for term in terms[1:]:
            total = total + term[...].astype(F32)
        mirror[j] = total[:, 0] * scale
        kernel[j] = total[:, 1] * scale


def quick(n_kp, n_ga, densities, screened, coulomb, block_rows):
    held, _, g_local, t = densities.shape
    transfers, g_total = screened.shape[0], screened.shape[3]
    count = block_rows.shape[1]
    chips = n_ga // 2
    half = g_local // 2
    shape = jax.ShapeDtypeStruct
    tie = lax.optimization_barrier

    def across(x, bit):
        return lax.ppermute(x, "kp", [(i, i ^ bit) for i in range(n_kp)])

    def other_core(x):
        return lax.ppermute(x, "ga", [(i, i ^ 1) for i in range(n_ga)])

    def along(x, chips_on):
        return lax.ppermute(x, "ga", [(i, 2 * chips_on[i // 2] + i % 2) for i in range(n_ga)])

    message = shape((2 * held * half + LABELS, t), BF16)

    def pack(panels):
        return run(pack_kernel, [message] * 2, block_rows, panels, specs=[SMEM, VMEM], name="pack")

    sums = shape((transfers, g_local, 2 * count * t), F32)

    def product(body, terms, *args):
        return run(
            body,
            sums,
            screened,
            *args,
            scratch=[pltpu.VMEM((terms * g_local, 2 * count * t), BF16)] * 2,
            aliases={} if terms == 1 else {3: 0},
            name="product",
            mib=24,
        )

    def pick(packed, came):
        sends = run(
            functools.partial(pick_kernel, held),
            [shape((count, 2, half, t), BF16)] * 2,
            *packed,
            *came,
            name="pick",
        )
        return [across(sends[h], BITS[h][1]) for h in range(2)]

    slices = shape((count, 2, g_local, t), BF16)

    def near_of(packed, came, picked):
        kernel = functools.partial(near_kernel, held)
        return run(kernel, slices, *packed, *came, *picked, name="near")

    before = along(densities, FORTH)
    packed = pack(densities)
    came = [across(packed[h], BITS[h][0]) for h in range(2)]
    source, packed = tie((screened, packed))
    screened = run(
        load_kernel,
        shape(screened.shape, screened.dtype),
        source,
        specs=[HBM],
        scratch=[pltpu.SemaphoreType.DMA((2 * transfers,))],
        name="load",
        mib=40,
    )
    came, screened = tie((came, screened))
    picked = pick(packed, came)
    packed_before = pack(before)
    rest_sends = run(
        functools.partial(rest_kernel, held, transfers, count),
        [shape((room, 2, half, t), BF16) for room in left_over(n_kp, held, transfers, count)],
        *packed,
        *came,
        name="rest",
    )
    picked = list(tie((picked, (packed_before, rest_sends)))[0])
    near = near_of(packed, came, picked)
    ahead = along(near, BACK)
    total = product(first_kernel, 1, near, coulomb[None, :])

    came_before = [across(packed_before[h], BITS[h][0]) for h in range(2)]
    came_before, total = tie((came_before, total))
    picked_before = pick(packed_before, came_before)
    near_before = near_of(packed_before, came_before, picked_before)
    behind = along(near_before, FORTH)

    rest_sends, ahead, _ = tie((rest_sends, ahead, near_before))
    rest = [across(rest_sends[h], BITS[h][1]) for h in range(2)]

    stack, _ = tie(((near, near_before), ahead))
    both = run(stack_kernel, shape((2, *slices.shape), BF16), *stack, name="stack")
    total = product(
        functools.partial(step_kernel, 1), 2, ahead, other_core(ahead), total
    )
    total = product(
        functools.partial(second_kernel, -1), 3, near_before, other_core(both), total
    )
    behind, rest, total = tie((behind, rest, total))
    far = run(
        functools.partial(far_kernel, held),
        shape((count, transfers, 2, g_local, t), BF16),
        *packed,
        *came,
        *picked,
        *rest,
        name="far",
    )

    parts = shape((chips, transfers, 2, 2, t // n_ga, t), F32)
    part = parts.shape[1:]
    pair = other_core(behind)
    swaps = []
    for j in range(count):
        keep, give = run(
            functools.partial(last_kernel, chips, -2, j),
            [parts, shape(parts.shape, BF16)],
            screened,
            behind,
            pair,
            total,
            far,
            scratch=[pltpu.VMEM((2 * g_local, 2 * t), BF16)] * 2,
            name="last",
            mib=24,
        )
        swaps.append((keep, other_core(give)))
    groups = []
    for j, (keep, came_j) in enumerate(swaps):
        near_z, far_z = ((1, 2), (2, 1))[j % 2]
        own, cross, sends = run(
            functools.partial(split_kernel, near_z, far_z),
            [shape(part, F32), shape(part, F32), shape((2, *part), BF16)],
            keep,
            came_j,
            name="split",
        )
        own, sends = run(
            merge_kernel,
            [shape(part, F32), shape(part, BF16)],
            own,
            cross,
            lax.ppermute(sends, "ga", [(i, i ^ (2 * near_z)) for i in range(n_ga)]),
            name="merge",
        )
        groups += [own, lax.ppermute(sends, "ga", [(i, i ^ (2 * far_z)) for i in range(n_ga)])]
    result = shape((count, transfers, 2, t // n_ga, t), F32)
    return tuple(
        run(
            functools.partial(finish_kernel, count, 2, -1.0 / math.sqrt(g_total)),
            [result] * 2,
            *groups,
            name="finish",
        )
    )


def plain(densities, screened, coulomb, block_rows):
    owner = lax.axis_index("kp")
    g_slot = lax.axis_index("ga")
    k_held = densities.shape[0]
    g_local = densities.shape[2]
    g_total = screened.shape[3]
    rows = block_rows[0]
    transfers = owner * k_held + jnp.arange(k_held, dtype=jnp.int32)
    far_rows = rows[:, None] + transfers[None, :]
    piece = lax.all_gather(densities, "kp", axis=0, tiled=True)
    labels = jnp.arange(piece.shape[0], dtype=jnp.int32)
    pick_near = (rows[:, None] == labels[None, :]).astype(jnp.bfloat16)
    pick_far = (far_rows[:, :, None] == labels[None, None, :]).astype(jnp.bfloat16)
    near_acc = jnp.einsum(
        "jp,pcgt->jcgt", pick_near, piece, preferred_element_type=jnp.float32
    ).astype(jnp.bfloat16)
    far_acc = jnp.einsum(
        "jsp,pcgt->jscgt", pick_far, piece, preferred_element_type=jnp.float32
    ).astype(jnp.bfloat16)
    columns = jnp.arange(g_total, dtype=jnp.int32)
    own_rows = g_slot * g_local + jnp.arange(g_local, dtype=jnp.int32)
    diag_mask = own_rows[:, None] == columns[None, :]
    coulomb_diag = jnp.where(diag_mask, 2.0 * coulomb[:, None], 0.0)
    screen_real = (coulomb_diag[None] - screened[:, 0].astype(jnp.float32)).astype(jnp.bfloat16)
    screen_imag = -screened[:, 1]
    near_all = lax.all_gather(near_acc, "ga", axis=2, tiled=True)
    piece_real = near_all[:, 0]
    piece_imag = near_all[:, 1]
    real_term = jnp.einsum(
        "sgh,jht->jsgt", screen_real, piece_real, preferred_element_type=jnp.float32
    ) - jnp.einsum("sgh,jht->jsgt", screen_imag, piece_imag, preferred_element_type=jnp.float32)
    imag_term = jnp.einsum(
        "sgh,jht->jsgt", screen_real, piece_imag, preferred_element_type=jnp.float32
    ) + jnp.einsum("sgh,jht->jsgt", screen_imag, piece_real, preferred_element_type=jnp.float32)
    image = jnp.stack([real_term, imag_term], 2)
    image = image.astype(jnp.bfloat16)
    image_real = image[:, :, 0]
    image_imag = image[:, :, 1]
    far_real = far_acc[:, :, 0]
    far_imag = far_acc[:, :, 1]
    lower_real = jnp.einsum(
        "jsga,jsgb->jsab", far_real, image_real, preferred_element_type=jnp.float32
    ) + jnp.einsum("jsga,jsgb->jsab", far_imag, image_imag, preferred_element_type=jnp.float32)
    lower_imag = jnp.einsum(
        "jsga,jsgb->jsab", far_real, image_imag, preferred_element_type=jnp.float32
    ) - jnp.einsum("jsga,jsgb->jsab", far_imag, image_real, preferred_element_type=jnp.float32)
    partial_lower = jnp.stack([lower_real, lower_imag], 2)
    inverse = 1.0 / math.sqrt(g_total)
    mirror = lax.psum_scatter(partial_lower, "ga", scatter_dimension=3, tiled=True) * inverse
    partial_upper = jnp.stack([jnp.swapaxes(lower_real, 2, 3), -jnp.swapaxes(lower_imag, 2, 3)], 2)
    kernel = lax.psum_scatter(partial_upper, "ga", scatter_dimension=3, tiled=True) * inverse
    return (kernel, mirror)


def solution(mesh):
    placed = (P("kp", None, "ga", None), P("kp", None, "ga", None), P("ga"), P("kp", None))
    n_kp, n_ga = mesh.shape["kp"], mesh.shape["ga"]

    def shards(densities, screened, coulomb, block_rows):
        g_local, t = densities.shape[2], densities.shape[3]
        fits = n_kp == 2 * 2 and n_ga == 4 * 2
        fits = fits and g_local % 128 == 0 and t % (8 * n_ga) == 0
        fits = fits and n_kp * densities.shape[0] <= 256
        if fits:
            return quick(n_kp, n_ga, densities, screened, coulomb, block_rows)
        return plain(densities, screened, coulomb, block_rows)

    return jax.shard_map(
        shards,
        mesh=mesh,
        in_specs=placed,
        out_specs=(P("kp", None, None, "ga", None), P("kp", None, None, "ga", None)),
        check_vma=False,
    )
```

```python
import functools
import itertools
import math

import jax
import jax.numpy as jnp
from jax import lax
from jax.experimental import pallas as pl
from jax.experimental.pallas import tpu as pltpu
from jax.sharding import PartitionSpec as P

F32 = jnp.float32
BF16 = jnp.bfloat16
LABELS = 16
VMEM = pl.BlockSpec(memory_space=pltpu.VMEM)
SMEM = pl.BlockSpec(memory_space=pltpu.SMEM)
HBM = pl.BlockSpec(memory_space=pltpu.HBM)


def dot(a, b):
    return jnp.dot(a, b, preferred_element_type=F32)


def tdot(a, b):
    return lax.dot_general(a, b, (((0,), (0,)), ((), ())), preferred_element_type=F32)


def run(body, out, *args, specs=None, scratch=(), name=None, aliases=None, mib=16):
    outs = out if isinstance(out, (list, tuple)) else [out]
    result = pl.pallas_call(
        body,
        in_specs=specs or [VMEM] * len(args),
        out_specs=[VMEM] * len(outs),
        out_shape=list(outs),
        scratch_shapes=list(scratch),
        input_output_aliases=aliases or {},
        compiler_params=pltpu.CompilerParams(vmem_limit_bytes=mib * 2**20),
        cost_estimate=pl.CostEstimate(flops=0, bytes_accessed=0, transcendentals=0),
        name=name,
    )(*args)
    return list(result) if isinstance(out, (list, tuple)) else result[0]


BITS = ((1, 2), (2, 1))


def pack_kernel(rows, densities, *sends):
    held, _, g_local, t = densities.shape
    half = g_local // 2
    for h in range(2):
        for k in range(held):
            for part in range(2):
                at = (2 * k + part) * half
                sends[h][at : at + half] = densities[k, part, h * half : (h + 1) * half]
        line = lax.broadcasted_iota(jnp.int32, (LABELS, t), 0)
        tile = jnp.zeros((LABELS, t), F32)
        for j in range(rows.shape[1]):
            tile = jnp.where(line == j, rows[0, j].astype(F32), tile)
        sends[h][2 * held * half :] = tile.astype(BF16)


def label_of(message, held, half, j):
    tail = message[2 * held * half :].astype(F32)
    return jnp.max(tail[j : j + 1]).astype(jnp.int32)


def entries(message, owner, held, half):
    return [(owner * held + k, message, 2 * k * half, (2 * k + 1) * half) for k in range(held)]


def copy_if(label, found, out):
    half = out.shape[1]
    hit = None
    for name, message, real, imag in found:
        match = label == name
        hit = match if hit is None else hit | match

        @pl.when(match)
        def _(message=message, real=real, imag=imag):
            out[0] = message[real : real + half]
            out[1] = message[imag : imag + half]

    return hit


def pick_kernel(held, packed_0, packed_1, came_0, came_1, *sends):
    owner = lax.axis_index("kp")
    packed, came = (packed_0, packed_1), (came_0, came_1)
    half = sends[0].shape[2]
    for j in range(sends[0].shape[0]):
        for h in range(2):
            found = entries(packed[h], owner, held, half)
            found += entries(came[h], owner ^ BITS[h][0], held, half)
            copy_if(label_of(came[1 - h], held, half, j), found, sends[h].at[j])


def near_kernel(held, packed_0, packed_1, came_0, came_1, picked_0, picked_1, near):
    owner = lax.axis_index("kp")
    packed, came, picked = (packed_0, packed_1), (came_0, came_1), (picked_0, picked_1)
    half = picked_0.shape[2]
    for j in range(near.shape[0]):
        label = label_of(packed_0, held, half, j)
        for h in range(2):
            out = near.at[j, :, h * half : (h + 1) * half]
            found = entries(packed[h], owner, held, half)
            found += entries(came[h], owner ^ BITS[h][0], held, half)
            hit = copy_if(label, found, out)

            @pl.when(jnp.logical_not(hit))
            def _(h=h, j=j, out=out):
                out[...] = picked[h][j]


def stack_kernel(*refs):
    for i, ref in enumerate(refs[:-1]):
        refs[-1][i] = ref[...]


def left_over(n_kp, held, transfers, count):
    most = []
    for first, second in BITS:
        worst = 0
        for owner in range(n_kp):
            side = {who * held + k for who in (owner ^ second, owner ^ second ^ first) for k in range(held)}
            rows = range(n_kp * held - transfers * (owner + 1) + 1)
            for chosen in itertools.product(rows, repeat=count):
                need = {r + owner * transfers + s for r in chosen for s in range(transfers)}
                worst = max(worst, len((need & side) - set(chosen)))
        most.append(max(worst, 1))
    return most


def slots(labels, rows, owner, transfers):
    found, place = [], jnp.int32(0)
    for label in labels:
        need, sent = jnp.bool_(False), jnp.bool_(False)
        for row in rows:
            first = row + owner * transfers
            need = need | ((label >= first) & (label < first + transfers))
            sent = sent | (label == row)
        need = need & jnp.logical_not(sent)
        found.append((need, place))
        place = place + need.astype(jnp.int32)
    return found


def rest_kernel(held, transfers, count, packed_0, packed_1, came_0, came_1, *sends):
    owner = lax.axis_index("kp")
    packed, came = (packed_0, packed_1), (came_0, came_1)
    for h in range(2):
        first, second = BITS[h]
        room, _, half, _ = sends[h].shape
        found = entries(packed[h], owner, held, half)
        found += entries(came[h], owner ^ first, held, half)
        rows = [label_of(came[1 - h], held, half, j) for j in range(count)]
        places = slots([label for label, *_ in found], rows, owner ^ second, transfers)
        for (_, message, real, imag), (need, place) in zip(found, places):
            for i in range(room):

                @pl.when(need & (place == i))
                def _(h=h, i=i, message=message, real=real, imag=imag, half=half):
                    sends[h][i, 0] = message[real : real + half]
                    sends[h][i, 1] = message[imag : imag + half]


def far_kernel(
    held, packed_0, packed_1, came_0, came_1, picked_0, picked_1, rest_0, rest_1, far
):
    owner = lax.axis_index("kp")
    packed, came = (packed_0, packed_1), (came_0, came_1)
    picked, rest = (picked_0, picked_1), (rest_0, rest_1)
    count, transfers, _, g_local, _ = far.shape
    half = g_local // 2
    rows = [label_of(packed_0, held, half, j) for j in range(count)]
    for h in range(2):
        first, second = BITS[h]
        found = entries(packed[h], owner, held, half)
        found += entries(came[h], owner ^ first, held, half)
        side = [
            who * held + k for who in (owner ^ second, owner ^ second ^ first) for k in range(held)
        ]
        places = slots(side, rows, owner, transfers)
        for j in range(count):
            for s in range(transfers):
                label = rows[j] + owner * transfers + s
                out = far.at[j, s, :, h * half : (h + 1) * half]
                hit = copy_if(label, found, out)
                for i in range(count):
                    match = (label == rows[i]) & jnp.logical_not(hit)
                    hit = hit | match

                    @pl.when(match)
                    def _(h=h, i=i, out=out):
                        out[...] = picked[h][i]

                for name, (need, place) in zip(side, places):
                    for i in range(rest[h].shape[0]):

                        @pl.when((label == name) & need & (place == i))
                        def _(h=h, i=i, out=out):
                            out[...] = rest[h][i]


def load_kernel(source, panels, sems):
    copies = []
    for s in range(source.shape[0]):
        for part in range(2):
            copy = pltpu.make_async_copy(source.at[s, part], panels.at[s, part], sems.at[2 * s + part])
            copy.start()
            copies.append(copy)
    for copy in copies:
        copy.wait()


FORTH = (1, 3, 0, 2)
BACK = (2, 0, 3, 1)


def chip_at(z, steps):
    if steps == 1:
        return jnp.where(z < 2, 2 * z + 1, 2 * z - 4)
    if steps == -1:
        return jnp.where(lax.rem(z, 2) == 0, 2 + z // 2, z // 2)
    return z if steps == 0 else 3 - z


def lay(terms, upper, lower):
    for ref, first in terms:
        count, _, g_local, t = ref.shape
        rows = pl.ds(first if isinstance(first, int) else pl.multiple_of(first, 128), g_local)
        for j in range(count):
            real, imag = slice(2 * j * t, (2 * j + 1) * t), slice((2 * j + 1) * t, (2 * j + 2) * t)
            upper[rows, real] = ref[j, 0]
            upper[rows, imag] = ref[j, 1]
            lower[rows, real] = -ref[j, 1]
            lower[rows, imag] = ref[j, 0]


def place():
    slot = lax.axis_index("ga")
    return slot // 2, lax.rem(slot, 2)


def multiply(screened, s, span, width, upper, lower, first=0):
    span = pl.ds(pl.multiple_of(span, 128), width)
    rows = slice(first, first + width)
    return dot(screened[s, 0, :, span], upper[rows]) + dot(screened[s, 1, :, span], lower[rows])


def first_kernel(screened, own, coulomb, total, upper, lower):
    z, core = place()
    g = screened.shape[2]
    lay([(own, 0)], upper, lower)
    span = pl.ds(pl.multiple_of((2 * z + core) * g, 128), g)
    line = lax.broadcasted_iota(jnp.int32, (g, g), 0)
    on = line == lax.broadcasted_iota(jnp.int32, (g, g), 1)
    for s in range(screened.shape[0]):
        real = screened[s, 0, :, span]
        real = jnp.where(on, (real.astype(F32) - 2.0 * coulomb[...]).astype(BF16), real)
        total[s] = dot(real, upper[...]) + dot(screened[s, 1, :, span], lower[...])


def step_kernel(steps, screened, own, pair, before, total, upper, lower):
    z, core = place()
    g = screened.shape[2]
    lay([(own, core * g), (pair, (1 - core) * g)], upper, lower)
    span = 2 * chip_at(z, steps) * g
    for s in range(screened.shape[0]):
        total[s] = before[s] + multiply(screened, s, span, 2 * g, upper, lower)


def second_kernel(steps, screened, own, pairs, before, total, upper, lower):
    z, core = place()
    g = screened.shape[2]
    lay([(own, core * g), (pairs.at[1], (1 - core) * g), (pairs.at[0], 2 * g)], upper, lower)
    span = 2 * chip_at(z, steps) * g
    left = (2 * z + 1 - core) * g
    for s in range(screened.shape[0]):
        value = before[s] + multiply(screened, s, span, 2 * g, upper, lower)
        total[s] = value + multiply(screened, s, left, g, upper, lower, 2 * g)


def last_kernel(chips, steps, j, screened, own, pair, before, far, keep, give, upper, lower):
    z, core = place()
    g = screened.shape[2]
    t = far.shape[-1]
    lay([(own.at[j : j + 1], core * g), (pair.at[j : j + 1], (1 - core) * g)], upper, lower)
    span = 2 * chip_at(z, steps) * g
    first = core == 0
    for s in range(screened.shape[0]):
        value = before[s, :, 2 * j * t : 2 * (j + 1) * t]
        image = (value + multiply(screened, s, span, 2 * g, upper, lower)).astype(BF16)
        by_real, by_imag = tdot(far[j, s, 0], image), tdot(far[j, s, 1], image)
        real = by_real[:, :t] + by_imag[:, t:]
        imag = by_real[:, t:] - by_imag[:, :t]
        parts = ((real, imag), (real.T, -imag.T))
        for which in range(2):
            for part in range(2):
                block = parts[which][part]
                block = block.reshape(chips, 2, t // (2 * chips), t)
                keep[:, s, which, part] = jnp.where(first, block[:, 0], block[:, 1])
                give[:, s, which, part] = jnp.where(first, block[:, 1], block[:, 0]).astype(BF16)


def split_kernel(near, far, keep, came, own, cross, sends):
    z = lax.axis_index("ga") // 2
    own[...] = keep[z] + came[z].astype(F32)
    cross[...] = keep[z ^ far] + came[z ^ far].astype(F32)
    for i, at in enumerate((z ^ near, z ^ 3)):
        sends[i] = (keep[at] + came[at].astype(F32)).astype(BF16)


def merge_kernel(own, cross, came, total, sends):
    total[...] = own[...] + came[0].astype(F32)
    sends[...] = (cross[...] + came[1].astype(F32)).astype(BF16)


def finish_kernel(count, chips, scale, *refs):
    kernel, mirror = refs[-2:]
    for j in range(count):
        terms = refs[j * chips : (j + 1) * chips]
        total = terms[0][...]
        for term in terms[1:]:
            total = total + term[...].astype(F32)
        mirror[j] = total[:, 0] * scale
        kernel[j] = total[:, 1] * scale


def quick(n_kp, n_ga, densities, screened, coulomb, block_rows):
    held, _, g_local, t = densities.shape
    transfers, g_total = screened.shape[0], screened.shape[3]
    count = block_rows.shape[1]
    chips = n_ga // 2
    half = g_local // 2
    shape = jax.ShapeDtypeStruct
    tie = lax.optimization_barrier

    def across(x, bit):
        return lax.ppermute(x, "kp", [(i, i ^ bit) for i in range(n_kp)])

    def other_core(x):
        return lax.ppermute(x, "ga", [(i, i ^ 1) for i in range(n_ga)])

    def along(x, chips_on):
        return lax.ppermute(x, "ga", [(i, 2 * chips_on[i // 2] + i % 2) for i in range(n_ga)])

    message = shape((2 * held * half + LABELS, t), BF16)

    def pack(panels):
        return run(pack_kernel, [message] * 2, block_rows, panels, specs=[SMEM, VMEM], name="pack")

    sums = shape((transfers, g_local, 2 * count * t), F32)

    def product(body, terms, *args):
        return run(
            body,
            sums,
            screened,
            *args,
            scratch=[pltpu.VMEM((terms * g_local, 2 * count * t), BF16)] * 2,
            aliases={} if terms == 1 else {3: 0},
            name="product",
            mib=24,
        )

    def pick(packed, came):
        sends = run(
            functools.partial(pick_kernel, held),
            [shape((count, 2, half, t), BF16)] * 2,
            *packed,
            *came,
            name="pick",
        )
        return [across(sends[h], BITS[h][1]) for h in range(2)]

    slices = shape((count, 2, g_local, t), BF16)

    def near_of(packed, came, picked):
        kernel = functools.partial(near_kernel, held)
        return run(kernel, slices, *packed, *came, *picked, name="near")

    before = along(densities, FORTH)
    packed = pack(densities)
    came = [across(packed[h], BITS[h][0]) for h in range(2)]
    source, packed = tie((screened, packed))
    screened = run(
        load_kernel,
        shape(screened.shape, screened.dtype),
        source,
        specs=[HBM],
        scratch=[pltpu.SemaphoreType.DMA((2 * transfers,))],
        name="load",
        mib=40,
    )
    came, screened = tie((came, screened))
    picked = pick(packed, came)
    packed_before = pack(before)
    rest_sends = run(
        functools.partial(rest_kernel, held, transfers, count),
        [shape((room, 2, half, t), BF16) for room in left_over(n_kp, held, transfers, count)],
        *packed,
        *came,
        name="rest",
    )
    picked = list(tie((picked, (packed_before, rest_sends)))[0])
    near = near_of(packed, came, picked)
    ahead = along(near, BACK)
    total = product(first_kernel, 1, near, coulomb[None, :])

    came_before = [across(packed_before[h], BITS[h][0]) for h in range(2)]
    came_before, total = tie((came_before, total))
    picked_before = pick(packed_before, came_before)
    near_before = near_of(packed_before, came_before, picked_before)
    behind = along(near_before, FORTH)

    rest_sends, ahead, _ = tie((rest_sends, ahead, near_before))
    rest = [across(rest_sends[h], BITS[h][1]) for h in range(2)]

    stack, _ = tie(((near, near_before), ahead))
    both = run(stack_kernel, shape((2, *slices.shape), BF16), *stack, name="stack")
    total = product(
        functools.partial(step_kernel, 1), 2, ahead, other_core(ahead), total
    )
    total = product(
        functools.partial(second_kernel, -1), 3, near_before, other_core(both), total
    )
    behind, rest, total = tie((behind, rest, total))
    far = run(
        functools.partial(far_kernel, held),
        shape((count, transfers, 2, g_local, t), BF16),
        *packed,
        *came,
        *picked,
        *rest,
        name="far",
    )

    parts = shape((chips, transfers, 2, 2, t // n_ga, t), F32)
    part = parts.shape[1:]
    pair = other_core(behind)
    swaps = []
    for j in range(count):
        keep, give = run(
            functools.partial(last_kernel, chips, -2, j),
            [parts, shape(parts.shape, BF16)],
            screened,
            behind,
            pair,
            total,
            far,
            scratch=[pltpu.VMEM((2 * g_local, 2 * t), BF16)] * 2,
            name="last",
            mib=24,
        )
        swaps.append((keep, other_core(give)))
    groups = []
    for j, (keep, came_j) in enumerate(swaps):
        near_z, far_z = ((2, 1), (1, 2))[j % 2]
        own, cross, sends = run(
            functools.partial(split_kernel, near_z, far_z),
            [shape(part, F32), shape(part, F32), shape((2, *part), BF16)],
            keep,
            came_j,
            name="split",
        )
        own, sends = run(
            merge_kernel,
            [shape(part, F32), shape(part, BF16)],
            own,
            cross,
            lax.ppermute(sends, "ga", [(i, i ^ (2 * near_z)) for i in range(n_ga)]),
            name="merge",
        )
        groups += [own, lax.ppermute(sends, "ga", [(i, i ^ (2 * far_z)) for i in range(n_ga)])]
    result = shape((count, transfers, 2, t // n_ga, t), F32)
    return tuple(
        run(
            functools.partial(finish_kernel, count, 2, -1.0 / math.sqrt(g_total)),
            [result] * 2,
            *groups,
            name="finish",
        )
    )


def plain(densities, screened, coulomb, block_rows):
    owner = lax.axis_index("kp")
    g_slot = lax.axis_index("ga")
    k_held = densities.shape[0]
    g_local = densities.shape[2]
    g_total = screened.shape[3]
    rows = block_rows[0]
    transfers = owner * k_held + jnp.arange(k_held, dtype=jnp.int32)
    far_rows = rows[:, None] + transfers[None, :]
    piece = lax.all_gather(densities, "kp", axis=0, tiled=True)
    labels = jnp.arange(piece.shape[0], dtype=jnp.int32)
    pick_near = (rows[:, None] == labels[None, :]).astype(jnp.bfloat16)
    pick_far = (far_rows[:, :, None] == labels[None, None, :]).astype(jnp.bfloat16)
    near_acc = jnp.einsum(
        "jp,pcgt->jcgt", pick_near, piece, preferred_element_type=jnp.float32
    ).astype(jnp.bfloat16)
    far_acc = jnp.einsum(
        "jsp,pcgt->jscgt", pick_far, piece, preferred_element_type=jnp.float32
    ).astype(jnp.bfloat16)
    columns = jnp.arange(g_total, dtype=jnp.int32)
    own_rows = g_slot * g_local + jnp.arange(g_local, dtype=jnp.int32)
    diag_mask = own_rows[:, None] == columns[None, :]
    coulomb_diag = jnp.where(diag_mask, 2.0 * coulomb[:, None], 0.0)
    screen_real = (coulomb_diag[None] - screened[:, 0].astype(jnp.float32)).astype(jnp.bfloat16)
    screen_imag = -screened[:, 1]
    near_all = lax.all_gather(near_acc, "ga", axis=2, tiled=True)
    piece_real = near_all[:, 0]
    piece_imag = near_all[:, 1]
    real_term = jnp.einsum(
        "sgh,jht->jsgt", screen_real, piece_real, preferred_element_type=jnp.float32
    ) - jnp.einsum("sgh,jht->jsgt", screen_imag, piece_imag, preferred_element_type=jnp.float32)
    imag_term = jnp.einsum(
        "sgh,jht->jsgt", screen_real, piece_imag, preferred_element_type=jnp.float32
    ) + jnp.einsum("sgh,jht->jsgt", screen_imag, piece_real, preferred_element_type=jnp.float32)
    image = jnp.stack([real_term, imag_term], 2)
    image = image.astype(jnp.bfloat16)
    image_real = image[:, :, 0]
    image_imag = image[:, :, 1]
    far_real = far_acc[:, :, 0]
    far_imag = far_acc[:, :, 1]
    lower_real = jnp.einsum(
        "jsga,jsgb->jsab", far_real, image_real, preferred_element_type=jnp.float32
    ) + jnp.einsum("jsga,jsgb->jsab", far_imag, image_imag, preferred_element_type=jnp.float32)
    lower_imag = jnp.einsum(
        "jsga,jsgb->jsab", far_real, image_imag, preferred_element_type=jnp.float32
    ) - jnp.einsum("jsga,jsgb->jsab", far_imag, image_real, preferred_element_type=jnp.float32)
    partial_lower = jnp.stack([lower_real, lower_imag], 2)
    inverse = 1.0 / math.sqrt(g_total)
    mirror = lax.psum_scatter(partial_lower, "ga", scatter_dimension=3, tiled=True) * inverse
    partial_upper = jnp.stack([jnp.swapaxes(lower_real, 2, 3), -jnp.swapaxes(lower_imag, 2, 3)], 2)
    kernel = lax.psum_scatter(partial_upper, "ga", scatter_dimension=3, tiled=True) * inverse
    return (kernel, mirror)


def solution(mesh):
    placed = (P("kp", None, "ga", None), P("kp", None, "ga", None), P("ga"), P("kp", None))
    n_kp, n_ga = mesh.shape["kp"], mesh.shape["ga"]

    def shards(densities, screened, coulomb, block_rows):
        g_local, t = densities.shape[2], densities.shape[3]
        fits = n_kp == 2 * 2 and n_ga == 4 * 2
        fits = fits and g_local % 128 == 0 and t % (8 * n_ga) == 0
        fits = fits and n_kp * densities.shape[0] <= 256
        if fits:
            return quick(n_kp, n_ga, densities, screened, coulomb, block_rows)
        return plain(densities, screened, coulomb, block_rows)

    return jax.shard_map(
        shards,
        mesh=mesh,
        in_specs=placed,
        out_specs=(P("kp", None, None, "ga", None), P("kp", None, None, "ga", None)),
        check_vma=False,
    )
```

```python
import functools
import itertools
import math

import jax
import jax.numpy as jnp
from jax import lax
from jax.experimental import pallas as pl
from jax.experimental.pallas import tpu as pltpu
from jax.sharding import PartitionSpec as P

F32 = jnp.float32
BF16 = jnp.bfloat16
LABELS = 16
VMEM = pl.BlockSpec(memory_space=pltpu.VMEM)
SMEM = pl.BlockSpec(memory_space=pltpu.SMEM)
HBM = pl.BlockSpec(memory_space=pltpu.HBM)


def dot(a, b):
    return jnp.dot(a, b, preferred_element_type=F32)


def tdot(a, b):
    return lax.dot_general(a, b, (((0,), (0,)), ((), ())), preferred_element_type=F32)


def run(body, out, *args, specs=None, scratch=(), name=None, aliases=None, mib=16):
    outs = out if isinstance(out, (list, tuple)) else [out]
    result = pl.pallas_call(
        body,
        in_specs=specs or [VMEM] * len(args),
        out_specs=[VMEM] * len(outs),
        out_shape=list(outs),
        scratch_shapes=list(scratch),
        input_output_aliases=aliases or {},
        compiler_params=pltpu.CompilerParams(vmem_limit_bytes=mib * 2**20),
        cost_estimate=pl.CostEstimate(flops=0, bytes_accessed=0, transcendentals=0),
        name=name,
    )(*args)
    return list(result) if isinstance(out, (list, tuple)) else result[0]


BITS = ((1, 2), (2, 1))


def pack_kernel(rows, densities, *sends):
    held, _, g_local, t = densities.shape
    half = g_local // 2
    for h in range(2):
        for k in range(held):
            for part in range(2):
                at = (2 * k + part) * half
                sends[h][at : at + half] = densities[k, part, h * half : (h + 1) * half]
        line = lax.broadcasted_iota(jnp.int32, (LABELS, t), 0)
        tile = jnp.zeros((LABELS, t), F32)
        for j in range(rows.shape[1]):
            tile = jnp.where(line == j, rows[0, j].astype(F32), tile)
        sends[h][2 * held * half :] = tile.astype(BF16)


def label_of(message, held, half, j):
    tail = message[2 * held * half :].astype(F32)
    return jnp.max(tail[j : j + 1]).astype(jnp.int32)


def entries(message, owner, held, half):
    return [(owner * held + k, message, 2 * k * half, (2 * k + 1) * half) for k in range(held)]


def copy_if(label, found, out):
    half = out.shape[1]
    hit = None
    for name, message, real, imag in found:
        match = label == name
        hit = match if hit is None else hit | match

        @pl.when(match)
        def _(message=message, real=real, imag=imag):
            out[0] = message[real : real + half]
            out[1] = message[imag : imag + half]

    return hit


def pick_kernel(held, packed_0, packed_1, came_0, came_1, *sends):
    owner = lax.axis_index("kp")
    packed, came = (packed_0, packed_1), (came_0, came_1)
    half = sends[0].shape[2]
    for j in range(sends[0].shape[0]):
        for h in range(2):
            found = entries(packed[h], owner, held, half)
            found += entries(came[h], owner ^ BITS[h][0], held, half)
            copy_if(label_of(came[1 - h], held, half, j), found, sends[h].at[j])


def near_kernel(held, packed_0, packed_1, came_0, came_1, picked_0, picked_1, near, *each):
    owner = lax.axis_index("kp")
    packed, came, picked = (packed_0, packed_1), (came_0, came_1), (picked_0, picked_1)
    half = picked_0.shape[2]
    for j in range(near.shape[0]):
        label = label_of(packed_0, held, half, j)
        for h in range(2):
            out = near.at[j, :, h * half : (h + 1) * half]
            found = entries(packed[h], owner, held, half)
            found += entries(came[h], owner ^ BITS[h][0], held, half)
            hit = copy_if(label, found, out)

            @pl.when(jnp.logical_not(hit))
            def _(h=h, j=j, out=out):
                out[...] = picked[h][j]

    for j, out in enumerate(each):
        out[...] = near[j]


def stack_kernel(*refs):
    for i, ref in enumerate(refs[:-1]):
        refs[-1][i] = ref[...]


def left_over(n_kp, held, transfers, count):
    most = []
    for first, second in BITS:
        worst = 0
        for owner in range(n_kp):
            side = {who * held + k for who in (owner ^ second, owner ^ second ^ first) for k in range(held)}
            rows = range(n_kp * held - transfers * (owner + 1) + 1)
            for chosen in itertools.product(rows, repeat=count):
                need = {r + owner * transfers + s for r in chosen for s in range(transfers)}
                worst = max(worst, len((need & side) - set(chosen)))
        most.append(max(worst, 1))
    return most


def slots(labels, rows, owner, transfers):
    found, place = [], jnp.int32(0)
    for label in labels:
        need, sent = jnp.bool_(False), jnp.bool_(False)
        for row in rows:
            first = row + owner * transfers
            need = need | ((label >= first) & (label < first + transfers))
            sent = sent | (label == row)
        need = need & jnp.logical_not(sent)
        found.append((need, place))
        place = place + need.astype(jnp.int32)
    return found


def rest_kernel(held, transfers, count, packed_0, packed_1, came_0, came_1, *sends):
    owner = lax.axis_index("kp")
    packed, came = (packed_0, packed_1), (came_0, came_1)
    for h in range(2):
        first, second = BITS[h]
        room, _, half, _ = sends[h].shape
        found = entries(packed[h], owner, held, half)
        found += entries(came[h], owner ^ first, held, half)
        rows = [label_of(came[1 - h], held, half, j) for j in range(count)]
        places = slots([label for label, *_ in found], rows, owner ^ second, transfers)
        for (_, message, real, imag), (need, place) in zip(found, places):
            for i in range(room):

                @pl.when(need & (place == i))
                def _(h=h, i=i, message=message, real=real, imag=imag, half=half):
                    sends[h][i, 0] = message[real : real + half]
                    sends[h][i, 1] = message[imag : imag + half]


def far_kernel(
    held, packed_0, packed_1, came_0, came_1, picked_0, picked_1, rest_0, rest_1, far
):
    owner = lax.axis_index("kp")
    packed, came = (packed_0, packed_1), (came_0, came_1)
    picked, rest = (picked_0, picked_1), (rest_0, rest_1)
    count, transfers, _, g_local, _ = far.shape
    half = g_local // 2
    rows = [label_of(packed_0, held, half, j) for j in range(count)]
    for h in range(2):
        first, second = BITS[h]
        found = entries(packed[h], owner, held, half)
        found += entries(came[h], owner ^ first, held, half)
        side = [
            who * held + k for who in (owner ^ second, owner ^ second ^ first) for k in range(held)
        ]
        places = slots(side, rows, owner, transfers)
        for j in range(count):
            for s in range(transfers):
                label = rows[j] + owner * transfers + s
                out = far.at[j, s, :, h * half : (h + 1) * half]
                hit = copy_if(label, found, out)
                for i in range(count):
                    match = (label == rows[i]) & jnp.logical_not(hit)
                    hit = hit | match

                    @pl.when(match)
                    def _(h=h, i=i, out=out):
                        out[...] = picked[h][i]

                for name, (need, place) in zip(side, places):
                    for i in range(rest[h].shape[0]):

                        @pl.when((label == name) & need & (place == i))
                        def _(h=h, i=i, out=out):
                            out[...] = rest[h][i]


def load_kernel(source, panels, sems):
    copies = []
    for s in range(source.shape[0]):
        for part in range(2):
            copy = pltpu.make_async_copy(source.at[s, part], panels.at[s, part], sems.at[2 * s + part])
            copy.start()
            copies.append(copy)
    for copy in copies:
        copy.wait()


FORTH = (1, 3, 0, 2)
BACK = (2, 0, 3, 1)


def chip_at(z, steps):
    if steps == 1:
        return jnp.where(z < 2, 2 * z + 1, 2 * z - 4)
    if steps == -1:
        return jnp.where(lax.rem(z, 2) == 0, 2 + z // 2, z // 2)
    return z if steps == 0 else 3 - z


def lay(terms, upper, lower):
    for ref, first in terms:
        *count, _, g_local, t = ref.shape
        rows = pl.ds(first if isinstance(first, int) else pl.multiple_of(first, 128), g_local)
        for j, panel in enumerate([ref.at[j] for j in range(count[0])] if count else [ref]):
            real, imag = slice(2 * j * t, (2 * j + 1) * t), slice((2 * j + 1) * t, (2 * j + 2) * t)
            upper[rows, real] = panel[0]
            upper[rows, imag] = panel[1]
            lower[rows, real] = -panel[1]
            lower[rows, imag] = panel[0]


def place():
    slot = lax.axis_index("ga")
    return slot // 2, lax.rem(slot, 2)


def multiply(screened, s, span, width, upper, lower, first=0):
    span = pl.ds(pl.multiple_of(span, 128), width)
    rows = slice(first, first + width)
    return dot(screened[s, 0, :, span], upper[rows]) + dot(screened[s, 1, :, span], lower[rows])


def first_kernel(screened, own, coulomb, total, upper, lower):
    z, core = place()
    g = screened.shape[2]
    lay([(own, 0)], upper, lower)
    span = pl.ds(pl.multiple_of((2 * z + core) * g, 128), g)
    line = lax.broadcasted_iota(jnp.int32, (g, g), 0)
    on = line == lax.broadcasted_iota(jnp.int32, (g, g), 1)
    for s in range(screened.shape[0]):
        real = screened[s, 0, :, span]
        real = jnp.where(on, (real.astype(F32) - 2.0 * coulomb[...]).astype(BF16), real)
        total[s] = dot(real, upper[...]) + dot(screened[s, 1, :, span], lower[...])


def step_kernel(steps, screened, own, pair, before, total, upper, lower):
    z, core = place()
    g = screened.shape[2]
    lay([(own, core * g), (pair, (1 - core) * g)], upper, lower)
    span = 2 * chip_at(z, steps) * g
    for s in range(screened.shape[0]):
        total[s] = before[s] + multiply(screened, s, span, 2 * g, upper, lower)


def second_kernel(steps, screened, own, pairs, before, total, upper, lower):
    z, core = place()
    g = screened.shape[2]
    lay([(own, core * g), (pairs.at[1], (1 - core) * g), (pairs.at[0], 2 * g)], upper, lower)
    span = 2 * chip_at(z, steps) * g
    left = (2 * z + 1 - core) * g
    for s in range(screened.shape[0]):
        value = before[s] + multiply(screened, s, span, 2 * g, upper, lower)
        total[s] = value + multiply(screened, s, left, g, upper, lower, 2 * g)


def last_kernel(chips, steps, j, screened, own, pair, before, far, keep, *refs):
    z, core = place()
    g = screened.shape[2]
    t = far.shape[-1]
    *gives, upper, lower = refs
    lay([(own, core * g), (pair, (1 - core) * g)], upper, lower)
    span = 2 * chip_at(z, steps) * g
    first = core == 0
    for s in range(screened.shape[0]):
        value = before[s, :, 2 * j * t : 2 * (j + 1) * t]
        image = (value + multiply(screened, s, span, 2 * g, upper, lower)).astype(BF16)
        by_real, by_imag = tdot(far[j, s, 0], image), tdot(far[j, s, 1], image)
        real = by_real[:, :t] + by_imag[:, t:]
        imag = by_real[:, t:] - by_imag[:, :t]
        parts = ((real, imag), (real.T, -imag.T))
        for which in range(2):
            for part in range(2):
                block = parts[which][part]
                block = block.reshape(chips, 2, t // (2 * chips), t)
                keep[:, s, which, part] = jnp.where(first, block[:, 0], block[:, 1])
                give = jnp.where(first, block[:, 1], block[:, 0])
                gives[2 * s + which][:, part] = give.astype(BF16)


def split_kernel(keep, *refs):
    *came, own, cross, sends = refs
    z = lax.axis_index("ga") // 2
    for s in range(keep.shape[1]):
        for which in range(2):

            def chip(at):
                return keep[at, s, which] + came[2 * s + which][at].astype(F32)

            own[s, which] = chip(z)
            cross[s, which] = chip(z ^ 2)
            for i, at in enumerate((z ^ 1, z ^ 3)):
                sends[i, s, which] = chip(at).astype(BF16)


def merge_kernel(own, cross, came, total, sends):
    total[...] = own[...] + came[0].astype(F32)
    sends[...] = (cross[...] + came[1].astype(F32)).astype(BF16)


def finish_kernel(count, chips, scale, *refs):
    kernel, mirror = refs[-2:]
    for j in range(count):
        terms = refs[j * chips : (j + 1) * chips]
        total = terms[0][...]
        for term in terms[1:]:
            total = total + term[...].astype(F32)
        mirror[j] = total[:, 0] * scale
        kernel[j] = total[:, 1] * scale


def quick(n_kp, n_ga, densities, screened, coulomb, block_rows):
    held, _, g_local, t = densities.shape
    transfers, g_total = screened.shape[0], screened.shape[3]
    count = block_rows.shape[1]
    chips = n_ga // 2
    half = g_local // 2
    shape = jax.ShapeDtypeStruct
    tie = lax.optimization_barrier

    def across(x, bit):
        return lax.ppermute(x, "kp", [(i, i ^ bit) for i in range(n_kp)])

    def other_core(x):
        return lax.ppermute(x, "ga", [(i, i ^ 1) for i in range(n_ga)])

    def along(x, chips_on):
        return lax.ppermute(x, "ga", [(i, 2 * chips_on[i // 2] + i % 2) for i in range(n_ga)])

    message = shape((2 * held * half + LABELS, t), BF16)

    def pack(panels):
        return run(pack_kernel, [message] * 2, block_rows, panels, specs=[SMEM, VMEM], name="pack")

    sums = shape((transfers, g_local, 2 * count * t), F32)

    def product(body, terms, *args):
        return run(
            body,
            sums,
            screened,
            *args,
            scratch=[pltpu.VMEM((terms * g_local, 2 * count * t), BF16)] * 2,
            aliases={} if terms == 1 else {3: 0},
            name="product",
            mib=24,
        )

    def pick(packed, came):
        sends = run(
            functools.partial(pick_kernel, held),
            [shape((count, 2, half, t), BF16)] * 2,
            *packed,
            *came,
            name="pick",
        )
        return [across(sends[h], BITS[h][1]) for h in range(2)]

    slices = shape((count, 2, g_local, t), BF16)

    def near_of(packed, came, picked, apart=False):
        kernel = functools.partial(near_kernel, held)
        outs = [slices] + [shape(slices.shape[1:], BF16)] * (count if apart else 0)
        near, *each = run(kernel, outs, *packed, *came, *picked, name="near")
        return (near, each) if apart else near

    before = along(densities, FORTH)
    packed = pack(densities)
    came = [across(packed[h], BITS[h][0]) for h in range(2)]
    source, packed = tie((screened, packed))
    screened = run(
        load_kernel,
        shape(screened.shape, screened.dtype),
        source,
        specs=[HBM],
        scratch=[pltpu.SemaphoreType.DMA((2 * transfers,))],
        name="load",
        mib=40,
    )
    came, screened = tie((came, screened))
    picked = pick(packed, came)
    packed_before = pack(before)
    rest_sends = run(
        functools.partial(rest_kernel, held, transfers, count),
        [shape((room, 2, half, t), BF16) for room in left_over(n_kp, held, transfers, count)],
        *packed,
        *came,
        name="rest",
    )
    picked = list(tie((picked, (packed_before, rest_sends)))[0])
    near = near_of(packed, came, picked)
    ahead = along(near, BACK)
    total = product(first_kernel, 1, near, coulomb[None, :])

    came_before = [across(packed_before[h], BITS[h][0]) for h in range(2)]
    came_before, total = tie((came_before, total))
    picked_before = pick(packed_before, came_before)
    near_before, before_each = near_of(packed_before, came_before, picked_before, True)
    behind = [along(x, FORTH) for x in before_each]

    rest_sends, ahead, _ = tie((rest_sends, ahead, near_before))
    rest = [across(rest_sends[h], BITS[h][1]) for h in range(2)]

    stack, _ = tie(((near, near_before), ahead))
    both = run(stack_kernel, shape((2, *slices.shape), BF16), *stack, name="stack")
    total = product(
        functools.partial(step_kernel, 1), 2, ahead, other_core(ahead), total
    )
    total = product(
        functools.partial(second_kernel, -1), 3, near_before, other_core(both), total
    )
    behind[0], _ = tie((behind[0], total))
    rest, total = tie((rest, total))
    far = run(
        functools.partial(far_kernel, held),
        shape((count, transfers, 2, g_local, t), BF16),
        *packed,
        *came,
        *picked,
        *rest,
        name="far",
    )

    parts = shape((chips, transfers, 2, 2, t // n_ga, t), F32)
    part = parts.shape[1:]
    behind[1:], _ = tie((behind[1:], far))
    stages = []
    done = total
    for j in range(count):
        total, _ = tie((total, done))
        keep, *gives = run(
            functools.partial(last_kernel, chips, -2, j),
            [parts] + [shape((chips, 2, t // n_ga, t), BF16)] * (2 * transfers),
            screened,
            behind[j],
            other_core(behind[j]),
            total,
            far,
            scratch=[pltpu.VMEM((2 * g_local, 2 * t), BF16)] * 2,
            name="last",
            mib=24,
        )
        own, cross, sends = run(
            split_kernel,
            [shape(part, F32), shape(part, F32), shape((2, *part), BF16)],
            keep,
            *[other_core(x) for x in gives],
            name="split",
        )
        if stages:
            sends, _ = tie((sends, stages[-1][2]))
        done = own
        came_j = lax.ppermute(sends, "ga", [(i, i ^ 2) for i in range(n_ga)])
        stages.append((own, cross, came_j))
    groups = []
    for own, cross, came_j in stages:
        own, sends = run(
            merge_kernel, [shape(part, F32), shape(part, BF16)], own, cross, came_j, name="merge"
        )
        groups += [own, lax.ppermute(sends, "ga", [(i, i ^ 4) for i in range(n_ga)])]
    result = shape((count, transfers, 2, t // n_ga, t), F32)
    return tuple(
        run(
            functools.partial(finish_kernel, count, 2, -1.0 / math.sqrt(g_total)),
            [result] * 2,
            *groups,
            name="finish",
        )
    )


def plain(densities, screened, coulomb, block_rows):
    owner = lax.axis_index("kp")
    g_slot = lax.axis_index("ga")
    k_held = densities.shape[0]
    g_local = densities.shape[2]
    g_total = screened.shape[3]
    rows = block_rows[0]
    transfers = owner * k_held + jnp.arange(k_held, dtype=jnp.int32)
    far_rows = rows[:, None] + transfers[None, :]
    piece = lax.all_gather(densities, "kp", axis=0, tiled=True)
    labels = jnp.arange(piece.shape[0], dtype=jnp.int32)
    pick_near = (rows[:, None] == labels[None, :]).astype(jnp.bfloat16)
    pick_far = (far_rows[:, :, None] == labels[None, None, :]).astype(jnp.bfloat16)
    near_acc = jnp.einsum(
        "jp,pcgt->jcgt", pick_near, piece, preferred_element_type=jnp.float32
    ).astype(jnp.bfloat16)
    far_acc = jnp.einsum(
        "jsp,pcgt->jscgt", pick_far, piece, preferred_element_type=jnp.float32
    ).astype(jnp.bfloat16)
    columns = jnp.arange(g_total, dtype=jnp.int32)
    own_rows = g_slot * g_local + jnp.arange(g_local, dtype=jnp.int32)
    diag_mask = own_rows[:, None] == columns[None, :]
    coulomb_diag = jnp.where(diag_mask, 2.0 * coulomb[:, None], 0.0)
    screen_real = (coulomb_diag[None] - screened[:, 0].astype(jnp.float32)).astype(jnp.bfloat16)
    screen_imag = -screened[:, 1]
    near_all = lax.all_gather(near_acc, "ga", axis=2, tiled=True)
    piece_real = near_all[:, 0]
    piece_imag = near_all[:, 1]
    real_term = jnp.einsum(
        "sgh,jht->jsgt", screen_real, piece_real, preferred_element_type=jnp.float32
    ) - jnp.einsum("sgh,jht->jsgt", screen_imag, piece_imag, preferred_element_type=jnp.float32)
    imag_term = jnp.einsum(
        "sgh,jht->jsgt", screen_real, piece_imag, preferred_element_type=jnp.float32
    ) + jnp.einsum("sgh,jht->jsgt", screen_imag, piece_real, preferred_element_type=jnp.float32)
    image = jnp.stack([real_term, imag_term], 2)
    image = image.astype(jnp.bfloat16)
    image_real = image[:, :, 0]
    image_imag = image[:, :, 1]
    far_real = far_acc[:, :, 0]
    far_imag = far_acc[:, :, 1]
    lower_real = jnp.einsum(
        "jsga,jsgb->jsab", far_real, image_real, preferred_element_type=jnp.float32
    ) + jnp.einsum("jsga,jsgb->jsab", far_imag, image_imag, preferred_element_type=jnp.float32)
    lower_imag = jnp.einsum(
        "jsga,jsgb->jsab", far_real, image_imag, preferred_element_type=jnp.float32
    ) - jnp.einsum("jsga,jsgb->jsab", far_imag, image_real, preferred_element_type=jnp.float32)
    partial_lower = jnp.stack([lower_real, lower_imag], 2)
    inverse = 1.0 / math.sqrt(g_total)
    mirror = lax.psum_scatter(partial_lower, "ga", scatter_dimension=3, tiled=True) * inverse
    partial_upper = jnp.stack([jnp.swapaxes(lower_real, 2, 3), -jnp.swapaxes(lower_imag, 2, 3)], 2)
    kernel = lax.psum_scatter(partial_upper, "ga", scatter_dimension=3, tiled=True) * inverse
    return (kernel, mirror)


def solution(mesh):
    placed = (P("kp", None, "ga", None), P("kp", None, "ga", None), P("ga"), P("kp", None))
    n_kp, n_ga = mesh.shape["kp"], mesh.shape["ga"]

    def shards(densities, screened, coulomb, block_rows):
        g_local, t = densities.shape[2], densities.shape[3]
        fits = n_kp == 2 * 2 and n_ga == 4 * 2
        fits = fits and g_local % 128 == 0 and t % (8 * n_ga) == 0
        fits = fits and n_kp * densities.shape[0] <= 256
        if fits:
            return quick(n_kp, n_ga, densities, screened, coulomb, block_rows)
        return plain(densities, screened, coulomb, block_rows)

    return jax.shard_map(
        shards,
        mesh=mesh,
        in_specs=placed,
        out_specs=(P("kp", None, None, "ga", None), P("kp", None, None, "ga", None)),
        check_vma=False,
    )
```

```python
import functools
import itertools
import math

import jax
import jax.numpy as jnp
from jax import lax
from jax.experimental import pallas as pl
from jax.experimental.pallas import tpu as pltpu
from jax.sharding import PartitionSpec as P

F32 = jnp.float32
BF16 = jnp.bfloat16
LABELS = 16
VMEM = pl.BlockSpec(memory_space=pltpu.VMEM)
SMEM = pl.BlockSpec(memory_space=pltpu.SMEM)
HBM = pl.BlockSpec(memory_space=pltpu.HBM)


def dot(a, b):
    return jnp.dot(a, b, preferred_element_type=F32)


def tdot(a, b):
    return lax.dot_general(a, b, (((0,), (0,)), ((), ())), preferred_element_type=F32)


def run(body, out, *args, specs=None, scratch=(), name=None, aliases=None, mib=16):
    outs = out if isinstance(out, (list, tuple)) else [out]
    result = pl.pallas_call(
        body,
        in_specs=specs or [VMEM] * len(args),
        out_specs=[VMEM] * len(outs),
        out_shape=list(outs),
        scratch_shapes=list(scratch),
        input_output_aliases=aliases or {},
        compiler_params=pltpu.CompilerParams(vmem_limit_bytes=mib * 2**20),
        cost_estimate=pl.CostEstimate(flops=0, bytes_accessed=0, transcendentals=0),
        name=name,
    )(*args)
    return list(result) if isinstance(out, (list, tuple)) else result[0]


BITS = ((1, 2), (2, 1))


def pack_kernel(rows, densities, *sends):
    held, _, g_local, t = densities.shape
    half = g_local // 2
    for h in range(2):
        for k in range(held):
            for part in range(2):
                at = (2 * k + part) * half
                sends[h][at : at + half] = densities[k, part, h * half : (h + 1) * half]
        line = lax.broadcasted_iota(jnp.int32, (LABELS, t), 0)
        tile = jnp.zeros((LABELS, t), F32)
        for j in range(rows.shape[1]):
            tile = jnp.where(line == j, rows[0, j].astype(F32), tile)
        sends[h][2 * held * half :] = tile.astype(BF16)


def label_of(message, held, half, j):
    tail = message[2 * held * half :].astype(F32)
    return jnp.max(tail[j : j + 1]).astype(jnp.int32)


def entries(message, owner, held, half):
    return [(owner * held + k, message, 2 * k * half, (2 * k + 1) * half) for k in range(held)]


def copy_if(label, found, out):
    half = out.shape[1]
    hit = None
    for name, message, real, imag in found:
        match = label == name
        hit = match if hit is None else hit | match

        @pl.when(match)
        def _(message=message, real=real, imag=imag):
            out[0] = message[real : real + half]
            out[1] = message[imag : imag + half]

    return hit


def pick_kernel(held, packed_0, packed_1, came_0, came_1, *sends):
    owner = lax.axis_index("kp")
    packed, came = (packed_0, packed_1), (came_0, came_1)
    half = sends[0].shape[2]
    for j in range(sends[0].shape[0]):
        for h in range(2):
            found = entries(packed[h], owner, held, half)
            found += entries(came[h], owner ^ BITS[h][0], held, half)
            copy_if(label_of(came[1 - h], held, half, j), found, sends[h].at[j])


def near_kernel(held, packed_0, packed_1, came_0, came_1, picked_0, picked_1, near, *each):
    owner = lax.axis_index("kp")
    packed, came, picked = (packed_0, packed_1), (came_0, came_1), (picked_0, picked_1)
    half = picked_0.shape[2]
    for j in range(near.shape[0]):
        label = label_of(packed_0, held, half, j)
        for h in range(2):
            out = near.at[j, :, h * half : (h + 1) * half]
            found = entries(packed[h], owner, held, half)
            found += entries(came[h], owner ^ BITS[h][0], held, half)
            hit = copy_if(label, found, out)

            @pl.when(jnp.logical_not(hit))
            def _(h=h, j=j, out=out):
                out[...] = picked[h][j]

    for j, out in enumerate(each):
        out[...] = near[j]


def stack_kernel(*refs):
    for i, ref in enumerate(refs[:-1]):
        refs[-1][i] = ref[...]


def left_over(n_kp, held, transfers, count):
    most = []
    for first, second in BITS:
        worst = 0
        for owner in range(n_kp):
            side = {who * held + k for who in (owner ^ second, owner ^ second ^ first) for k in range(held)}
            rows = range(n_kp * held - transfers * (owner + 1) + 1)
            for chosen in itertools.product(rows, repeat=count):
                need = {r + owner * transfers + s for r in chosen for s in range(transfers)}
                worst = max(worst, len((need & side) - set(chosen)))
        most.append(max(worst, 1))
    return most


def slots(labels, rows, owner, transfers):
    found, place = [], jnp.int32(0)
    for label in labels:
        need, sent = jnp.bool_(False), jnp.bool_(False)
        for row in rows:
            first = row + owner * transfers
            need = need | ((label >= first) & (label < first + transfers))
            sent = sent | (label == row)
        need = need & jnp.logical_not(sent)
        found.append((need, place))
        place = place + need.astype(jnp.int32)
    return found


def rest_kernel(held, transfers, count, packed_0, packed_1, came_0, came_1, *sends):
    owner = lax.axis_index("kp")
    packed, came = (packed_0, packed_1), (came_0, came_1)
    for h in range(2):
        first, second = BITS[h]
        room, _, half, _ = sends[h].shape
        found = entries(packed[h], owner, held, half)
        found += entries(came[h], owner ^ first, held, half)
        rows = [label_of(came[1 - h], held, half, j) for j in range(count)]
        places = slots([label for label, *_ in found], rows, owner ^ second, transfers)
        for (_, message, real, imag), (need, place) in zip(found, places):
            for i in range(room):

                @pl.when(need & (place == i))
                def _(h=h, i=i, message=message, real=real, imag=imag, half=half):
                    sends[h][i, 0] = message[real : real + half]
                    sends[h][i, 1] = message[imag : imag + half]


def far_kernel(
    held, packed_0, packed_1, came_0, came_1, picked_0, picked_1, rest_0, rest_1, far
):
    owner = lax.axis_index("kp")
    packed, came = (packed_0, packed_1), (came_0, came_1)
    picked, rest = (picked_0, picked_1), (rest_0, rest_1)
    count, transfers, _, g_local, _ = far.shape
    half = g_local // 2
    rows = [label_of(packed_0, held, half, j) for j in range(count)]
    for h in range(2):
        first, second = BITS[h]
        found = entries(packed[h], owner, held, half)
        found += entries(came[h], owner ^ first, held, half)
        side = [
            who * held + k for who in (owner ^ second, owner ^ second ^ first) for k in range(held)
        ]
        places = slots(side, rows, owner, transfers)
        for j in range(count):
            for s in range(transfers):
                label = rows[j] + owner * transfers + s
                out = far.at[j, s, :, h * half : (h + 1) * half]
                hit = copy_if(label, found, out)
                for i in range(count):
                    match = (label == rows[i]) & jnp.logical_not(hit)
                    hit = hit | match

                    @pl.when(match)
                    def _(h=h, i=i, out=out):
                        out[...] = picked[h][i]

                for name, (need, place) in zip(side, places):
                    for i in range(rest[h].shape[0]):

                        @pl.when((label == name) & need & (place == i))
                        def _(h=h, i=i, out=out):
                            out[...] = rest[h][i]


def load_kernel(source, panels, sems):
    copies = []
    for s in range(source.shape[0]):
        for part in range(2):
            copy = pltpu.make_async_copy(source.at[s, part], panels.at[s, part], sems.at[2 * s + part])
            copy.start()
            copies.append(copy)
    for copy in copies:
        copy.wait()


FORTH = (1, 3, 0, 2)
BACK = (2, 0, 3, 1)


def chip_at(z, steps):
    if steps == 1:
        return jnp.where(z < 2, 2 * z + 1, 2 * z - 4)
    if steps == -1:
        return jnp.where(lax.rem(z, 2) == 0, 2 + z // 2, z // 2)
    return z if steps == 0 else 3 - z


def lay(terms, upper, lower):
    for ref, first in terms:
        *count, _, g_local, t = ref.shape
        rows = pl.ds(first if isinstance(first, int) else pl.multiple_of(first, 128), g_local)
        for j, panel in enumerate([ref.at[j] for j in range(count[0])] if count else [ref]):
            real, imag = slice(2 * j * t, (2 * j + 1) * t), slice((2 * j + 1) * t, (2 * j + 2) * t)
            upper[rows, real] = panel[0]
            upper[rows, imag] = panel[1]
            lower[rows, real] = -panel[1]
            lower[rows, imag] = panel[0]


def place():
    slot = lax.axis_index("ga")
    return slot // 2, lax.rem(slot, 2)


def multiply(screened, s, span, width, upper, lower, first=0):
    span = pl.ds(pl.multiple_of(span, 128), width)
    rows = slice(first, first + width)
    return dot(screened[s, 0, :, span], upper[rows]) + dot(screened[s, 1, :, span], lower[rows])


def first_kernel(screened, own, coulomb, total, upper, lower):
    z, core = place()
    g = screened.shape[2]
    lay([(own, 0)], upper, lower)
    span = pl.ds(pl.multiple_of((2 * z + core) * g, 128), g)
    line = lax.broadcasted_iota(jnp.int32, (g, g), 0)
    on = line == lax.broadcasted_iota(jnp.int32, (g, g), 1)
    for s in range(screened.shape[0]):
        real = screened[s, 0, :, span]
        real = jnp.where(on, (real.astype(F32) - 2.0 * coulomb[...]).astype(BF16), real)
        total[s] = dot(real, upper[...]) + dot(screened[s, 1, :, span], lower[...])


def step_kernel(steps, screened, own, pair, before, total, upper, lower):
    z, core = place()
    g = screened.shape[2]
    lay([(own, core * g), (pair, (1 - core) * g)], upper, lower)
    span = 2 * chip_at(z, steps) * g
    for s in range(screened.shape[0]):
        total[s] = before[s] + multiply(screened, s, span, 2 * g, upper, lower)


def second_kernel(steps, screened, own, pairs, before, total, upper, lower):
    z, core = place()
    g = screened.shape[2]
    lay([(own, core * g), (pairs.at[1], (1 - core) * g), (pairs.at[0], 2 * g)], upper, lower)
    span = 2 * chip_at(z, steps) * g
    left = (2 * z + 1 - core) * g
    for s in range(screened.shape[0]):
        value = before[s] + multiply(screened, s, span, 2 * g, upper, lower)
        total[s] = value + multiply(screened, s, left, g, upper, lower, 2 * g)


def last_kernel(chips, steps, j, screened, own, pair_real, pair_imag, before, far, keep, *refs):
    z, core = place()
    g = screened.shape[2]
    t = far.shape[-1]
    *gives, upper, lower = refs
    lay([(own, core * g)], upper, lower)
    rows = pl.ds(pl.multiple_of((1 - core) * g, 128), g)
    upper[rows, :t] = pair_real[...]
    upper[rows, t:] = pair_imag[...]
    lower[rows, :t] = -pair_imag[...]
    lower[rows, t:] = pair_real[...]
    span = 2 * chip_at(z, steps) * g
    first = core == 0
    for s in range(screened.shape[0]):
        value = before[s, :, 2 * j * t : 2 * (j + 1) * t]
        image = (value + multiply(screened, s, span, 2 * g, upper, lower)).astype(BF16)
        by_real, by_imag = tdot(far[j, s, 0], image), tdot(far[j, s, 1], image)
        real = by_real[:, :t] + by_imag[:, t:]
        imag = by_real[:, t:] - by_imag[:, :t]
        parts = ((real, imag), (real.T, -imag.T))
        for which in range(2):
            for part in range(2):
                block = parts[which][part]
                block = block.reshape(chips, 2, t // (2 * chips), t)
                keep[:, s, which, part] = jnp.where(first, block[:, 0], block[:, 1])
                give = jnp.where(first, block[:, 1], block[:, 0])
                gives[2 * s + which][:, part] = give.astype(BF16)


def split_kernel(keep, *refs):
    *came, own, cross, sends = refs
    z = lax.axis_index("ga") // 2
    for s in range(keep.shape[1]):
        for which in range(2):

            def chip(at):
                return keep[at, s, which] + came[2 * s + which][at].astype(F32)

            own[s, which] = chip(z)
            cross[s, which] = chip(z ^ 2)
            for i, at in enumerate((z ^ 1, z ^ 3)):
                sends[i, s, which] = chip(at).astype(BF16)


def merge_kernel(own, cross, came, total, sends):
    total[...] = own[...] + came[0].astype(F32)
    sends[...] = (cross[...] + came[1].astype(F32)).astype(BF16)


def finish_kernel(count, chips, scale, *refs):
    kernel, mirror = refs[-2:]
    for j in range(count):
        terms = refs[j * chips : (j + 1) * chips]
        total = terms[0][...]
        for term in terms[1:]:
            total = total + term[...].astype(F32)
        mirror[j] = total[:, 0] * scale
        kernel[j] = total[:, 1] * scale


def quick(n_kp, n_ga, densities, screened, coulomb, block_rows):
    held, _, g_local, t = densities.shape
    transfers, g_total = screened.shape[0], screened.shape[3]
    count = block_rows.shape[1]
    chips = n_ga // 2
    half = g_local // 2
    shape = jax.ShapeDtypeStruct
    tie = lax.optimization_barrier

    def across(x, bit):
        return lax.ppermute(x, "kp", [(i, i ^ bit) for i in range(n_kp)])

    def other_core(x):
        return lax.ppermute(x, "ga", [(i, i ^ 1) for i in range(n_ga)])

    def along(x, chips_on):
        return lax.ppermute(x, "ga", [(i, 2 * chips_on[i // 2] + i % 2) for i in range(n_ga)])

    message = shape((2 * held * half + LABELS, t), BF16)

    def pack(panels):
        return run(pack_kernel, [message] * 2, block_rows, panels, specs=[SMEM, VMEM], name="pack")

    sums = shape((transfers, g_local, 2 * count * t), F32)

    def product(body, terms, *args):
        return run(
            body,
            sums,
            screened,
            *args,
            scratch=[pltpu.VMEM((terms * g_local, 2 * count * t), BF16)] * 2,
            aliases={} if terms == 1 else {3: 0},
            name="product",
            mib=24,
        )

    def pick(packed, came):
        sends = run(
            functools.partial(pick_kernel, held),
            [shape((count, 2, half, t), BF16)] * 2,
            *packed,
            *came,
            name="pick",
        )
        return [across(sends[h], BITS[h][1]) for h in range(2)]

    slices = shape((count, 2, g_local, t), BF16)

    def near_of(packed, came, picked, apart=False):
        kernel = functools.partial(near_kernel, held)
        outs = [slices] + [shape(slices.shape[1:], BF16)] * (count if apart else 0)
        near, *each = run(kernel, outs, *packed, *came, *picked, name="near")
        return (near, each) if apart else near

    before = along(densities, FORTH)
    packed = pack(densities)
    came = [across(packed[h], BITS[h][0]) for h in range(2)]
    source, packed = tie((screened, packed))
    screened = run(
        load_kernel,
        shape(screened.shape, screened.dtype),
        source,
        specs=[HBM],
        scratch=[pltpu.SemaphoreType.DMA((2 * transfers,))],
        name="load",
        mib=40,
    )
    came, screened = tie((came, screened))
    picked = pick(packed, came)
    packed_before = pack(before)
    rest_sends = run(
        functools.partial(rest_kernel, held, transfers, count),
        [shape((room, 2, half, t), BF16) for room in left_over(n_kp, held, transfers, count)],
        *packed,
        *came,
        name="rest",
    )
    picked = list(tie((picked, (packed_before, rest_sends)))[0])
    near = near_of(packed, came, picked)
    ahead = along(near, BACK)
    total = product(first_kernel, 1, near, coulomb[None, :])

    came_before = [across(packed_before[h], BITS[h][0]) for h in range(2)]
    came_before, total = tie((came_before, total))
    picked_before = pick(packed_before, came_before)
    near_before, before_each = near_of(packed_before, came_before, picked_before, True)
    behind = [along(x, FORTH) for x in before_each]

    rest_sends, ahead, _ = tie((rest_sends, ahead, near_before))
    rest = [across(rest_sends[h], BITS[h][1]) for h in range(2)]

    stack, _ = tie(((near, near_before), ahead))
    both = run(stack_kernel, shape((2, *slices.shape), BF16), *stack, name="stack")
    total = product(
        functools.partial(step_kernel, 1), 2, ahead, other_core(ahead), total
    )
    total = product(
        functools.partial(second_kernel, -1), 3, near_before, other_core(both), total
    )
    behind[0], _ = tie((behind[0], total))
    rest, total = tie((rest, total))
    far = run(
        functools.partial(far_kernel, held),
        shape((count, transfers, 2, g_local, t), BF16),
        *packed,
        *came,
        *picked,
        *rest,
        name="far",
    )

    parts = shape((chips, transfers, 2, 2, t // n_ga, t), F32)
    part = parts.shape[1:]
    stages = []
    done = total
    for j in range(count):
        total, _ = tie((total, done))
        keep, *gives = run(
            functools.partial(last_kernel, chips, -2, j),
            [parts] + [shape((chips, 2, t // n_ga, t), BF16)] * (2 * transfers),
            screened,
            behind[j],
            *[other_core(behind[j][part]) for part in range(2)],
            total,
            far,
            scratch=[pltpu.VMEM((2 * g_local, 2 * t), BF16)] * 2,
            name="last",
            mib=24,
        )
        own, cross, sends = run(
            split_kernel,
            [shape(part, F32), shape(part, F32), shape((2, *part), BF16)],
            keep,
            *[other_core(x) for x in gives],
            name="split",
        )
        if j + 1 < count:
            behind[j + 1], _ = tie((behind[j + 1], keep))
        if stages:
            sends, _ = tie((sends, stages[-1][2]))
        done = own
        came_j = lax.ppermute(sends, "ga", [(i, i ^ 2) for i in range(n_ga)])
        stages.append((own, cross, came_j))
    groups = []
    for own, cross, came_j in stages:
        own, sends = run(
            merge_kernel, [shape(part, F32), shape(part, BF16)], own, cross, came_j, name="merge"
        )
        groups += [own, lax.ppermute(sends, "ga", [(i, i ^ 4) for i in range(n_ga)])]
    result = shape((count, transfers, 2, t // n_ga, t), F32)
    return tuple(
        run(
            functools.partial(finish_kernel, count, 2, -1.0 / math.sqrt(g_total)),
            [result] * 2,
            *groups,
            name="finish",
        )
    )


def plain(densities, screened, coulomb, block_rows):
    owner = lax.axis_index("kp")
    g_slot = lax.axis_index("ga")
    k_held = densities.shape[0]
    g_local = densities.shape[2]
    g_total = screened.shape[3]
    rows = block_rows[0]
    transfers = owner * k_held + jnp.arange(k_held, dtype=jnp.int32)
    far_rows = rows[:, None] + transfers[None, :]
    piece = lax.all_gather(densities, "kp", axis=0, tiled=True)
    labels = jnp.arange(piece.shape[0], dtype=jnp.int32)
    pick_near = (rows[:, None] == labels[None, :]).astype(jnp.bfloat16)
    pick_far = (far_rows[:, :, None] == labels[None, None, :]).astype(jnp.bfloat16)
    near_acc = jnp.einsum(
        "jp,pcgt->jcgt", pick_near, piece, preferred_element_type=jnp.float32
    ).astype(jnp.bfloat16)
    far_acc = jnp.einsum(
        "jsp,pcgt->jscgt", pick_far, piece, preferred_element_type=jnp.float32
    ).astype(jnp.bfloat16)
    columns = jnp.arange(g_total, dtype=jnp.int32)
    own_rows = g_slot * g_local + jnp.arange(g_local, dtype=jnp.int32)
    diag_mask = own_rows[:, None] == columns[None, :]
    coulomb_diag = jnp.where(diag_mask, 2.0 * coulomb[:, None], 0.0)
    screen_real = (coulomb_diag[None] - screened[:, 0].astype(jnp.float32)).astype(jnp.bfloat16)
    screen_imag = -screened[:, 1]
    near_all = lax.all_gather(near_acc, "ga", axis=2, tiled=True)
    piece_real = near_all[:, 0]
    piece_imag = near_all[:, 1]
    real_term = jnp.einsum(
        "sgh,jht->jsgt", screen_real, piece_real, preferred_element_type=jnp.float32
    ) - jnp.einsum("sgh,jht->jsgt", screen_imag, piece_imag, preferred_element_type=jnp.float32)
    imag_term = jnp.einsum(
        "sgh,jht->jsgt", screen_real, piece_imag, preferred_element_type=jnp.float32
    ) + jnp.einsum("sgh,jht->jsgt", screen_imag, piece_real, preferred_element_type=jnp.float32)
    image = jnp.stack([real_term, imag_term], 2)
    image = image.astype(jnp.bfloat16)
    image_real = image[:, :, 0]
    image_imag = image[:, :, 1]
    far_real = far_acc[:, :, 0]
    far_imag = far_acc[:, :, 1]
    lower_real = jnp.einsum(
        "jsga,jsgb->jsab", far_real, image_real, preferred_element_type=jnp.float32
    ) + jnp.einsum("jsga,jsgb->jsab", far_imag, image_imag, preferred_element_type=jnp.float32)
    lower_imag = jnp.einsum(
        "jsga,jsgb->jsab", far_real, image_imag, preferred_element_type=jnp.float32
    ) - jnp.einsum("jsga,jsgb->jsab", far_imag, image_real, preferred_element_type=jnp.float32)
    partial_lower = jnp.stack([lower_real, lower_imag], 2)
    inverse = 1.0 / math.sqrt(g_total)
    mirror = lax.psum_scatter(partial_lower, "ga", scatter_dimension=3, tiled=True) * inverse
    partial_upper = jnp.stack([jnp.swapaxes(lower_real, 2, 3), -jnp.swapaxes(lower_imag, 2, 3)], 2)
    kernel = lax.psum_scatter(partial_upper, "ga", scatter_dimension=3, tiled=True) * inverse
    return (kernel, mirror)


def solution(mesh):
    placed = (P("kp", None, "ga", None), P("kp", None, "ga", None), P("ga"), P("kp", None))
    n_kp, n_ga = mesh.shape["kp"], mesh.shape["ga"]

    def shards(densities, screened, coulomb, block_rows):
        g_local, t = densities.shape[2], densities.shape[3]
        fits = n_kp == 2 * 2 and n_ga == 4 * 2
        fits = fits and g_local % 128 == 0 and t % (8 * n_ga) == 0
        fits = fits and n_kp * densities.shape[0] <= 256
        if fits:
            return quick(n_kp, n_ga, densities, screened, coulomb, block_rows)
        return plain(densities, screened, coulomb, block_rows)

    return jax.shard_map(
        shards,
        mesh=mesh,
        in_specs=placed,
        out_specs=(P("kp", None, None, "ga", None), P("kp", None, None, "ga", None)),
        check_vma=False,
    )
```

```python
import functools
import itertools
import math

import jax
import jax.numpy as jnp
from jax import lax
from jax.experimental import pallas as pl
from jax.experimental.pallas import tpu as pltpu
from jax.sharding import PartitionSpec as P

F32 = jnp.float32
BF16 = jnp.bfloat16
LABELS = 16
VMEM = pl.BlockSpec(memory_space=pltpu.VMEM)
SMEM = pl.BlockSpec(memory_space=pltpu.SMEM)
HBM = pl.BlockSpec(memory_space=pltpu.HBM)


def dot(a, b):
    return jnp.dot(a, b, preferred_element_type=F32)


def tdot(a, b):
    return lax.dot_general(a, b, (((0,), (0,)), ((), ())), preferred_element_type=F32)


def run(body, out, *args, specs=None, scratch=(), name=None, aliases=None, mib=16):
    outs = out if isinstance(out, (list, tuple)) else [out]
    result = pl.pallas_call(
        body,
        in_specs=specs or [VMEM] * len(args),
        out_specs=[VMEM] * len(outs),
        out_shape=list(outs),
        scratch_shapes=list(scratch),
        input_output_aliases=aliases or {},
        compiler_params=pltpu.CompilerParams(vmem_limit_bytes=mib * 2**20),
        cost_estimate=pl.CostEstimate(flops=0, bytes_accessed=0, transcendentals=0),
        name=name,
    )(*args)
    return list(result) if isinstance(out, (list, tuple)) else result[0]


BITS = ((1, 2), (2, 1))


def pack_kernel(rows, densities, *sends):
    held, _, g_local, t = densities.shape
    half = g_local // 2
    for h in range(2):
        for k in range(held):
            for part in range(2):
                at = (2 * k + part) * half
                sends[h][at : at + half] = densities[k, part, h * half : (h + 1) * half]
        line = lax.broadcasted_iota(jnp.int32, (LABELS, t), 0)
        tile = jnp.zeros((LABELS, t), F32)
        for j in range(rows.shape[1]):
            tile = jnp.where(line == j, rows[0, j].astype(F32), tile)
        sends[h][2 * held * half :] = tile.astype(BF16)


def label_of(message, held, half, j):
    tail = message[2 * held * half :].astype(F32)
    return jnp.max(tail[j : j + 1]).astype(jnp.int32)


def entries(message, owner, held, half):
    return [(owner * held + k, message, 2 * k * half, (2 * k + 1) * half) for k in range(held)]


def copy_if(label, found, out):
    half = out.shape[1]
    hit = None
    for name, message, real, imag in found:
        match = label == name
        hit = match if hit is None else hit | match

        @pl.when(match)
        def _(message=message, real=real, imag=imag):
            out[0] = message[real : real + half]
            out[1] = message[imag : imag + half]

    return hit


def pick_kernel(held, packed_0, packed_1, came_0, came_1, *sends):
    owner = lax.axis_index("kp")
    packed, came = (packed_0, packed_1), (came_0, came_1)
    half = sends[0].shape[2]
    for j in range(sends[0].shape[0]):
        for h in range(2):
            found = entries(packed[h], owner, held, half)
            found += entries(came[h], owner ^ BITS[h][0], held, half)
            copy_if(label_of(came[1 - h], held, half, j), found, sends[h].at[j])


def near_kernel(held, packed_0, packed_1, came_0, came_1, picked_0, picked_1, near, *each):
    owner = lax.axis_index("kp")
    packed, came, picked = (packed_0, packed_1), (came_0, came_1), (picked_0, picked_1)
    half = picked_0.shape[2]
    for j in range(near.shape[0]):
        label = label_of(packed_0, held, half, j)
        for h in range(2):
            out = near.at[j, :, h * half : (h + 1) * half]
            found = entries(packed[h], owner, held, half)
            found += entries(came[h], owner ^ BITS[h][0], held, half)
            hit = copy_if(label, found, out)

            @pl.when(jnp.logical_not(hit))
            def _(h=h, j=j, out=out):
                out[...] = picked[h][j]

    for j, out in enumerate(each):
        out[...] = near[j]


def stack_kernel(*refs):
    for i, ref in enumerate(refs[:-1]):
        refs[-1][i] = ref[...]


def left_over(n_kp, held, transfers, count):
    most = []
    for first, second in BITS:
        worst = 0
        for owner in range(n_kp):
            side = {who * held + k for who in (owner ^ second, owner ^ second ^ first) for k in range(held)}
            rows = range(n_kp * held - transfers * (owner + 1) + 1)
            for chosen in itertools.product(rows, repeat=count):
                need = {r + owner * transfers + s for r in chosen for s in range(transfers)}
                worst = max(worst, len((need & side) - set(chosen)))
        most.append(max(worst, 1))
    return most


def slots(labels, rows, owner, transfers):
    found, place = [], jnp.int32(0)
    for label in labels:
        need, sent = jnp.bool_(False), jnp.bool_(False)
        for row in rows:
            first = row + owner * transfers
            need = need | ((label >= first) & (label < first + transfers))
            sent = sent | (label == row)
        need = need & jnp.logical_not(sent)
        found.append((need, place))
        place = place + need.astype(jnp.int32)
    return found


def rest_kernel(held, transfers, count, packed_0, packed_1, came_0, came_1, *sends):
    owner = lax.axis_index("kp")
    packed, came = (packed_0, packed_1), (came_0, came_1)
    for h in range(2):
        first, second = BITS[h]
        room, _, half, _ = sends[h].shape
        found = entries(packed[h], owner, held, half)
        found += entries(came[h], owner ^ first, held, half)
        rows = [label_of(came[1 - h], held, half, j) for j in range(count)]
        places = slots([label for label, *_ in found], rows, owner ^ second, transfers)
        for (_, message, real, imag), (need, place) in zip(found, places):
            for i in range(room):

                @pl.when(need & (place == i))
                def _(h=h, i=i, message=message, real=real, imag=imag, half=half):
                    sends[h][i, 0] = message[real : real + half]
                    sends[h][i, 1] = message[imag : imag + half]


def far_kernel(
    held, j, count, packed_0, packed_1, came_0, came_1, picked_0, picked_1, rest_0, rest_1, far
):
    owner = lax.axis_index("kp")
    packed, came = (packed_0, packed_1), (came_0, came_1)
    picked, rest = (picked_0, picked_1), (rest_0, rest_1)
    transfers, _, g_local, _ = far.shape
    half = g_local // 2
    rows = [label_of(packed_0, held, half, j) for j in range(count)]
    for h in range(2):
        first, second = BITS[h]
        found = entries(packed[h], owner, held, half)
        found += entries(came[h], owner ^ first, held, half)
        side = [
            who * held + k for who in (owner ^ second, owner ^ second ^ first) for k in range(held)
        ]
        places = slots(side, rows, owner, transfers)
        for s in range(transfers):
            label = rows[j] + owner * transfers + s
            out = far.at[s, :, h * half : (h + 1) * half]
            hit = copy_if(label, found, out)
            for i in range(count):
                match = (label == rows[i]) & jnp.logical_not(hit)
                hit = hit | match

                @pl.when(match)
                def _(h=h, i=i, out=out):
                    out[...] = picked[h][i]

            for name, (need, place) in zip(side, places):
                for i in range(rest[h].shape[0]):

                    @pl.when((label == name) & need & (place == i))
                    def _(h=h, i=i, out=out):
                        out[...] = rest[h][i]


def load_kernel(source, panels, sems):
    copies = []
    for s in range(source.shape[0]):
        for part in range(2):
            copy = pltpu.make_async_copy(source.at[s, part], panels.at[s, part], sems.at[2 * s + part])
            copy.start()
            copies.append(copy)
    for copy in copies:
        copy.wait()


FORTH = (1, 3, 0, 2)
BACK = (2, 0, 3, 1)


def chip_at(z, steps):
    if steps == 1:
        return jnp.where(z < 2, 2 * z + 1, 2 * z - 4)
    if steps == -1:
        return jnp.where(lax.rem(z, 2) == 0, 2 + z // 2, z // 2)
    return z if steps == 0 else 3 - z


def lay(terms, upper, lower):
    for ref, first in terms:
        *count, _, g_local, t = ref.shape
        rows = pl.ds(first if isinstance(first, int) else pl.multiple_of(first, 128), g_local)
        for j, panel in enumerate([ref.at[j] for j in range(count[0])] if count else [ref]):
            real, imag = slice(2 * j * t, (2 * j + 1) * t), slice((2 * j + 1) * t, (2 * j + 2) * t)
            upper[rows, real] = panel[0]
            upper[rows, imag] = panel[1]
            lower[rows, real] = -panel[1]
            lower[rows, imag] = panel[0]


def place():
    slot = lax.axis_index("ga")
    return slot // 2, lax.rem(slot, 2)


def multiply(screened, s, span, width, upper, lower, first=0):
    span = pl.ds(pl.multiple_of(span, 128), width)
    rows = slice(first, first + width)
    return dot(screened[s, 0, :, span], upper[rows]) + dot(screened[s, 1, :, span], lower[rows])


def first_kernel(screened, own, coulomb, total, upper, lower):
    z, core = place()
    g = screened.shape[2]
    lay([(own, 0)], upper, lower)
    span = pl.ds(pl.multiple_of((2 * z + core) * g, 128), g)
    line = lax.broadcasted_iota(jnp.int32, (g, g), 0)
    on = line == lax.broadcasted_iota(jnp.int32, (g, g), 1)
    for s in range(screened.shape[0]):
        real = screened[s, 0, :, span]
        real = jnp.where(on, (real.astype(F32) - 2.0 * coulomb[...]).astype(BF16), real)
        total[s] = dot(real, upper[...]) + dot(screened[s, 1, :, span], lower[...])


def step_kernel(steps, screened, own, pair, before, total, upper, lower):
    z, core = place()
    g = screened.shape[2]
    lay([(own, core * g), (pair, (1 - core) * g)], upper, lower)
    span = 2 * chip_at(z, steps) * g
    for s in range(screened.shape[0]):
        total[s] = before[s] + multiply(screened, s, span, 2 * g, upper, lower)


def second_kernel(steps, screened, own, pairs, before, total, upper, lower):
    z, core = place()
    g = screened.shape[2]
    lay([(own, core * g), (pairs.at[1], (1 - core) * g), (pairs.at[0], 2 * g)], upper, lower)
    span = 2 * chip_at(z, steps) * g
    left = (2 * z + 1 - core) * g
    for s in range(screened.shape[0]):
        value = before[s] + multiply(screened, s, span, 2 * g, upper, lower)
        total[s] = value + multiply(screened, s, left, g, upper, lower, 2 * g)


def image_kernel(steps, j, screened, own, pair_real, pair_imag, before, image, upper, lower):
    z, core = place()
    g = screened.shape[2]
    t = own.shape[2]
    lay([(own, core * g)], upper, lower)
    rows = pl.ds(pl.multiple_of((1 - core) * g, 128), g)
    upper[rows, :t] = pair_real[...]
    upper[rows, t:] = pair_imag[...]
    lower[rows, :t] = -pair_imag[...]
    lower[rows, t:] = pair_real[...]
    span = 2 * chip_at(z, steps) * g
    for s in range(screened.shape[0]):
        value = before[s, :, 2 * j * t : 2 * (j + 1) * t]
        image[s] = (value + multiply(screened, s, span, 2 * g, upper, lower)).astype(BF16)


def mirror_kernel(chips, image, far, keep, *gives):
    first = lax.rem(lax.axis_index("ga"), 2) == 0
    t = far.shape[-1]
    for s in range(image.shape[0]):
        by_real, by_imag = tdot(far[s, 0], image[s]), tdot(far[s, 1], image[s])
        real = by_real[:, :t] + by_imag[:, t:]
        imag = by_real[:, t:] - by_imag[:, :t]
        parts = ((real, imag), (real.T, -imag.T))
        for which in range(2):
            for part in range(2):
                block = parts[which][part]
                block = block.reshape(chips, 2, t // (2 * chips), t)
                keep[:, s, which, part] = jnp.where(first, block[:, 0], block[:, 1])
                give = jnp.where(first, block[:, 1], block[:, 0])
                gives[2 * s + which][:, part] = give.astype(BF16)


def split_kernel(keep, *refs):
    *came, own, cross, sends = refs
    z = lax.axis_index("ga") // 2
    for s in range(keep.shape[1]):
        for which in range(2):

            def chip(at):
                return keep[at, s, which] + came[2 * s + which][at].astype(F32)

            own[s, which] = chip(z)
            cross[s, which] = chip(z ^ 2)
            for i, at in enumerate((z ^ 1, z ^ 3)):
                sends[i, s, which] = chip(at).astype(BF16)


def merge_kernel(own, cross, came, total, sends):
    total[...] = own[...] + came[0].astype(F32)
    sends[...] = (cross[...] + came[1].astype(F32)).astype(BF16)


def finish_kernel(count, chips, scale, *refs):
    kernel, mirror = refs[-2:]
    for j in range(count):
        terms = refs[j * chips : (j + 1) * chips]
        total = terms[0][...]
        for term in terms[1:]:
            total = total + term[...].astype(F32)
        mirror[j] = total[:, 0] * scale
        kernel[j] = total[:, 1] * scale


def quick(n_kp, n_ga, densities, screened, coulomb, block_rows):
    held, _, g_local, t = densities.shape
    transfers, g_total = screened.shape[0], screened.shape[3]
    count = block_rows.shape[1]
    chips = n_ga // 2
    half = g_local // 2
    shape = jax.ShapeDtypeStruct
    tie = lax.optimization_barrier

    def across(x, bit):
        return lax.ppermute(x, "kp", [(i, i ^ bit) for i in range(n_kp)])

    def other_core(x):
        return lax.ppermute(x, "ga", [(i, i ^ 1) for i in range(n_ga)])

    def along(x, chips_on):
        return lax.ppermute(x, "ga", [(i, 2 * chips_on[i // 2] + i % 2) for i in range(n_ga)])

    message = shape((2 * held * half + LABELS, t), BF16)

    def pack(panels):
        return run(pack_kernel, [message] * 2, block_rows, panels, specs=[SMEM, VMEM], name="pack")

    sums = shape((transfers, g_local, 2 * count * t), F32)

    def product(body, terms, *args):
        return run(
            body,
            sums,
            screened,
            *args,
            scratch=[pltpu.VMEM((terms * g_local, 2 * count * t), BF16)] * 2,
            aliases={} if terms == 1 else {3: 0},
            name="product",
            mib=24,
        )

    def pick(packed, came):
        sends = run(
            functools.partial(pick_kernel, held),
            [shape((count, 2, half, t), BF16)] * 2,
            *packed,
            *came,
            name="pick",
        )
        return [across(sends[h], BITS[h][1]) for h in range(2)]

    slices = shape((count, 2, g_local, t), BF16)

    def near_of(packed, came, picked, apart=False):
        kernel = functools.partial(near_kernel, held)
        outs = [slices] + [shape(slices.shape[1:], BF16)] * (count if apart else 0)
        near, *each = run(kernel, outs, *packed, *came, *picked, name="near")
        return (near, each) if apart else near

    before = along(densities, FORTH)
    packed = pack(densities)
    came = [across(packed[h], BITS[h][0]) for h in range(2)]
    source, packed = tie((screened, packed))
    screened = run(
        load_kernel,
        shape(screened.shape, screened.dtype),
        source,
        specs=[HBM],
        scratch=[pltpu.SemaphoreType.DMA((2 * transfers,))],
        name="load",
        mib=40,
    )
    came, screened = tie((came, screened))
    picked = pick(packed, came)
    packed_before = pack(before)
    rest_sends = run(
        functools.partial(rest_kernel, held, transfers, count),
        [shape((room, 2, half, t), BF16) for room in left_over(n_kp, held, transfers, count)],
        *packed,
        *came,
        name="rest",
    )
    picked = list(tie((picked, (packed_before, rest_sends)))[0])
    near = near_of(packed, came, picked)
    ahead = along(near, BACK)
    total = product(first_kernel, 1, near, coulomb[None, :])

    came_before = [across(packed_before[h], BITS[h][0]) for h in range(2)]
    came_before, total = tie((came_before, total))
    picked_before = pick(packed_before, came_before)
    near_before, before_each = near_of(packed_before, came_before, picked_before, True)
    behind = [along(x, FORTH) for x in before_each]

    rest_sends, ahead, _ = tie((rest_sends, ahead, near_before))
    rest = [across(rest_sends[h], BITS[h][1]) for h in range(2)]

    stack, _ = tie(((near, near_before), ahead))
    both = run(stack_kernel, shape((2, *slices.shape), BF16), *stack, name="stack")
    total = product(
        functools.partial(step_kernel, 1), 2, ahead, other_core(ahead), total
    )
    total = product(
        functools.partial(second_kernel, -1), 3, near_before, other_core(both), total
    )
    behind[0], _ = tie((behind[0], total))
    parts = shape((chips, transfers, 2, 2, t // n_ga, t), F32)
    part = parts.shape[1:]
    stages = []
    done = total
    for j in range(count):
        total, _ = tie((total, done))
        image = run(
            functools.partial(image_kernel, -2, j),
            shape((transfers, g_local, 2 * t), BF16),
            screened,
            behind[j],
            *[other_core(behind[j][part]) for part in range(2)],
            total,
            scratch=[pltpu.VMEM((2 * g_local, 2 * t), BF16)] * 2,
            name="image",
            mib=24,
        )
        rest, _ = tie((rest, image if j == 0 else done))
        far = run(
            functools.partial(far_kernel, held, j, count),
            shape((transfers, 2, g_local, t), BF16),
            *packed,
            *came,
            *picked,
            *rest,
            name="far",
        )
        keep, *gives = run(
            functools.partial(mirror_kernel, chips),
            [parts] + [shape((chips, 2, t // n_ga, t), BF16)] * (2 * transfers),
            image,
            far,
            name="mirror",
            mib=24,
        )
        own, cross, sends = run(
            split_kernel,
            [shape(part, F32), shape(part, F32), shape((2, *part), BF16)],
            keep,
            *[other_core(x) for x in gives],
            name="split",
        )
        if j + 1 < count:
            behind[j + 1], _ = tie((behind[j + 1], keep))
        if stages:
            sends, _ = tie((sends, stages[-1][2]))
        done = own
        came_j = lax.ppermute(sends, "ga", [(i, i ^ 2) for i in range(n_ga)])
        stages.append((own, cross, came_j))
    groups = []
    for own, cross, came_j in stages:
        own, sends = run(
            merge_kernel, [shape(part, F32), shape(part, BF16)], own, cross, came_j, name="merge"
        )
        groups += [own, lax.ppermute(sends, "ga", [(i, i ^ 4) for i in range(n_ga)])]
    result = shape((count, transfers, 2, t // n_ga, t), F32)
    return tuple(
        run(
            functools.partial(finish_kernel, count, 2, -1.0 / math.sqrt(g_total)),
            [result] * 2,
            *groups,
            name="finish",
        )
    )


def plain(densities, screened, coulomb, block_rows):
    owner = lax.axis_index("kp")
    g_slot = lax.axis_index("ga")
    k_held = densities.shape[0]
    g_local = densities.shape[2]
    g_total = screened.shape[3]
    rows = block_rows[0]
    transfers = owner * k_held + jnp.arange(k_held, dtype=jnp.int32)
    far_rows = rows[:, None] + transfers[None, :]
    piece = lax.all_gather(densities, "kp", axis=0, tiled=True)
    labels = jnp.arange(piece.shape[0], dtype=jnp.int32)
    pick_near = (rows[:, None] == labels[None, :]).astype(jnp.bfloat16)
    pick_far = (far_rows[:, :, None] == labels[None, None, :]).astype(jnp.bfloat16)
    near_acc = jnp.einsum(
        "jp,pcgt->jcgt", pick_near, piece, preferred_element_type=jnp.float32
    ).astype(jnp.bfloat16)
    far_acc = jnp.einsum(
        "jsp,pcgt->jscgt", pick_far, piece, preferred_element_type=jnp.float32
    ).astype(jnp.bfloat16)
    columns = jnp.arange(g_total, dtype=jnp.int32)
    own_rows = g_slot * g_local + jnp.arange(g_local, dtype=jnp.int32)
    diag_mask = own_rows[:, None] == columns[None, :]
    coulomb_diag = jnp.where(diag_mask, 2.0 * coulomb[:, None], 0.0)
    screen_real = (coulomb_diag[None] - screened[:, 0].astype(jnp.float32)).astype(jnp.bfloat16)
    screen_imag = -screened[:, 1]
    near_all = lax.all_gather(near_acc, "ga", axis=2, tiled=True)
    piece_real = near_all[:, 0]
    piece_imag = near_all[:, 1]
    real_term = jnp.einsum(
        "sgh,jht->jsgt", screen_real, piece_real, preferred_element_type=jnp.float32
    ) - jnp.einsum("sgh,jht->jsgt", screen_imag, piece_imag, preferred_element_type=jnp.float32)
    imag_term = jnp.einsum(
        "sgh,jht->jsgt", screen_real, piece_imag, preferred_element_type=jnp.float32
    ) + jnp.einsum("sgh,jht->jsgt", screen_imag, piece_real, preferred_element_type=jnp.float32)
    image = jnp.stack([real_term, imag_term], 2)
    image = image.astype(jnp.bfloat16)
    image_real = image[:, :, 0]
    image_imag = image[:, :, 1]
    far_real = far_acc[:, :, 0]
    far_imag = far_acc[:, :, 1]
    lower_real = jnp.einsum(
        "jsga,jsgb->jsab", far_real, image_real, preferred_element_type=jnp.float32
    ) + jnp.einsum("jsga,jsgb->jsab", far_imag, image_imag, preferred_element_type=jnp.float32)
    lower_imag = jnp.einsum(
        "jsga,jsgb->jsab", far_real, image_imag, preferred_element_type=jnp.float32
    ) - jnp.einsum("jsga,jsgb->jsab", far_imag, image_real, preferred_element_type=jnp.float32)
    partial_lower = jnp.stack([lower_real, lower_imag], 2)
    inverse = 1.0 / math.sqrt(g_total)
    mirror = lax.psum_scatter(partial_lower, "ga", scatter_dimension=3, tiled=True) * inverse
    partial_upper = jnp.stack([jnp.swapaxes(lower_real, 2, 3), -jnp.swapaxes(lower_imag, 2, 3)], 2)
    kernel = lax.psum_scatter(partial_upper, "ga", scatter_dimension=3, tiled=True) * inverse
    return (kernel, mirror)


def solution(mesh):
    placed = (P("kp", None, "ga", None), P("kp", None, "ga", None), P("ga"), P("kp", None))
    n_kp, n_ga = mesh.shape["kp"], mesh.shape["ga"]

    def shards(densities, screened, coulomb, block_rows):
        g_local, t = densities.shape[2], densities.shape[3]
        fits = n_kp == 2 * 2 and n_ga == 4 * 2
        fits = fits and g_local % 128 == 0 and t % (8 * n_ga) == 0
        fits = fits and n_kp * densities.shape[0] <= 256
        if fits:
            return quick(n_kp, n_ga, densities, screened, coulomb, block_rows)
        return plain(densities, screened, coulomb, block_rows)

    return jax.shard_map(
        shards,
        mesh=mesh,
        in_specs=placed,
        out_specs=(P("kp", None, None, "ga", None), P("kp", None, None, "ga", None)),
        check_vma=False,
    )
```

```python
import functools
import itertools
import math

import jax
import jax.numpy as jnp
from jax import lax
from jax.experimental import pallas as pl
from jax.experimental.pallas import tpu as pltpu
from jax.sharding import PartitionSpec as P

F32 = jnp.float32
BF16 = jnp.bfloat16
LABELS = 16
VMEM = pl.BlockSpec(memory_space=pltpu.VMEM)
SMEM = pl.BlockSpec(memory_space=pltpu.SMEM)
HBM = pl.BlockSpec(memory_space=pltpu.HBM)


def dot(a, b):
    return jnp.dot(a, b, preferred_element_type=F32)


def tdot(a, b):
    return lax.dot_general(a, b, (((0,), (0,)), ((), ())), preferred_element_type=F32)


def run(body, out, *args, specs=None, scratch=(), name=None, aliases=None, mib=16):
    outs = out if isinstance(out, (list, tuple)) else [out]
    result = pl.pallas_call(
        body,
        in_specs=specs or [VMEM] * len(args),
        out_specs=[VMEM] * len(outs),
        out_shape=list(outs),
        scratch_shapes=list(scratch),
        input_output_aliases=aliases or {},
        compiler_params=pltpu.CompilerParams(vmem_limit_bytes=mib * 2**20),
        cost_estimate=pl.CostEstimate(flops=0, bytes_accessed=0, transcendentals=0),
        name=name,
    )(*args)
    return list(result) if isinstance(out, (list, tuple)) else result[0]


BITS = ((1, 2), (2, 1))


def pack_kernel(rows, densities, *sends):
    held, _, g_local, t = densities.shape
    half = g_local // 2
    for h in range(2):
        for k in range(held):
            for part in range(2):
                at = (2 * k + part) * half
                sends[h][at : at + half] = densities[k, part, h * half : (h + 1) * half]
        line = lax.broadcasted_iota(jnp.int32, (LABELS, t), 0)
        tile = jnp.zeros((LABELS, t), F32)
        for j in range(rows.shape[1]):
            tile = jnp.where(line == j, rows[0, j].astype(F32), tile)
        sends[h][2 * held * half :] = tile.astype(BF16)


def label_of(message, held, half, j):
    tail = message[2 * held * half :].astype(F32)
    return jnp.max(tail[j : j + 1]).astype(jnp.int32)


def entries(message, owner, held, half):
    return [(owner * held + k, message, 2 * k * half, (2 * k + 1) * half) for k in range(held)]


def copy_if(label, found, out):
    half = out.shape[1]
    hit = None
    for name, message, real, imag in found:
        match = label == name
        hit = match if hit is None else hit | match

        @pl.when(match)
        def _(message=message, real=real, imag=imag):
            out[0] = message[real : real + half]
            out[1] = message[imag : imag + half]

    return hit


def pick_kernel(held, packed_0, packed_1, came_0, came_1, *sends):
    owner = lax.axis_index("kp")
    packed, came = (packed_0, packed_1), (came_0, came_1)
    half = sends[0].shape[2]
    for j in range(sends[0].shape[0]):
        for h in range(2):
            found = entries(packed[h], owner, held, half)
            found += entries(came[h], owner ^ BITS[h][0], held, half)
            copy_if(label_of(came[1 - h], held, half, j), found, sends[h].at[j])


def near_kernel(held, packed_0, packed_1, came_0, came_1, picked_0, picked_1, near, *each):
    owner = lax.axis_index("kp")
    packed, came, picked = (packed_0, packed_1), (came_0, came_1), (picked_0, picked_1)
    half = picked_0.shape[2]
    for j in range(near.shape[0]):
        label = label_of(packed_0, held, half, j)
        for h in range(2):
            out = near.at[j, :, h * half : (h + 1) * half]
            found = entries(packed[h], owner, held, half)
            found += entries(came[h], owner ^ BITS[h][0], held, half)
            hit = copy_if(label, found, out)

            @pl.when(jnp.logical_not(hit))
            def _(h=h, j=j, out=out):
                out[...] = picked[h][j]

    for j, out in enumerate(each):
        out[...] = near[j]


def stack_kernel(*refs):
    for i, ref in enumerate(refs[:-1]):
        refs[-1][i] = ref[...]


def left_over(n_kp, held, transfers, count):
    most = []
    for first, second in BITS:
        worst = 0
        for owner in range(n_kp):
            side = {who * held + k for who in (owner ^ second, owner ^ second ^ first) for k in range(held)}
            rows = range(n_kp * held - transfers * (owner + 1) + 1)
            for chosen in itertools.product(rows, repeat=count):
                need = {r + owner * transfers + s for r in chosen for s in range(transfers)}
                worst = max(worst, len((need & side) - set(chosen)))
        most.append(max(worst, 1))
    return most


def slots(labels, rows, owner, transfers):
    found, place = [], jnp.int32(0)
    for label in labels:
        need, sent = jnp.bool_(False), jnp.bool_(False)
        for row in rows:
            first = row + owner * transfers
            need = need | ((label >= first) & (label < first + transfers))
            sent = sent | (label == row)
        need = need & jnp.logical_not(sent)
        found.append((need, place))
        place = place + need.astype(jnp.int32)
    return found


def rest_kernel(held, transfers, count, packed_0, packed_1, came_0, came_1, *sends):
    owner = lax.axis_index("kp")
    packed, came = (packed_0, packed_1), (came_0, came_1)
    for h in range(2):
        first, second = BITS[h]
        room, _, half, _ = sends[h].shape
        found = entries(packed[h], owner, held, half)
        found += entries(came[h], owner ^ first, held, half)
        rows = [label_of(came[1 - h], held, half, j) for j in range(count)]
        places = slots([label for label, *_ in found], rows, owner ^ second, transfers)
        for (_, message, real, imag), (need, place) in zip(found, places):
            for i in range(room):

                @pl.when(need & (place == i))
                def _(h=h, i=i, message=message, real=real, imag=imag, half=half):
                    sends[h][i, 0] = message[real : real + half]
                    sends[h][i, 1] = message[imag : imag + half]


def far_kernel(
    held, j, count, packed_0, packed_1, came_0, came_1, picked_0, picked_1, rest_0, rest_1, far
):
    owner = lax.axis_index("kp")
    packed, came = (packed_0, packed_1), (came_0, came_1)
    picked, rest = (picked_0, picked_1), (rest_0, rest_1)
    transfers, _, g_local, _ = far.shape
    half = g_local // 2
    rows = [label_of(packed_0, held, half, j) for j in range(count)]
    for h in range(2):
        first, second = BITS[h]
        found = entries(packed[h], owner, held, half)
        found += entries(came[h], owner ^ first, held, half)
        side = [
            who * held + k for who in (owner ^ second, owner ^ second ^ first) for k in range(held)
        ]
        places = slots(side, rows, owner, transfers)
        for s in range(transfers):
            label = rows[j] + owner * transfers + s
            out = far.at[s, :, h * half : (h + 1) * half]
            hit = copy_if(label, found, out)
            for i in range(count):
                match = (label == rows[i]) & jnp.logical_not(hit)
                hit = hit | match

                @pl.when(match)
                def _(h=h, i=i, out=out):
                    out[...] = picked[h][i]

            for name, (need, place) in zip(side, places):
                for i in range(rest[h].shape[0]):

                    @pl.when((label == name) & need & (place == i))
                    def _(h=h, i=i, out=out):
                        out[...] = rest[h][i]


def load_kernel(source, panels, sems):
    copies = []
    for s in range(source.shape[0]):
        for part in range(2):
            copy = pltpu.make_async_copy(source.at[s, part], panels.at[s, part], sems.at[2 * s + part])
            copy.start()
            copies.append(copy)
    for copy in copies:
        copy.wait()


FORTH = (1, 3, 0, 2)
BACK = (2, 0, 3, 1)


def chip_at(z, steps):
    if steps == 1:
        return jnp.where(z < 2, 2 * z + 1, 2 * z - 4)
    if steps == -1:
        return jnp.where(lax.rem(z, 2) == 0, 2 + z // 2, z // 2)
    return z if steps == 0 else 3 - z


def lay(terms, upper, lower):
    for ref, first in terms:
        *count, _, g_local, t = ref.shape
        rows = pl.ds(first if isinstance(first, int) else pl.multiple_of(first, 128), g_local)
        for j, panel in enumerate([ref.at[j] for j in range(count[0])] if count else [ref]):
            real, imag = slice(2 * j * t, (2 * j + 1) * t), slice((2 * j + 1) * t, (2 * j + 2) * t)
            upper[rows, real] = panel[0]
            upper[rows, imag] = panel[1]
            lower[rows, real] = -panel[1]
            lower[rows, imag] = panel[0]


def place():
    slot = lax.axis_index("ga")
    return slot // 2, lax.rem(slot, 2)


def multiply(screened, s, span, width, upper, lower, first=0):
    span = pl.ds(pl.multiple_of(span, 128), width)
    rows = slice(first, first + width)
    return dot(screened[s, 0, :, span], upper[rows]) + dot(screened[s, 1, :, span], lower[rows])


def first_kernel(screened, own, coulomb, total, upper, lower):
    z, core = place()
    g = screened.shape[2]
    lay([(own, 0)], upper, lower)
    span = pl.ds(pl.multiple_of((2 * z + core) * g, 128), g)
    line = lax.broadcasted_iota(jnp.int32, (g, g), 0)
    on = line == lax.broadcasted_iota(jnp.int32, (g, g), 1)
    for s in range(screened.shape[0]):
        real = screened[s, 0, :, span]
        real = jnp.where(on, (real.astype(F32) - 2.0 * coulomb[...]).astype(BF16), real)
        total[s] = dot(real, upper[...]) + dot(screened[s, 1, :, span], lower[...])


def step_kernel(steps, screened, own, pair, before, total, upper, lower):
    z, core = place()
    g = screened.shape[2]
    lay([(own, core * g), (pair, (1 - core) * g)], upper, lower)
    span = 2 * chip_at(z, steps) * g
    for s in range(screened.shape[0]):
        total[s] = before[s] + multiply(screened, s, span, 2 * g, upper, lower)


def second_kernel(steps, screened, own, pairs, before, total, upper, lower):
    z, core = place()
    g = screened.shape[2]
    lay([(own, core * g), (pairs.at[1], (1 - core) * g), (pairs.at[0], 2 * g)], upper, lower)
    span = 2 * chip_at(z, steps) * g
    left = (2 * z + 1 - core) * g
    for s in range(screened.shape[0]):
        value = before[s] + multiply(screened, s, span, 2 * g, upper, lower)
        total[s] = value + multiply(screened, s, left, g, upper, lower, 2 * g)


def image_kernel(steps, j, screened, own, pair_real, pair_imag, before, image, upper, lower):
    z, core = place()
    g = screened.shape[2]
    t = own.shape[2]
    lay([(own, core * g)], upper, lower)
    rows = pl.ds(pl.multiple_of((1 - core) * g, 128), g)
    upper[rows, :t] = pair_real[...]
    upper[rows, t:] = pair_imag[...]
    lower[rows, :t] = -pair_imag[...]
    lower[rows, t:] = pair_real[...]
    span = 2 * chip_at(z, steps) * g
    for s in range(screened.shape[0]):
        value = before[s, :, 2 * j * t : 2 * (j + 1) * t]
        image[s] = (value + multiply(screened, s, span, 2 * g, upper, lower)).astype(BF16)


def mirror_kernel(chips, image, far, keep, *gives):
    first = lax.rem(lax.axis_index("ga"), 2) == 0
    t = far.shape[-1]
    for s in range(image.shape[0]):
        by_real, by_imag = tdot(far[s, 0], image[s]), tdot(far[s, 1], image[s])
        real = by_real[:, :t] + by_imag[:, t:]
        imag = by_real[:, t:] - by_imag[:, :t]
        parts = ((real, imag), (real.T, -imag.T))
        for which in range(2):
            for part in range(2):
                block = parts[which][part]
                block = block.reshape(chips, 2, t // (2 * chips), t)
                keep[:, s, which, part] = jnp.where(first, block[:, 0], block[:, 1])
                give = jnp.where(first, block[:, 1], block[:, 0])
                gives[2 * s + which][:, part] = give.astype(BF16)


def split_kernel(keep, *refs):
    *came, own, cross, sends = refs
    z = lax.axis_index("ga") // 2
    for s in range(keep.shape[1]):
        for which in range(2):

            def chip(at):
                return keep[at, s, which] + came[2 * s + which][at].astype(F32)

            own[s, which] = chip(z)
            cross[s, which] = chip(z ^ 2)
            for i, at in enumerate((z ^ 1, z ^ 3)):
                sends[i, s, which] = chip(at).astype(BF16)


def merge_kernel(own, cross, came, total, sends):
    total[...] = own[...] + came[0].astype(F32)
    sends[...] = (cross[...] + came[1].astype(F32)).astype(BF16)


def finish_kernel(count, chips, scale, *refs):
    kernel, mirror = refs[-2:]
    for j in range(count):
        terms = refs[j * chips : (j + 1) * chips]
        total = terms[0][...]
        for term in terms[1:]:
            total = total + term[...].astype(F32)
        mirror[j] = total[:, 0] * scale
        kernel[j] = total[:, 1] * scale


def quick(n_kp, n_ga, densities, screened, coulomb, block_rows):
    held, _, g_local, t = densities.shape
    transfers, g_total = screened.shape[0], screened.shape[3]
    count = block_rows.shape[1]
    chips = n_ga // 2
    half = g_local // 2
    shape = jax.ShapeDtypeStruct
    tie = lax.optimization_barrier

    def across(x, bit):
        return lax.ppermute(x, "kp", [(i, i ^ bit) for i in range(n_kp)])

    def other_core(x):
        return lax.ppermute(x, "ga", [(i, i ^ 1) for i in range(n_ga)])

    def along(x, chips_on):
        return lax.ppermute(x, "ga", [(i, 2 * chips_on[i // 2] + i % 2) for i in range(n_ga)])

    message = shape((2 * held * half + LABELS, t), BF16)

    sums = shape((transfers, g_local, 2 * count * t), F32)

    def product(body, terms, *args):
        return run(
            body,
            sums,
            screened,
            *args,
            scratch=[pltpu.VMEM((terms * g_local, 2 * count * t), BF16)] * 2,
            aliases={} if terms == 1 else {3: 0},
            name="product",
            mib=24,
        )

    def pick(packed, came):
        sends = run(
            functools.partial(pick_kernel, held),
            [shape((count, 2, half, t), BF16)] * 2,
            *packed,
            *came,
            name="pick",
        )
        return [across(sends[h], BITS[h][1]) for h in range(2)]

    slices = shape((count, 2, g_local, t), BF16)

    def near_of(packed, came, picked, apart=False):
        kernel = functools.partial(near_kernel, held)
        outs = [slices] + [shape(slices.shape[1:], BF16)] * (count if apart else 0)
        near, *each = run(kernel, outs, *packed, *came, *picked, name="near")
        return (near, each) if apart else near

    packed = run(
        pack_kernel, [message] * 2, block_rows, densities, specs=[SMEM, VMEM], name="pack", mib=53
    )
    packed_before = [along(x, FORTH) for x in packed]
    came = [across(packed[h], BITS[h][0]) for h in range(2)]
    source, packed = tie((screened, packed))
    screened = run(
        load_kernel,
        shape(screened.shape, screened.dtype),
        source,
        specs=[HBM],
        scratch=[pltpu.SemaphoreType.DMA((2 * transfers,))],
        name="load",
        mib=40,
    )
    came, screened = tie((came, screened))
    picked = pick(packed, came)
    rest_sends = run(
        functools.partial(rest_kernel, held, transfers, count),
        [shape((room, 2, half, t), BF16) for room in left_over(n_kp, held, transfers, count)],
        *packed,
        *came,
        name="rest",
    )
    picked = list(tie((picked, (packed_before, rest_sends)))[0])
    near = near_of(packed, came, picked)
    ahead = along(near, BACK)
    total = product(first_kernel, 1, near, coulomb[None, :])

    came_before = [across(packed_before[h], BITS[h][0]) for h in range(2)]
    came_before, total = tie((came_before, total))
    picked_before = pick(packed_before, came_before)
    near_before, before_each = near_of(packed_before, came_before, picked_before, True)
    behind = [along(x, FORTH) for x in before_each]

    rest_sends, ahead, _ = tie((rest_sends, ahead, near_before))
    rest = [across(rest_sends[h], BITS[h][1]) for h in range(2)]

    stack, _ = tie(((near, near_before), ahead))
    both = run(stack_kernel, shape((2, *slices.shape), BF16), *stack, name="stack")
    total = product(
        functools.partial(step_kernel, 1), 2, ahead, other_core(ahead), total
    )
    total = product(
        functools.partial(second_kernel, -1), 3, near_before, other_core(both), total
    )
    behind[0], _ = tie((behind[0], total))
    parts = shape((chips, transfers, 2, 2, t // n_ga, t), F32)
    part = parts.shape[1:]
    stages = []
    done = total
    for j in range(count):
        total, _ = tie((total, done))
        image = run(
            functools.partial(image_kernel, -2, j),
            shape((transfers, g_local, 2 * t), BF16),
            screened,
            behind[j],
            *[other_core(behind[j][part]) for part in range(2)],
            total,
            scratch=[pltpu.VMEM((2 * g_local, 2 * t), BF16)] * 2,
            name="image",
            mib=24,
        )
        rest, _ = tie((rest, image if j == 0 else done))
        far = run(
            functools.partial(far_kernel, held, j, count),
            shape((transfers, 2, g_local, t), BF16),
            *packed,
            *came,
            *picked,
            *rest,
            name="far",
        )
        keep, *gives = run(
            functools.partial(mirror_kernel, chips),
            [parts] + [shape((chips, 2, t // n_ga, t), BF16)] * (2 * transfers),
            image,
            far,
            name="mirror",
            mib=24,
        )
        own, cross, sends = run(
            split_kernel,
            [shape(part, F32), shape(part, F32), shape((2, *part), BF16)],
            keep,
            *[other_core(x) for x in gives],
            name="split",
        )
        if j + 1 < count:
            behind[j + 1], _ = tie((behind[j + 1], keep))
        if stages:
            sends, _ = tie((sends, stages[-1][2]))
        done = own
        came_j = lax.ppermute(sends, "ga", [(i, i ^ 2) for i in range(n_ga)])
        stages.append((own, cross, came_j))
    groups = []
    for own, cross, came_j in stages:
        own, sends = run(
            merge_kernel, [shape(part, F32), shape(part, BF16)], own, cross, came_j, name="merge"
        )
        groups += [own, lax.ppermute(sends, "ga", [(i, i ^ 4) for i in range(n_ga)])]
    result = shape((count, transfers, 2, t // n_ga, t), F32)
    return tuple(
        run(
            functools.partial(finish_kernel, count, 2, -1.0 / math.sqrt(g_total)),
            [result] * 2,
            *groups,
            name="finish",
        )
    )


def plain(densities, screened, coulomb, block_rows):
    owner = lax.axis_index("kp")
    g_slot = lax.axis_index("ga")
    k_held = densities.shape[0]
    g_local = densities.shape[2]
    g_total = screened.shape[3]
    rows = block_rows[0]
    transfers = owner * k_held + jnp.arange(k_held, dtype=jnp.int32)
    far_rows = rows[:, None] + transfers[None, :]
    piece = lax.all_gather(densities, "kp", axis=0, tiled=True)
    labels = jnp.arange(piece.shape[0], dtype=jnp.int32)
    pick_near = (rows[:, None] == labels[None, :]).astype(jnp.bfloat16)
    pick_far = (far_rows[:, :, None] == labels[None, None, :]).astype(jnp.bfloat16)
    near_acc = jnp.einsum(
        "jp,pcgt->jcgt", pick_near, piece, preferred_element_type=jnp.float32
    ).astype(jnp.bfloat16)
    far_acc = jnp.einsum(
        "jsp,pcgt->jscgt", pick_far, piece, preferred_element_type=jnp.float32
    ).astype(jnp.bfloat16)
    columns = jnp.arange(g_total, dtype=jnp.int32)
    own_rows = g_slot * g_local + jnp.arange(g_local, dtype=jnp.int32)
    diag_mask = own_rows[:, None] == columns[None, :]
    coulomb_diag = jnp.where(diag_mask, 2.0 * coulomb[:, None], 0.0)
    screen_real = (coulomb_diag[None] - screened[:, 0].astype(jnp.float32)).astype(jnp.bfloat16)
    screen_imag = -screened[:, 1]
    near_all = lax.all_gather(near_acc, "ga", axis=2, tiled=True)
    piece_real = near_all[:, 0]
    piece_imag = near_all[:, 1]
    real_term = jnp.einsum(
        "sgh,jht->jsgt", screen_real, piece_real, preferred_element_type=jnp.float32
    ) - jnp.einsum("sgh,jht->jsgt", screen_imag, piece_imag, preferred_element_type=jnp.float32)
    imag_term = jnp.einsum(
        "sgh,jht->jsgt", screen_real, piece_imag, preferred_element_type=jnp.float32
    ) + jnp.einsum("sgh,jht->jsgt", screen_imag, piece_real, preferred_element_type=jnp.float32)
    image = jnp.stack([real_term, imag_term], 2)
    image = image.astype(jnp.bfloat16)
    image_real = image[:, :, 0]
    image_imag = image[:, :, 1]
    far_real = far_acc[:, :, 0]
    far_imag = far_acc[:, :, 1]
    lower_real = jnp.einsum(
        "jsga,jsgb->jsab", far_real, image_real, preferred_element_type=jnp.float32
    ) + jnp.einsum("jsga,jsgb->jsab", far_imag, image_imag, preferred_element_type=jnp.float32)
    lower_imag = jnp.einsum(
        "jsga,jsgb->jsab", far_real, image_imag, preferred_element_type=jnp.float32
    ) - jnp.einsum("jsga,jsgb->jsab", far_imag, image_real, preferred_element_type=jnp.float32)
    partial_lower = jnp.stack([lower_real, lower_imag], 2)
    inverse = 1.0 / math.sqrt(g_total)
    mirror = lax.psum_scatter(partial_lower, "ga", scatter_dimension=3, tiled=True) * inverse
    partial_upper = jnp.stack([jnp.swapaxes(lower_real, 2, 3), -jnp.swapaxes(lower_imag, 2, 3)], 2)
    kernel = lax.psum_scatter(partial_upper, "ga", scatter_dimension=3, tiled=True) * inverse
    return (kernel, mirror)


def solution(mesh):
    placed = (P("kp", None, "ga", None), P("kp", None, "ga", None), P("ga"), P("kp", None))
    n_kp, n_ga = mesh.shape["kp"], mesh.shape["ga"]

    def shards(densities, screened, coulomb, block_rows):
        g_local, t = densities.shape[2], densities.shape[3]
        fits = n_kp == 2 * 2 and n_ga == 4 * 2
        fits = fits and g_local % 128 == 0 and t % (8 * n_ga) == 0
        fits = fits and n_kp * densities.shape[0] <= 256
        if fits:
            return quick(n_kp, n_ga, densities, screened, coulomb, block_rows)
        return plain(densities, screened, coulomb, block_rows)

    return jax.shard_map(
        shards,
        mesh=mesh,
        in_specs=placed,
        out_specs=(P("kp", None, None, "ga", None), P("kp", None, None, "ga", None)),
        check_vma=False,
    )
```

```python
import functools
import itertools
import math

import jax
import jax.numpy as jnp
from jax import lax
from jax.experimental import pallas as pl
from jax.experimental.pallas import tpu as pltpu
from jax.sharding import PartitionSpec as P

F32 = jnp.float32
BF16 = jnp.bfloat16
LABELS = 16
VMEM = pl.BlockSpec(memory_space=pltpu.VMEM)
SMEM = pl.BlockSpec(memory_space=pltpu.SMEM)
HBM = pl.BlockSpec(memory_space=pltpu.HBM)


def dot(a, b):
    return jnp.dot(a, b, preferred_element_type=F32)


def tdot(a, b):
    return lax.dot_general(a, b, (((0,), (0,)), ((), ())), preferred_element_type=F32)


def run(body, out, *args, specs=None, scratch=(), name=None, aliases=None, mib=16):
    outs = out if isinstance(out, (list, tuple)) else [out]
    result = pl.pallas_call(
        body,
        in_specs=specs or [VMEM] * len(args),
        out_specs=[VMEM] * len(outs),
        out_shape=list(outs),
        scratch_shapes=list(scratch),
        input_output_aliases=aliases or {},
        compiler_params=pltpu.CompilerParams(vmem_limit_bytes=mib * 2**20),
        cost_estimate=pl.CostEstimate(flops=0, bytes_accessed=0, transcendentals=0),
        name=name,
    )(*args)
    return list(result) if isinstance(out, (list, tuple)) else result[0]


BITS = ((1, 2), (2, 1))


def pack_kernel(rows, densities, *sends):
    held, _, g_local, t = densities.shape
    half = g_local // 2
    for h in range(2):
        for k in range(held):
            for part in range(2):
                at = (2 * k + part) * half
                sends[h][at : at + half] = densities[k, part, h * half : (h + 1) * half]
        line = lax.broadcasted_iota(jnp.int32, (LABELS, t), 0)
        tile = jnp.zeros((LABELS, t), F32)
        for j in range(rows.shape[1]):
            tile = jnp.where(line == j, rows[0, j].astype(F32), tile)
        sends[h][2 * held * half :] = tile.astype(BF16)


def label_of(message, held, half, j):
    tail = message[2 * held * half :].astype(F32)
    return jnp.max(tail[j : j + 1]).astype(jnp.int32)


def entries(message, owner, held, half):
    return [(owner * held + k, message, 2 * k * half, (2 * k + 1) * half) for k in range(held)]


def copy_if(label, found, out):
    half = out.shape[1]
    hit = None
    for name, message, real, imag in found:
        match = label == name
        hit = match if hit is None else hit | match

        @pl.when(match)
        def _(message=message, real=real, imag=imag):
            out[0] = message[real : real + half]
            out[1] = message[imag : imag + half]

    return hit


def pick_kernel(held, packed_0, packed_1, came_0, came_1, *sends):
    owner = lax.axis_index("kp")
    packed, came = (packed_0, packed_1), (came_0, came_1)
    half = sends[0].shape[2]
    for j in range(sends[0].shape[0]):
        for h in range(2):
            found = entries(packed[h], owner, held, half)
            found += entries(came[h], owner ^ BITS[h][0], held, half)
            copy_if(label_of(came[1 - h], held, half, j), found, sends[h].at[j])


def pick_half_kernel(held, count, h, packed, came, labels, send):
    owner = lax.axis_index("kp")
    half = (packed.shape[0] - LABELS) // (2 * held)
    found = entries(packed, owner, held, half)
    found += entries(came, owner ^ BITS[h][0], held, half)
    if len(send.shape) == 2:
        send[2 * count * half :] = jnp.zeros((LABELS, send.shape[1]), BF16)
    for j in range(count):
        label = label_of(labels, held, half, j)
        if len(send.shape) == 4:
            copy_if(label, found, send.at[j])
            continue
        for name, message, real, imag in found:

            @pl.when(label == name)
            def _(j=j, message=message, real=real, imag=imag):
                send[2 * j * half : (2 * j + 1) * half] = message[real : real + half]
                send[(2 * j + 1) * half : (2 * j + 2) * half] = message[imag : imag + half]


def near_kernel(held, packed_0, packed_1, came_0, came_1, picked_0, picked_1, near, *each):
    owner = lax.axis_index("kp")
    packed, came, picked = (packed_0, packed_1), (came_0, came_1), (picked_0, picked_1)
    half = picked_1.shape[2]
    for j in range(near.shape[0]):
        label = label_of(packed_0, held, half, j)
        for h in range(2):
            out = near.at[j, :, h * half : (h + 1) * half]
            found = entries(packed[h], owner, held, half)
            found += entries(came[h], owner ^ BITS[h][0], held, half)
            hit = copy_if(label, found, out)

            @pl.when(jnp.logical_not(hit))
            def _(h=h, j=j, out=out):
                if len(picked[h].shape) == 4:
                    out[...] = picked[h][j]
                else:
                    out[0] = picked[h][2 * j * half : (2 * j + 1) * half]
                    out[1] = picked[h][(2 * j + 1) * half : (2 * j + 2) * half]

    for j, out in enumerate(each):
        out[...] = near[j]


def stack_kernel(*refs):
    for i, ref in enumerate(refs[:-1]):
        refs[-1][i] = ref[...]


def left_over(n_kp, held, transfers, count):
    most = []
    for first, second in BITS:
        worst = 0
        for owner in range(n_kp):
            side = {who * held + k for who in (owner ^ second, owner ^ second ^ first) for k in range(held)}
            rows = range(n_kp * held - transfers * (owner + 1) + 1)
            for chosen in itertools.product(rows, repeat=count):
                need = {r + owner * transfers + s for r in chosen for s in range(transfers)}
                worst = max(worst, len((need & side) - set(chosen)))
        most.append(max(worst, 1))
    return most


def slots(labels, rows, owner, transfers):
    found, place = [], jnp.int32(0)
    for label in labels:
        need, sent = jnp.bool_(False), jnp.bool_(False)
        for row in rows:
            first = row + owner * transfers
            need = need | ((label >= first) & (label < first + transfers))
            sent = sent | (label == row)
        need = need & jnp.logical_not(sent)
        found.append((need, place))
        place = place + need.astype(jnp.int32)
    return found


def rest_kernel(held, transfers, count, packed_0, packed_1, came_0, came_1, *sends):
    owner = lax.axis_index("kp")
    packed, came = (packed_0, packed_1), (came_0, came_1)
    for h in range(2):
        first, second = BITS[h]
        room, _, half, _ = sends[h].shape
        found = entries(packed[h], owner, held, half)
        found += entries(came[h], owner ^ first, held, half)
        rows = [label_of(came[1 - h], held, half, j) for j in range(count)]
        places = slots([label for label, *_ in found], rows, owner ^ second, transfers)
        for (_, message, real, imag), (need, place) in zip(found, places):
            for i in range(room):

                @pl.when(need & (place == i))
                def _(h=h, i=i, message=message, real=real, imag=imag, half=half):
                    sends[h][i, 0] = message[real : real + half]
                    sends[h][i, 1] = message[imag : imag + half]


def far_kernel(
    held, j, count, packed_0, packed_1, came_0, came_1, picked_0, picked_1, rest_0, rest_1, far
):
    owner = lax.axis_index("kp")
    packed, came = (packed_0, packed_1), (came_0, came_1)
    picked, rest = (picked_0, picked_1), (rest_0, rest_1)
    transfers, _, g_local, _ = far.shape
    half = g_local // 2
    rows = [label_of(packed_0, held, half, j) for j in range(count)]
    for h in range(2):
        first, second = BITS[h]
        found = entries(packed[h], owner, held, half)
        found += entries(came[h], owner ^ first, held, half)
        side = [
            who * held + k for who in (owner ^ second, owner ^ second ^ first) for k in range(held)
        ]
        places = slots(side, rows, owner, transfers)
        for s in range(transfers):
            label = rows[j] + owner * transfers + s
            out = far.at[s, :, h * half : (h + 1) * half]
            hit = copy_if(label, found, out)
            for i in range(count):
                match = (label == rows[i]) & jnp.logical_not(hit)
                hit = hit | match

                @pl.when(match)
                def _(h=h, i=i, out=out):
                    out[...] = picked[h][i]

            for name, (need, place) in zip(side, places):
                for i in range(rest[h].shape[0]):

                    @pl.when((label == name) & need & (place == i))
                    def _(h=h, i=i, out=out):
                        out[...] = rest[h][i]


def load_kernel(source, panels, sems):
    copies = []
    for s in range(source.shape[0]):
        for part in range(2):
            copy = pltpu.make_async_copy(source.at[s, part], panels.at[s, part], sems.at[2 * s + part])
            copy.start()
            copies.append(copy)
    for copy in copies:
        copy.wait()


FORTH = (1, 3, 0, 2)
BACK = (2, 0, 3, 1)


def chip_at(z, steps):
    if steps == 1:
        return jnp.where(z < 2, 2 * z + 1, 2 * z - 4)
    if steps == -1:
        return jnp.where(lax.rem(z, 2) == 0, 2 + z // 2, z // 2)
    return z if steps == 0 else 3 - z


def lay(terms, upper, lower):
    for ref, first in terms:
        *count, _, g_local, t = ref.shape
        rows = pl.ds(first if isinstance(first, int) else pl.multiple_of(first, 128), g_local)
        for j, panel in enumerate([ref.at[j] for j in range(count[0])] if count else [ref]):
            real, imag = slice(2 * j * t, (2 * j + 1) * t), slice((2 * j + 1) * t, (2 * j + 2) * t)
            upper[rows, real] = panel[0]
            upper[rows, imag] = panel[1]
            lower[rows, real] = -panel[1]
            lower[rows, imag] = panel[0]


def place():
    slot = lax.axis_index("ga")
    return slot // 2, lax.rem(slot, 2)


def multiply(screened, s, span, width, upper, lower, first=0):
    span = pl.ds(pl.multiple_of(span, 128), width)
    rows = slice(first, first + width)
    return dot(screened[s, 0, :, span], upper[rows]) + dot(screened[s, 1, :, span], lower[rows])


def first_kernel(screened, own, coulomb, total, upper, lower):
    z, core = place()
    g = screened.shape[2]
    lay([(own, 0)], upper, lower)
    span = pl.ds(pl.multiple_of((2 * z + core) * g, 128), g)
    line = lax.broadcasted_iota(jnp.int32, (g, g), 0)
    on = line == lax.broadcasted_iota(jnp.int32, (g, g), 1)
    for s in range(screened.shape[0]):
        real = screened[s, 0, :, span]
        real = jnp.where(on, (real.astype(F32) - 2.0 * coulomb[...]).astype(BF16), real)
        total[s] = dot(real, upper[...]) + dot(screened[s, 1, :, span], lower[...])


def step_kernel(steps, screened, own, pair, before, total, upper, lower):
    z, core = place()
    g = screened.shape[2]
    lay([(own, core * g), (pair, (1 - core) * g)], upper, lower)
    span = 2 * chip_at(z, steps) * g
    for s in range(screened.shape[0]):
        total[s] = before[s] + multiply(screened, s, span, 2 * g, upper, lower)


def second_kernel(steps, screened, own, pairs, before, total, upper, lower):
    z, core = place()
    g = screened.shape[2]
    lay([(own, core * g), (pairs.at[1], (1 - core) * g), (pairs.at[0], 2 * g)], upper, lower)
    span = 2 * chip_at(z, steps) * g
    left = (2 * z + 1 - core) * g
    for s in range(screened.shape[0]):
        value = before[s] + multiply(screened, s, span, 2 * g, upper, lower)
        total[s] = value + multiply(screened, s, left, g, upper, lower, 2 * g)


def image_kernel(steps, j, screened, own, pair_real, pair_imag, before, image, upper, lower):
    z, core = place()
    g = screened.shape[2]
    t = own.shape[2]
    lay([(own, core * g)], upper, lower)
    rows = pl.ds(pl.multiple_of((1 - core) * g, 128), g)
    upper[rows, :t] = pair_real[...]
    upper[rows, t:] = pair_imag[...]
    lower[rows, :t] = -pair_imag[...]
    lower[rows, t:] = pair_real[...]
    span = 2 * chip_at(z, steps) * g
    for s in range(screened.shape[0]):
        value = before[s, :, 2 * j * t : 2 * (j + 1) * t]
        image[s] = (value + multiply(screened, s, span, 2 * g, upper, lower)).astype(BF16)


def mirror_kernel(chips, image, far, keep, *gives):
    first = lax.rem(lax.axis_index("ga"), 2) == 0
    t = far.shape[-1]
    for s in range(image.shape[0]):
        by_real, by_imag = tdot(far[s, 0], image[s]), tdot(far[s, 1], image[s])
        real = by_real[:, :t] + by_imag[:, t:]
        imag = by_real[:, t:] - by_imag[:, :t]
        parts = ((real, imag), (real.T, -imag.T))
        for which in range(2):
            for part in range(2):
                block = parts[which][part]
                block = block.reshape(chips, 2, t // (2 * chips), t)
                keep[:, s, which, part] = jnp.where(first, block[:, 0], block[:, 1])
                give = jnp.where(first, block[:, 1], block[:, 0])
                gives[2 * s + which][:, part] = give.astype(BF16)


def split_kernel(keep, *refs):
    *came, own, cross, sends = refs
    z = lax.axis_index("ga") // 2
    for s in range(keep.shape[1]):
        for which in range(2):

            def chip(at):
                return keep[at, s, which] + came[2 * s + which][at].astype(F32)

            own[s, which] = chip(z)
            cross[s, which] = chip(z ^ 2)
            for i, at in enumerate((z ^ 1, z ^ 3)):
                sends[i, s, which] = chip(at).astype(BF16)


def merge_kernel(own, cross, came, total, sends):
    total[...] = own[...] + came[0].astype(F32)
    sends[...] = (cross[...] + came[1].astype(F32)).astype(BF16)


def finish_kernel(count, chips, scale, *refs):
    kernel, mirror = refs[-2:]
    for j in range(count):
        terms = refs[j * chips : (j + 1) * chips]
        total = terms[0][...]
        for term in terms[1:]:
            total = total + term[...].astype(F32)
        mirror[j] = total[:, 0] * scale
        kernel[j] = total[:, 1] * scale


def quick(n_kp, n_ga, densities, screened, coulomb, block_rows):
    held, _, g_local, t = densities.shape
    transfers, g_total = screened.shape[0], screened.shape[3]
    count = block_rows.shape[1]
    chips = n_ga // 2
    half = g_local // 2
    shape = jax.ShapeDtypeStruct
    tie = lax.optimization_barrier

    def across(x, bit):
        return lax.ppermute(x, "kp", [(i, i ^ bit) for i in range(n_kp)])

    def other_core(x):
        return lax.ppermute(x, "ga", [(i, i ^ 1) for i in range(n_ga)])

    def along(x, chips_on):
        return lax.ppermute(x, "ga", [(i, 2 * chips_on[i // 2] + i % 2) for i in range(n_ga)])

    message = shape((2 * held * half + LABELS, t), BF16)

    sums = shape((transfers, g_local, 2 * count * t), F32)

    def product(body, terms, *args):
        return run(
            body,
            sums,
            screened,
            *args,
            scratch=[pltpu.VMEM((terms * g_local, 2 * count * t), BF16)] * 2,
            aliases={} if terms == 1 else {3: 0},
            name="product",
            mib=24,
        )

    def pick(packed, came):
        sends = run(
            functools.partial(pick_kernel, held),
            [shape((count, 2, half, t), BF16)] * 2,
            *packed,
            *came,
            name="pick",
        )
        return [across(sends[h], BITS[h][1]) for h in range(2)]

    slices = shape((count, 2, g_local, t), BF16)

    def near_of(packed, came, picked, apart=False):
        kernel = functools.partial(near_kernel, held)
        outs = [slices] + [shape(slices.shape[1:], BF16)] * (count if apart else 0)
        near, *each = run(kernel, outs, *packed, *came, *picked, name="near")
        return (near, each) if apart else near

    packed = run(
        pack_kernel, [message] * 2, block_rows, densities, specs=[SMEM, VMEM], name="pack", mib=53
    )
    packed_before = [along(x, FORTH) for x in packed]
    came = [across(packed[h], BITS[h][0]) for h in range(2)]
    source, packed = tie((screened, packed))
    screened = run(
        load_kernel,
        shape(screened.shape, screened.dtype),
        source,
        specs=[HBM],
        scratch=[pltpu.SemaphoreType.DMA((2 * transfers,))],
        name="load",
        mib=40,
    )
    came, screened = tie((came, screened))
    picked = pick(packed, came)
    rest_sends = run(
        functools.partial(rest_kernel, held, transfers, count),
        [shape((room, 2, half, t), BF16) for room in left_over(n_kp, held, transfers, count)],
        *packed,
        *came,
        name="rest",
    )
    picked = list(tie((picked, (packed_before, rest_sends)))[0])
    near = near_of(packed, came, picked)
    ahead = along(near, BACK)
    total = product(first_kernel, 1, near, coulomb[None, :])

    came_before = [across(packed_before[h], BITS[h][0]) for h in range(2)]
    picked_before, sent = [None, None], total
    for h in range(2):
        came_h, _ = tie((came_before[h], sent))
        sent = run(
            functools.partial(pick_half_kernel, held, count, h),
            shape((count, 2, half, t) if h else (2 * count * half + LABELS, t), BF16),
            packed_before[h],
            came_h,
            came[1 - h],
            name="pick_half",
        )
        picked_before[h] = across(sent, BITS[h][1])
    near_before, before_each = near_of(packed_before, came_before, picked_before, True)
    behind = [along(x, FORTH) for x in before_each]

    rest_sends, ahead, _ = tie((rest_sends, ahead, near_before))
    rest = [across(rest_sends[h], BITS[h][1]) for h in range(2)]

    stack, _ = tie(((near, near_before), ahead))
    both = run(stack_kernel, shape((2, *slices.shape), BF16), *stack, name="stack")
    total = product(
        functools.partial(step_kernel, 1), 2, ahead, other_core(ahead), total
    )
    total = product(
        functools.partial(second_kernel, -1), 3, near_before, other_core(both), total
    )
    behind[0], _ = tie((behind[0], total))
    parts = shape((chips, transfers, 2, 2, t // n_ga, t), F32)
    part = parts.shape[1:]
    stages = []
    done = total
    for j in range(count):
        total, _ = tie((total, done))
        image = run(
            functools.partial(image_kernel, -2, j),
            shape((transfers, g_local, 2 * t), BF16),
            screened,
            behind[j],
            *[other_core(behind[j][part]) for part in range(2)],
            total,
            scratch=[pltpu.VMEM((2 * g_local, 2 * t), BF16)] * 2,
            name="image",
            mib=24,
        )
        rest, _ = tie((rest, image if j == 0 else done))
        far = run(
            functools.partial(far_kernel, held, j, count),
            shape((transfers, 2, g_local, t), BF16),
            *packed,
            *came,
            *picked,
            *rest,
            name="far",
        )
        keep, *gives = run(
            functools.partial(mirror_kernel, chips),
            [parts] + [shape((chips, 2, t // n_ga, t), BF16)] * (2 * transfers),
            image,
            far,
            name="mirror",
            mib=24,
        )
        own, cross, sends = run(
            split_kernel,
            [shape(part, F32), shape(part, F32), shape((2, *part), BF16)],
            keep,
            *[other_core(x) for x in gives],
            name="split",
        )
        if j + 1 < count:
            behind[j + 1], _ = tie((behind[j + 1], keep))
        if stages:
            sends, _ = tie((sends, stages[-1][2]))
        done = own
        came_j = lax.ppermute(sends, "ga", [(i, i ^ 2) for i in range(n_ga)])
        stages.append((own, cross, came_j))
    groups = []
    for own, cross, came_j in stages:
        own, sends = run(
            merge_kernel, [shape(part, F32), shape(part, BF16)], own, cross, came_j, name="merge"
        )
        groups += [own, lax.ppermute(sends, "ga", [(i, i ^ 4) for i in range(n_ga)])]
    result = shape((count, transfers, 2, t // n_ga, t), F32)
    return tuple(
        run(
            functools.partial(finish_kernel, count, 2, -1.0 / math.sqrt(g_total)),
            [result] * 2,
            *groups,
            name="finish",
        )
    )


def plain(densities, screened, coulomb, block_rows):
    owner = lax.axis_index("kp")
    g_slot = lax.axis_index("ga")
    k_held = densities.shape[0]
    g_local = densities.shape[2]
    g_total = screened.shape[3]
    rows = block_rows[0]
    transfers = owner * k_held + jnp.arange(k_held, dtype=jnp.int32)
    far_rows = rows[:, None] + transfers[None, :]
    piece = lax.all_gather(densities, "kp", axis=0, tiled=True)
    labels = jnp.arange(piece.shape[0], dtype=jnp.int32)
    pick_near = (rows[:, None] == labels[None, :]).astype(jnp.bfloat16)
    pick_far = (far_rows[:, :, None] == labels[None, None, :]).astype(jnp.bfloat16)
    near_acc = jnp.einsum(
        "jp,pcgt->jcgt", pick_near, piece, preferred_element_type=jnp.float32
    ).astype(jnp.bfloat16)
    far_acc = jnp.einsum(
        "jsp,pcgt->jscgt", pick_far, piece, preferred_element_type=jnp.float32
    ).astype(jnp.bfloat16)
    columns = jnp.arange(g_total, dtype=jnp.int32)
    own_rows = g_slot * g_local + jnp.arange(g_local, dtype=jnp.int32)
    diag_mask = own_rows[:, None] == columns[None, :]
    coulomb_diag = jnp.where(diag_mask, 2.0 * coulomb[:, None], 0.0)
    screen_real = (coulomb_diag[None] - screened[:, 0].astype(jnp.float32)).astype(jnp.bfloat16)
    screen_imag = -screened[:, 1]
    near_all = lax.all_gather(near_acc, "ga", axis=2, tiled=True)
    piece_real = near_all[:, 0]
    piece_imag = near_all[:, 1]
    real_term = jnp.einsum(
        "sgh,jht->jsgt", screen_real, piece_real, preferred_element_type=jnp.float32
    ) - jnp.einsum("sgh,jht->jsgt", screen_imag, piece_imag, preferred_element_type=jnp.float32)
    imag_term = jnp.einsum(
        "sgh,jht->jsgt", screen_real, piece_imag, preferred_element_type=jnp.float32
    ) + jnp.einsum("sgh,jht->jsgt", screen_imag, piece_real, preferred_element_type=jnp.float32)
    image = jnp.stack([real_term, imag_term], 2)
    image = image.astype(jnp.bfloat16)
    image_real = image[:, :, 0]
    image_imag = image[:, :, 1]
    far_real = far_acc[:, :, 0]
    far_imag = far_acc[:, :, 1]
    lower_real = jnp.einsum(
        "jsga,jsgb->jsab", far_real, image_real, preferred_element_type=jnp.float32
    ) + jnp.einsum("jsga,jsgb->jsab", far_imag, image_imag, preferred_element_type=jnp.float32)
    lower_imag = jnp.einsum(
        "jsga,jsgb->jsab", far_real, image_imag, preferred_element_type=jnp.float32
    ) - jnp.einsum("jsga,jsgb->jsab", far_imag, image_real, preferred_element_type=jnp.float32)
    partial_lower = jnp.stack([lower_real, lower_imag], 2)
    inverse = 1.0 / math.sqrt(g_total)
    mirror = lax.psum_scatter(partial_lower, "ga", scatter_dimension=3, tiled=True) * inverse
    partial_upper = jnp.stack([jnp.swapaxes(lower_real, 2, 3), -jnp.swapaxes(lower_imag, 2, 3)], 2)
    kernel = lax.psum_scatter(partial_upper, "ga", scatter_dimension=3, tiled=True) * inverse
    return (kernel, mirror)


def solution(mesh):
    placed = (P("kp", None, "ga", None), P("kp", None, "ga", None), P("ga"), P("kp", None))
    n_kp, n_ga = mesh.shape["kp"], mesh.shape["ga"]

    def shards(densities, screened, coulomb, block_rows):
        g_local, t = densities.shape[2], densities.shape[3]
        fits = n_kp == 2 * 2 and n_ga == 4 * 2
        fits = fits and g_local % 128 == 0 and t % (8 * n_ga) == 0
        fits = fits and n_kp * densities.shape[0] <= 256
        if fits:
            return quick(n_kp, n_ga, densities, screened, coulomb, block_rows)
        return plain(densities, screened, coulomb, block_rows)

    return jax.shard_map(
        shards,
        mesh=mesh,
        in_specs=placed,
        out_specs=(P("kp", None, None, "ga", None), P("kp", None, None, "ga", None)),
        check_vma=False,
    )
```

```python
import functools
import itertools
import math

import jax
import jax.numpy as jnp
from jax import lax
from jax.experimental import pallas as pl
from jax.experimental.pallas import tpu as pltpu
from jax.sharding import PartitionSpec as P

F32 = jnp.float32
BF16 = jnp.bfloat16
LABELS = 16
VMEM = pl.BlockSpec(memory_space=pltpu.VMEM)
SMEM = pl.BlockSpec(memory_space=pltpu.SMEM)
HBM = pl.BlockSpec(memory_space=pltpu.HBM)


def dot(a, b):
    return jnp.dot(a, b, preferred_element_type=F32)


def tdot(a, b):
    return lax.dot_general(a, b, (((0,), (0,)), ((), ())), preferred_element_type=F32)


def run(body, out, *args, specs=None, scratch=(), name=None, aliases=None, mib=16):
    outs = out if isinstance(out, (list, tuple)) else [out]
    result = pl.pallas_call(
        body,
        in_specs=specs or [VMEM] * len(args),
        out_specs=[VMEM] * len(outs),
        out_shape=list(outs),
        scratch_shapes=list(scratch),
        input_output_aliases=aliases or {},
        compiler_params=pltpu.CompilerParams(vmem_limit_bytes=mib * 2**20),
        cost_estimate=pl.CostEstimate(flops=0, bytes_accessed=0, transcendentals=0),
        name=name,
    )(*args)
    return list(result) if isinstance(out, (list, tuple)) else result[0]


BITS = ((1, 2), (2, 1))


def pack_kernel(rows, densities, *sends):
    held, _, g_local, t = densities.shape
    half = g_local // 2
    for h in range(2):
        for k in range(held):
            for part in range(2):
                at = (2 * k + part) * half
                sends[h][at : at + half] = densities[k, part, h * half : (h + 1) * half]
        line = lax.broadcasted_iota(jnp.int32, (LABELS, t), 0)
        tile = jnp.zeros((LABELS, t), F32)
        for j in range(rows.shape[1]):
            tile = jnp.where(line == j, rows[0, j].astype(F32), tile)
        sends[h][2 * held * half :] = tile.astype(BF16)


def label_of(message, held, half, j):
    tail = message[2 * held * half :].astype(F32)
    return jnp.max(tail[j : j + 1]).astype(jnp.int32)


def entries(message, owner, held, half):
    return [(owner * held + k, message, 2 * k * half, (2 * k + 1) * half) for k in range(held)]


def copy_if(label, found, out):
    half = out.shape[1]
    hit = None
    for name, message, real, imag in found:
        match = label == name
        hit = match if hit is None else hit | match

        @pl.when(match)
        def _(message=message, real=real, imag=imag):
            out[0] = message[real : real + half]
            out[1] = message[imag : imag + half]

    return hit


def pick_kernel(held, packed_0, packed_1, came_0, came_1, *sends):
    owner = lax.axis_index("kp")
    packed, came = (packed_0, packed_1), (came_0, came_1)
    half = sends[0].shape[2]
    for j in range(sends[0].shape[0]):
        for h in range(2):
            found = entries(packed[h], owner, held, half)
            found += entries(came[h], owner ^ BITS[h][0], held, half)
            copy_if(label_of(came[1 - h], held, half, j), found, sends[h].at[j])


def pick_half_kernel(held, count, h, packed, came, labels, send):
    owner = lax.axis_index("kp")
    half = (packed.shape[0] - LABELS) // (2 * held)
    found = entries(packed, owner, held, half)
    found += entries(came, owner ^ BITS[h][0], held, half)
    if len(send.shape) == 2:
        send[2 * count * half :] = jnp.zeros((LABELS, send.shape[1]), BF16)
    for j in range(count):
        label = label_of(labels, held, half, j)
        if len(send.shape) == 4:
            copy_if(label, found, send.at[j])
            continue
        for name, message, real, imag in found:

            @pl.when(label == name)
            def _(j=j, message=message, real=real, imag=imag):
                send[2 * j * half : (2 * j + 1) * half] = message[real : real + half]
                send[(2 * j + 1) * half : (2 * j + 2) * half] = message[imag : imag + half]


def near_kernel(held, packed_0, packed_1, came_0, came_1, picked_0, picked_1, near, *each):
    owner = lax.axis_index("kp")
    packed, came, picked = (packed_0, packed_1), (came_0, came_1), (picked_0, picked_1)
    half = picked_1.shape[2]
    for j in range(near.shape[0]):
        label = label_of(packed_0, held, half, j)
        for h in range(2):
            out = near.at[j, :, h * half : (h + 1) * half]
            found = entries(packed[h], owner, held, half)
            found += entries(came[h], owner ^ BITS[h][0], held, half)
            hit = copy_if(label, found, out)

            @pl.when(jnp.logical_not(hit))
            def _(h=h, j=j, out=out):
                if len(picked[h].shape) == 4:
                    out[...] = picked[h][j]
                else:
                    out[0] = picked[h][2 * j * half : (2 * j + 1) * half]
                    out[1] = picked[h][(2 * j + 1) * half : (2 * j + 2) * half]

    for j, out in enumerate(each):
        out[...] = near[j]


def stack_kernel(*refs):
    for i, ref in enumerate(refs[:-1]):
        refs[-1][i] = ref[...]


def left_over(n_kp, held, transfers, count):
    most = []
    for first, second in BITS:
        worst = 0
        for owner in range(n_kp):
            side = {who * held + k for who in (owner ^ second, owner ^ second ^ first) for k in range(held)}
            rows = range(n_kp * held - transfers * (owner + 1) + 1)
            for chosen in itertools.product(rows, repeat=count):
                need = {r + owner * transfers + s for r in chosen for s in range(transfers)}
                worst = max(worst, len((need & side) - set(chosen)))
        most.append(max(worst, 1))
    return most


def slots(labels, rows, owner, transfers):
    found, place = [], jnp.int32(0)
    for label in labels:
        need, sent = jnp.bool_(False), jnp.bool_(False)
        for row in rows:
            first = row + owner * transfers
            need = need | ((label >= first) & (label < first + transfers))
            sent = sent | (label == row)
        need = need & jnp.logical_not(sent)
        found.append((need, place))
        place = place + need.astype(jnp.int32)
    return found


def rest_kernel(held, transfers, count, packed_0, packed_1, came_0, came_1, *sends):
    owner = lax.axis_index("kp")
    packed, came = (packed_0, packed_1), (came_0, came_1)
    for h in range(2):
        first, second = BITS[h]
        room, _, half, _ = sends[h].shape
        found = entries(packed[h], owner, held, half)
        found += entries(came[h], owner ^ first, held, half)
        rows = [label_of(came[1 - h], held, half, j) for j in range(count)]
        places = slots([label for label, *_ in found], rows, owner ^ second, transfers)
        for (_, message, real, imag), (need, place) in zip(found, places):
            for i in range(room):

                @pl.when(need & (place == i))
                def _(h=h, i=i, message=message, real=real, imag=imag, half=half):
                    sends[h][i, 0] = message[real : real + half]
                    sends[h][i, 1] = message[imag : imag + half]


def far_kernel(
    held, j, count, packed_0, packed_1, came_0, came_1, picked_0, picked_1, rest_0, rest_1, far
):
    owner = lax.axis_index("kp")
    packed, came = (packed_0, packed_1), (came_0, came_1)
    picked, rest = (picked_0, picked_1), (rest_0, rest_1)
    transfers, _, g_local, _ = far.shape
    half = g_local // 2
    rows = [label_of(packed_0, held, half, j) for j in range(count)]
    for h in range(2):
        first, second = BITS[h]
        found = entries(packed[h], owner, held, half)
        found += entries(came[h], owner ^ first, held, half)
        side = [
            who * held + k for who in (owner ^ second, owner ^ second ^ first) for k in range(held)
        ]
        places = slots(side, rows, owner, transfers)
        for s in range(transfers):
            label = rows[j] + owner * transfers + s
            out = far.at[s, :, h * half : (h + 1) * half]
            hit = copy_if(label, found, out)
            for i in range(count):
                match = (label == rows[i]) & jnp.logical_not(hit)
                hit = hit | match

                @pl.when(match)
                def _(h=h, i=i, out=out):
                    out[...] = picked[h][i]

            for name, (need, place) in zip(side, places):
                for i in range(rest[h].shape[0]):

                    @pl.when((label == name) & need & (place == i))
                    def _(h=h, i=i, out=out):
                        out[...] = rest[h][i]


def load_kernel(source, panels, sems):
    copies = []
    for s in range(source.shape[0]):
        for part in range(2):
            copy = pltpu.make_async_copy(source.at[s, part], panels.at[s, part], sems.at[2 * s + part])
            copy.start()
            copies.append(copy)
    for copy in copies:
        copy.wait()


FORTH = (1, 3, 0, 2)
BACK = (2, 0, 3, 1)


def chip_at(z, steps):
    if steps == 1:
        return jnp.where(z < 2, 2 * z + 1, 2 * z - 4)
    if steps == -1:
        return jnp.where(lax.rem(z, 2) == 0, 2 + z // 2, z // 2)
    return z if steps == 0 else 3 - z


def lay(terms, upper, lower):
    for ref, first in terms:
        *count, _, g_local, t = ref.shape
        rows = pl.ds(first if isinstance(first, int) else pl.multiple_of(first, 128), g_local)
        for j, panel in enumerate([ref.at[j] for j in range(count[0])] if count else [ref]):
            real, imag = slice(2 * j * t, (2 * j + 1) * t), slice((2 * j + 1) * t, (2 * j + 2) * t)
            upper[rows, real] = panel[0]
            upper[rows, imag] = panel[1]
            lower[rows, real] = -panel[1]
            lower[rows, imag] = panel[0]


def place():
    slot = lax.axis_index("ga")
    return slot // 2, lax.rem(slot, 2)


def multiply(screened, s, span, width, upper, lower, first=0):
    span = pl.ds(pl.multiple_of(span, 128), width)
    rows = slice(first, first + width)
    return dot(screened[s, 0, :, span], upper[rows]) + dot(screened[s, 1, :, span], lower[rows])


def first_kernel(screened, own, coulomb, total, upper, lower):
    z, core = place()
    g = screened.shape[2]
    lay([(own, 0)], upper, lower)
    span = pl.ds(pl.multiple_of((2 * z + core) * g, 128), g)
    line = lax.broadcasted_iota(jnp.int32, (g, g), 0)
    on = line == lax.broadcasted_iota(jnp.int32, (g, g), 1)
    for s in range(screened.shape[0]):
        real = screened[s, 0, :, span]
        real = jnp.where(on, (real.astype(F32) - 2.0 * coulomb[...]).astype(BF16), real)
        total[s] = dot(real, upper[...]) + dot(screened[s, 1, :, span], lower[...])


def step_kernel(steps, screened, own, pair, before, total, upper, lower):
    z, core = place()
    g = screened.shape[2]
    lay([(own, core * g), (pair, (1 - core) * g)], upper, lower)
    span = 2 * chip_at(z, steps) * g
    for s in range(screened.shape[0]):
        total[s] = before[s] + multiply(screened, s, span, 2 * g, upper, lower)


def second_kernel(steps, screened, own, pairs, before, total, upper, lower):
    z, core = place()
    g = screened.shape[2]
    lay([(own, core * g), (pairs.at[1], (1 - core) * g), (pairs.at[0], 2 * g)], upper, lower)
    span = 2 * chip_at(z, steps) * g
    left = (2 * z + 1 - core) * g
    for s in range(screened.shape[0]):
        value = before[s] + multiply(screened, s, span, 2 * g, upper, lower)
        total[s] = value + multiply(screened, s, left, g, upper, lower, 2 * g)


def image_kernel(steps, j, screened, own, pair_real, pair_imag, before, image, upper, lower):
    z, core = place()
    g = screened.shape[2]
    t = own.shape[2]
    lay([(own, core * g)], upper, lower)
    rows = pl.ds(pl.multiple_of((1 - core) * g, 128), g)
    upper[rows, :t] = pair_real[...]
    upper[rows, t:] = pair_imag[...]
    lower[rows, :t] = -pair_imag[...]
    lower[rows, t:] = pair_real[...]
    span = 2 * chip_at(z, steps) * g
    for s in range(screened.shape[0]):
        value = before[s, :, 2 * j * t : 2 * (j + 1) * t]
        image[s] = (value + multiply(screened, s, span, 2 * g, upper, lower)).astype(BF16)


def mirror_kernel(chips, image, far, keep, *gives):
    first = lax.rem(lax.axis_index("ga"), 2) == 0
    t = far.shape[-1]
    for s in range(image.shape[0]):
        by_real, by_imag = tdot(far[s, 0], image[s]), tdot(far[s, 1], image[s])
        real = by_real[:, :t] + by_imag[:, t:]
        imag = by_real[:, t:] - by_imag[:, :t]
        parts = ((real, imag), (real.T, -imag.T))
        for which in range(2):
            for part in range(2):
                block = parts[which][part]
                block = block.reshape(chips, 2, t // (2 * chips), t)
                keep[:, s, which, part] = jnp.where(first, block[:, 0], block[:, 1])
                give = jnp.where(first, block[:, 1], block[:, 0])
                gives[2 * s + which][:, part] = give.astype(BF16)


def split_kernel(keep, *refs):
    count = 2 * keep.shape[1]
    came, (own, cross, *sends) = refs[:count], refs[count:]
    z = lax.axis_index("ga") // 2
    for s in range(keep.shape[1]):
        for which in range(2):

            def chip(at):
                return keep[at, s, which] + came[2 * s + which][at].astype(F32)

            own[s, which] = chip(z)
            cross[s, which] = chip(z ^ 2)
            for i, at in enumerate((z ^ 1, z ^ 3)):
                out = sends[0].at[i] if len(sends) == 1 else sends[i]
                out[s, which] = chip(at).astype(BF16)


def merge_kernel(own, cross, *refs):
    *came, total, sends = refs
    shares = came if len(came) == 2 else (came[0].at[0], came[0].at[1])
    total[...] = own[...] + shares[0][...].astype(F32)
    sends[...] = (cross[...] + shares[1][...].astype(F32)).astype(BF16)


def finish_kernel(count, chips, scale, *refs):
    kernel, mirror = refs[-2:]
    for j in range(count):
        terms = refs[j * chips : (j + 1) * chips]
        total = terms[0][...]
        for term in terms[1:]:
            total = total + term[...].astype(F32)
        mirror[j] = total[:, 0] * scale
        kernel[j] = total[:, 1] * scale


def quick(n_kp, n_ga, densities, screened, coulomb, block_rows):
    held, _, g_local, t = densities.shape
    transfers, g_total = screened.shape[0], screened.shape[3]
    count = block_rows.shape[1]
    chips = n_ga // 2
    half = g_local // 2
    shape = jax.ShapeDtypeStruct
    tie = lax.optimization_barrier

    def across(x, bit):
        return lax.ppermute(x, "kp", [(i, i ^ bit) for i in range(n_kp)])

    def other_core(x):
        return lax.ppermute(x, "ga", [(i, i ^ 1) for i in range(n_ga)])

    def along(x, chips_on):
        return lax.ppermute(x, "ga", [(i, 2 * chips_on[i // 2] + i % 2) for i in range(n_ga)])

    message = shape((2 * held * half + LABELS, t), BF16)

    sums = shape((transfers, g_local, 2 * count * t), F32)

    def product(body, terms, *args):
        return run(
            body,
            sums,
            screened,
            *args,
            scratch=[pltpu.VMEM((terms * g_local, 2 * count * t), BF16)] * 2,
            aliases={} if terms == 1 else {3: 0},
            name="product",
            mib=24,
        )

    def pick(packed, came):
        sends = run(
            functools.partial(pick_kernel, held),
            [shape((count, 2, half, t), BF16)] * 2,
            *packed,
            *came,
            name="pick",
        )
        return [across(sends[h], BITS[h][1]) for h in range(2)]

    slices = shape((count, 2, g_local, t), BF16)

    def near_of(packed, came, picked, apart=False):
        kernel = functools.partial(near_kernel, held)
        outs = [slices] + [shape(slices.shape[1:], BF16)] * (count if apart else 0)
        near, *each = run(kernel, outs, *packed, *came, *picked, name="near")
        return (near, each) if apart else near

    packed = run(
        pack_kernel, [message] * 2, block_rows, densities, specs=[SMEM, VMEM], name="pack", mib=53
    )
    packed_before = [along(x, FORTH) for x in packed]
    came = [across(packed[h], BITS[h][0]) for h in range(2)]
    source, packed = tie((screened, packed))
    screened = run(
        load_kernel,
        shape(screened.shape, screened.dtype),
        source,
        specs=[HBM],
        scratch=[pltpu.SemaphoreType.DMA((2 * transfers,))],
        name="load",
        mib=40,
    )
    came, screened = tie((came, screened))
    picked = pick(packed, came)
    rest_sends = run(
        functools.partial(rest_kernel, held, transfers, count),
        [shape((room, 2, half, t), BF16) for room in left_over(n_kp, held, transfers, count)],
        *packed,
        *came,
        name="rest",
    )
    picked = list(tie((picked, (packed_before, rest_sends)))[0])
    near = near_of(packed, came, picked)
    ahead = along(near, BACK)
    total = product(first_kernel, 1, near, coulomb[None, :])

    came_before = [across(packed_before[h], BITS[h][0]) for h in range(2)]
    picked_before, sent = [None, None], total
    for h in range(2):
        came_h, _ = tie((came_before[h], sent))
        sent = run(
            functools.partial(pick_half_kernel, held, count, h),
            shape((count, 2, half, t) if h else (2 * count * half + LABELS, t), BF16),
            packed_before[h],
            came_h,
            came[1 - h],
            name="pick_half",
        )
        picked_before[h] = across(sent, BITS[h][1])
    near_before, before_each = near_of(packed_before, came_before, picked_before, True)
    behind = [along(x, FORTH) for x in before_each]

    rest_sends, ahead, _ = tie((rest_sends, ahead, near_before))
    rest = [across(rest_sends[h], BITS[h][1]) for h in range(2)]

    stack, _ = tie(((near, near_before), ahead))
    both = run(stack_kernel, shape((2, *slices.shape), BF16), *stack, name="stack")
    total = product(
        functools.partial(step_kernel, 1), 2, ahead, other_core(ahead), total
    )
    total = product(
        functools.partial(second_kernel, -1), 3, near_before, other_core(both), total
    )
    behind[0], _ = tie((behind[0], total))
    parts = shape((chips, transfers, 2, 2, t // n_ga, t), F32)
    part = parts.shape[1:]
    stages = []
    done = total
    for j in range(count):
        total, _ = tie((total, done))
        image = run(
            functools.partial(image_kernel, -2, j),
            shape((transfers, g_local, 2 * t), BF16),
            screened,
            behind[j],
            *[other_core(behind[j][part]) for part in range(2)],
            total,
            scratch=[pltpu.VMEM((2 * g_local, 2 * t), BF16)] * 2,
            name="image",
            mib=24,
        )
        rest, _ = tie((rest, image if j == 0 else done))
        far = run(
            functools.partial(far_kernel, held, j, count),
            shape((transfers, 2, g_local, t), BF16),
            *packed,
            *came,
            *picked,
            *rest,
            name="far",
        )
        keep, *gives = run(
            functools.partial(mirror_kernel, chips),
            [parts] + [shape((chips, 2, t // n_ga, t), BF16)] * (2 * transfers),
            image,
            far,
            name="mirror",
            mib=24,
        )
        own, cross, *sends = run(
            split_kernel,
            [shape(part, F32)] * 2 + ([shape(part, BF16)] * 2 if j else [shape((2, *part), BF16)]),
            keep,
            *[other_core(x) for x in gives],
            name="split",
        )
        done = own
        came_j = [lax.ppermute(x, "ga", [(i, i ^ 2) for i in range(n_ga)]) for x in sends]
        stages.append((own, cross, came_j))
    groups = []
    for own, cross, came_j in stages:
        if groups:
            groups[-1], came_j = tie((groups[-1], came_j))
        own, sends = run(
            merge_kernel, [shape(part, F32), shape(part, BF16)], own, cross, *came_j, name="merge"
        )
        groups += [own, lax.ppermute(sends, "ga", [(i, i ^ 4) for i in range(n_ga)])]
    result = shape((count, transfers, 2, t // n_ga, t), F32)
    return tuple(
        run(
            functools.partial(finish_kernel, count, 2, -1.0 / math.sqrt(g_total)),
            [result] * 2,
            *groups,
            name="finish",
        )
    )


def plain(densities, screened, coulomb, block_rows):
    owner = lax.axis_index("kp")
    g_slot = lax.axis_index("ga")
    k_held = densities.shape[0]
    g_local = densities.shape[2]
    g_total = screened.shape[3]
    rows = block_rows[0]
    transfers = owner * k_held + jnp.arange(k_held, dtype=jnp.int32)
    far_rows = rows[:, None] + transfers[None, :]
    piece = lax.all_gather(densities, "kp", axis=0, tiled=True)
    labels = jnp.arange(piece.shape[0], dtype=jnp.int32)
    pick_near = (rows[:, None] == labels[None, :]).astype(jnp.bfloat16)
    pick_far = (far_rows[:, :, None] == labels[None, None, :]).astype(jnp.bfloat16)
    near_acc = jnp.einsum(
        "jp,pcgt->jcgt", pick_near, piece, preferred_element_type=jnp.float32
    ).astype(jnp.bfloat16)
    far_acc = jnp.einsum(
        "jsp,pcgt->jscgt", pick_far, piece, preferred_element_type=jnp.float32
    ).astype(jnp.bfloat16)
    columns = jnp.arange(g_total, dtype=jnp.int32)
    own_rows = g_slot * g_local + jnp.arange(g_local, dtype=jnp.int32)
    diag_mask = own_rows[:, None] == columns[None, :]
    coulomb_diag = jnp.where(diag_mask, 2.0 * coulomb[:, None], 0.0)
    screen_real = (coulomb_diag[None] - screened[:, 0].astype(jnp.float32)).astype(jnp.bfloat16)
    screen_imag = -screened[:, 1]
    near_all = lax.all_gather(near_acc, "ga", axis=2, tiled=True)
    piece_real = near_all[:, 0]
    piece_imag = near_all[:, 1]
    real_term = jnp.einsum(
        "sgh,jht->jsgt", screen_real, piece_real, preferred_element_type=jnp.float32
    ) - jnp.einsum("sgh,jht->jsgt", screen_imag, piece_imag, preferred_element_type=jnp.float32)
    imag_term = jnp.einsum(
        "sgh,jht->jsgt", screen_real, piece_imag, preferred_element_type=jnp.float32
    ) + jnp.einsum("sgh,jht->jsgt", screen_imag, piece_real, preferred_element_type=jnp.float32)
    image = jnp.stack([real_term, imag_term], 2)
    image = image.astype(jnp.bfloat16)
    image_real = image[:, :, 0]
    image_imag = image[:, :, 1]
    far_real = far_acc[:, :, 0]
    far_imag = far_acc[:, :, 1]
    lower_real = jnp.einsum(
        "jsga,jsgb->jsab", far_real, image_real, preferred_element_type=jnp.float32
    ) + jnp.einsum("jsga,jsgb->jsab", far_imag, image_imag, preferred_element_type=jnp.float32)
    lower_imag = jnp.einsum(
        "jsga,jsgb->jsab", far_real, image_imag, preferred_element_type=jnp.float32
    ) - jnp.einsum("jsga,jsgb->jsab", far_imag, image_real, preferred_element_type=jnp.float32)
    partial_lower = jnp.stack([lower_real, lower_imag], 2)
    inverse = 1.0 / math.sqrt(g_total)
    mirror = lax.psum_scatter(partial_lower, "ga", scatter_dimension=3, tiled=True) * inverse
    partial_upper = jnp.stack([jnp.swapaxes(lower_real, 2, 3), -jnp.swapaxes(lower_imag, 2, 3)], 2)
    kernel = lax.psum_scatter(partial_upper, "ga", scatter_dimension=3, tiled=True) * inverse
    return (kernel, mirror)


def solution(mesh):
    placed = (P("kp", None, "ga", None), P("kp", None, "ga", None), P("ga"), P("kp", None))
    n_kp, n_ga = mesh.shape["kp"], mesh.shape["ga"]

    def shards(densities, screened, coulomb, block_rows):
        g_local, t = densities.shape[2], densities.shape[3]
        fits = n_kp == 2 * 2 and n_ga == 4 * 2
        fits = fits and g_local % 128 == 0 and t % (8 * n_ga) == 0
        fits = fits and n_kp * densities.shape[0] <= 256
        if fits:
            return quick(n_kp, n_ga, densities, screened, coulomb, block_rows)
        return plain(densities, screened, coulomb, block_rows)

    return jax.shard_map(
        shards,
        mesh=mesh,
        in_specs=placed,
        out_specs=(P("kp", None, None, "ga", None), P("kp", None, None, "ga", None)),
        check_vma=False,
    )
```

```python
import functools
import itertools
import math

import jax
import jax.numpy as jnp
from jax import lax
from jax.experimental import pallas as pl
from jax.experimental.pallas import tpu as pltpu
from jax.sharding import PartitionSpec as P

F32 = jnp.float32
BF16 = jnp.bfloat16
LABELS = 16
VMEM = pl.BlockSpec(memory_space=pltpu.VMEM)
SMEM = pl.BlockSpec(memory_space=pltpu.SMEM)
HBM = pl.BlockSpec(memory_space=pltpu.HBM)


def dot(a, b):
    return jnp.dot(a, b, preferred_element_type=F32)


def tdot(a, b):
    return lax.dot_general(a, b, (((0,), (0,)), ((), ())), preferred_element_type=F32)


def run(body, out, *args, specs=None, scratch=(), name=None, aliases=None, mib=16):
    outs = out if isinstance(out, (list, tuple)) else [out]
    result = pl.pallas_call(
        body,
        in_specs=specs or [VMEM] * len(args),
        out_specs=[VMEM] * len(outs),
        out_shape=list(outs),
        scratch_shapes=list(scratch),
        input_output_aliases=aliases or {},
        compiler_params=pltpu.CompilerParams(vmem_limit_bytes=mib * 2**20),
        cost_estimate=pl.CostEstimate(flops=0, bytes_accessed=0, transcendentals=0),
        name=name,
    )(*args)
    return list(result) if isinstance(out, (list, tuple)) else result[0]


BITS = ((1, 2), (2, 1))


def pack_kernel(rows, densities, *sends):
    held, _, g_local, t = densities.shape
    half = g_local // 2
    for h in range(2):
        for k in range(held):
            for part in range(2):
                at = (2 * k + part) * half
                sends[h][at : at + half] = densities[k, part, h * half : (h + 1) * half]
        line = lax.broadcasted_iota(jnp.int32, (LABELS, t), 0)
        tile = jnp.zeros((LABELS, t), F32)
        for j in range(rows.shape[1]):
            tile = jnp.where(line == j, rows[0, j].astype(F32), tile)
        sends[h][2 * held * half :] = tile.astype(BF16)


def label_of(message, held, half, j):
    tail = message[2 * held * half :].astype(F32)
    return jnp.max(tail[j : j + 1]).astype(jnp.int32)


def entries(message, owner, held, half):
    return [(owner * held + k, message, 2 * k * half, (2 * k + 1) * half) for k in range(held)]


def copy_if(label, found, out):
    half = out.shape[1]
    hit = None
    for name, message, real, imag in found:
        match = label == name
        hit = match if hit is None else hit | match

        @pl.when(match)
        def _(message=message, real=real, imag=imag):
            out[0] = message[real : real + half]
            out[1] = message[imag : imag + half]

    return hit


def pick_kernel(held, packed_0, packed_1, came_0, came_1, *sends):
    owner = lax.axis_index("kp")
    packed, came = (packed_0, packed_1), (came_0, came_1)
    half = sends[0].shape[2]
    for j in range(sends[0].shape[0]):
        for h in range(2):
            found = entries(packed[h], owner, held, half)
            found += entries(came[h], owner ^ BITS[h][0], held, half)
            copy_if(label_of(came[1 - h], held, half, j), found, sends[h].at[j])


def pick_half_kernel(held, count, h, packed, came, labels, send):
    owner = lax.axis_index("kp")
    half = (packed.shape[0] - LABELS) // (2 * held)
    found = entries(packed, owner, held, half)
    found += entries(came, owner ^ BITS[h][0], held, half)
    if len(send.shape) == 2:
        send[2 * count * half :] = jnp.zeros((LABELS, send.shape[1]), BF16)
    for j in range(count):
        label = label_of(labels, held, half, j)
        if len(send.shape) == 4:
            copy_if(label, found, send.at[j])
            continue
        for name, message, real, imag in found:

            @pl.when(label == name)
            def _(j=j, message=message, real=real, imag=imag):
                send[2 * j * half : (2 * j + 1) * half] = message[real : real + half]
                send[(2 * j + 1) * half : (2 * j + 2) * half] = message[imag : imag + half]


def near_kernel(held, packed_0, packed_1, came_0, came_1, picked_0, picked_1, near, *each):
    owner = lax.axis_index("kp")
    packed, came, picked = (packed_0, packed_1), (came_0, came_1), (picked_0, picked_1)
    half = picked_1.shape[2]
    for j in range(near.shape[0]):
        label = label_of(packed_0, held, half, j)
        for h in range(2):
            out = near.at[j, :, h * half : (h + 1) * half]
            found = entries(packed[h], owner, held, half)
            found += entries(came[h], owner ^ BITS[h][0], held, half)
            hit = copy_if(label, found, out)

            @pl.when(jnp.logical_not(hit))
            def _(h=h, j=j, out=out):
                if len(picked[h].shape) == 4:
                    out[...] = picked[h][j]
                else:
                    out[0] = picked[h][2 * j * half : (2 * j + 1) * half]
                    out[1] = picked[h][(2 * j + 1) * half : (2 * j + 2) * half]

    for j, out in enumerate(each):
        out[...] = near[j]


def stack_kernel(*refs):
    for i, ref in enumerate(refs[:-1]):
        refs[-1][i] = ref[...]


def left_over(n_kp, held, transfers, count):
    most = []
    for first, second in BITS:
        worst = 0
        for owner in range(n_kp):
            side = {who * held + k for who in (owner ^ second, owner ^ second ^ first) for k in range(held)}
            rows = range(n_kp * held - transfers * (owner + 1) + 1)
            for chosen in itertools.product(rows, repeat=count):
                need = {r + owner * transfers + s for r in chosen for s in range(transfers)}
                worst = max(worst, len((need & side) - set(chosen)))
        most.append(max(worst, 1))
    return most


def slots(labels, rows, owner, transfers):
    found, place = [], jnp.int32(0)
    for label in labels:
        need, sent = jnp.bool_(False), jnp.bool_(False)
        for row in rows:
            first = row + owner * transfers
            need = need | ((label >= first) & (label < first + transfers))
            sent = sent | (label == row)
        need = need & jnp.logical_not(sent)
        found.append((need, place))
        place = place + need.astype(jnp.int32)
    return found


def rest_kernel(held, transfers, count, packed_0, packed_1, came_0, came_1, *sends):
    owner = lax.axis_index("kp")
    packed, came = (packed_0, packed_1), (came_0, came_1)
    for h in range(2):
        first, second = BITS[h]
        room, _, half, _ = sends[h].shape
        found = entries(packed[h], owner, held, half)
        found += entries(came[h], owner ^ first, held, half)
        rows = [label_of(came[1 - h], held, half, j) for j in range(count)]
        places = slots([label for label, *_ in found], rows, owner ^ second, transfers)
        for (_, message, real, imag), (need, place) in zip(found, places):
            for i in range(room):

                @pl.when(need & (place == i))
                def _(h=h, i=i, message=message, real=real, imag=imag, half=half):
                    sends[h][i, 0] = message[real : real + half]
                    sends[h][i, 1] = message[imag : imag + half]


def far_kernel(
    held, j, count, packed_0, packed_1, came_0, came_1, picked_0, picked_1, rest_0, rest_1, far
):
    owner = lax.axis_index("kp")
    packed, came = (packed_0, packed_1), (came_0, came_1)
    picked, rest = (picked_0, picked_1), (rest_0, rest_1)
    transfers, _, g_local, _ = far.shape
    half = g_local // 2
    rows = [label_of(packed_0, held, half, j) for j in range(count)]
    for h in range(2):
        first, second = BITS[h]
        found = entries(packed[h], owner, held, half)
        found += entries(came[h], owner ^ first, held, half)
        side = [
            who * held + k for who in (owner ^ second, owner ^ second ^ first) for k in range(held)
        ]
        places = slots(side, rows, owner, transfers)
        for s in range(transfers):
            label = rows[j] + owner * transfers + s
            out = far.at[s, :, h * half : (h + 1) * half]
            hit = copy_if(label, found, out)
            for i in range(count):
                match = (label == rows[i]) & jnp.logical_not(hit)
                hit = hit | match

                @pl.when(match)
                def _(h=h, i=i, out=out):
                    out[...] = picked[h][i]

            for name, (need, place) in zip(side, places):
                for i in range(rest[h].shape[0]):

                    @pl.when((label == name) & need & (place == i))
                    def _(h=h, i=i, out=out):
                        out[...] = rest[h][i]


def load_kernel(source, panels, sems):
    copies = []
    for s in range(source.shape[0]):
        for part in range(2):
            copy = pltpu.make_async_copy(source.at[s, part], panels.at[s, part], sems.at[2 * s + part])
            copy.start()
            copies.append(copy)
    for copy in copies:
        copy.wait()


FORTH = (1, 3, 0, 2)
BACK = (2, 0, 3, 1)


def chip_at(z, steps):
    if steps == 1:
        return jnp.where(z < 2, 2 * z + 1, 2 * z - 4)
    if steps == -1:
        return jnp.where(lax.rem(z, 2) == 0, 2 + z // 2, z // 2)
    return z if steps == 0 else 3 - z


def lay(terms, upper, lower):
    for ref, first in terms:
        *count, _, g_local, t = ref.shape
        rows = pl.ds(first if isinstance(first, int) else pl.multiple_of(first, 128), g_local)
        for j, panel in enumerate([ref.at[j] for j in range(count[0])] if count else [ref]):
            real, imag = slice(2 * j * t, (2 * j + 1) * t), slice((2 * j + 1) * t, (2 * j + 2) * t)
            upper[rows, real] = panel[0]
            upper[rows, imag] = panel[1]
            lower[rows, real] = -panel[1]
            lower[rows, imag] = panel[0]


def place():
    slot = lax.axis_index("ga")
    return slot // 2, lax.rem(slot, 2)


def multiply(screened, s, span, width, upper, lower, first=0):
    span = pl.ds(pl.multiple_of(span, 128), width)
    rows = slice(first, first + width)
    return dot(screened[s, 0, :, span], upper[rows]) + dot(screened[s, 1, :, span], lower[rows])


def first_kernel(screened, own, coulomb, total, upper, lower):
    z, core = place()
    g = screened.shape[2]
    lay([(own, 0)], upper, lower)
    span = pl.ds(pl.multiple_of((2 * z + core) * g, 128), g)
    line = lax.broadcasted_iota(jnp.int32, (g, g), 0)
    on = line == lax.broadcasted_iota(jnp.int32, (g, g), 1)
    for s in range(screened.shape[0]):
        real = screened[s, 0, :, span]
        real = jnp.where(on, (real.astype(F32) - 2.0 * coulomb[...]).astype(BF16), real)
        total[s] = dot(real, upper[...]) + dot(screened[s, 1, :, span], lower[...])


def step_kernel(steps, screened, own, pair, before, total, upper, lower):
    z, core = place()
    g = screened.shape[2]
    lay([(own, core * g), (pair, (1 - core) * g)], upper, lower)
    span = 2 * chip_at(z, steps) * g
    for s in range(screened.shape[0]):
        total[s] = before[s] + multiply(screened, s, span, 2 * g, upper, lower)


def second_kernel(steps, screened, own, pairs, before, total, upper, lower):
    z, core = place()
    g = screened.shape[2]
    lay([(own, core * g), (pairs.at[1], (1 - core) * g), (pairs.at[0], 2 * g)], upper, lower)
    span = 2 * chip_at(z, steps) * g
    left = (2 * z + 1 - core) * g
    for s in range(screened.shape[0]):
        value = before[s] + multiply(screened, s, span, 2 * g, upper, lower)
        total[s] = value + multiply(screened, s, left, g, upper, lower, 2 * g)


def image_kernel(steps, j, screened, own, pair_real, pair_imag, before, image, upper, lower):
    z, core = place()
    g = screened.shape[2]
    t = own.shape[2]
    lay([(own, core * g)], upper, lower)
    rows = pl.ds(pl.multiple_of((1 - core) * g, 128), g)
    upper[rows, :t] = pair_real[...]
    upper[rows, t:] = pair_imag[...]
    lower[rows, :t] = -pair_imag[...]
    lower[rows, t:] = pair_real[...]
    span = 2 * chip_at(z, steps) * g
    for s in range(screened.shape[0]):
        value = before[s, :, 2 * j * t : 2 * (j + 1) * t]
        image[s] = (value + multiply(screened, s, span, 2 * g, upper, lower)).astype(BF16)


def mirror_kernel(chips, image, far, keep, *gives):
    first = lax.rem(lax.axis_index("ga"), 2) == 0
    t = far.shape[-1]
    for s in range(image.shape[0]):
        by_real, by_imag = tdot(far[s, 0], image[s]), tdot(far[s, 1], image[s])
        real = by_real[:, :t] + by_imag[:, t:]
        imag = by_real[:, t:] - by_imag[:, :t]
        parts = ((real, imag), (real.T, -imag.T))
        for which in range(2):
            for part in range(2):
                block = parts[which][part]
                block = block.reshape(chips, 2, t // (2 * chips), t)
                keep[:, s, which, part] = jnp.where(first, block[:, 0], block[:, 1])
                give = jnp.where(first, block[:, 1], block[:, 0])
                gives[2 * s + which][:, part] = give.astype(BF16)


def split_kernel(near, keep, *refs):
    transfers, _, _, rows, t = keep.shape[1:]
    came, (own, cross, *sends) = refs[: 2 * transfers], refs[2 * transfers :]
    z = lax.axis_index("ga") // 2
    for s in range(transfers):
        for which in range(2):

            def chip(at):
                return keep[at, s, which] + came[2 * s + which][at].astype(F32)

            own[s, which] = chip(z)
            cross[s, which] = chip(z ^ 3 ^ near)
            for i, at in enumerate((z ^ near, z ^ 3)):
                share = chip(at).astype(BF16)
                if len(sends) == 2:
                    sends[i][s, which] = share
                else:
                    first = ((i * transfers + s) * 2 + which) * 2 * rows
                    sends[0][first : first + 2 * rows] = share.reshape(2 * rows, t)
    if len(sends) == 1:
        rest = sends[0].shape[0] - 8 * transfers * rows
        sends[0][8 * transfers * rows :] = jnp.zeros((rest, t), BF16)


def merge_kernel(own, cross, *refs):
    *came, total, sends = refs
    transfers, _, _, rows, t = own.shape
    for s in range(transfers):
        for which in range(2):
            shares = []
            for i in range(2):
                if len(came) == 2:
                    share = came[i][s, which]
                else:
                    first = ((i * transfers + s) * 2 + which) * 2 * rows
                    share = came[0][first : first + 2 * rows].reshape(2, rows, t)
                shares.append(share.astype(F32))
            total[s, which] = own[s, which] + shares[0]
            sends[s, which] = (cross[s, which] + shares[1]).astype(BF16)


def finish_kernel(count, chips, scale, *refs):
    kernel, mirror = refs[-2:]
    for j in range(count):
        terms = refs[j * chips : (j + 1) * chips]
        total = terms[0][...]
        for term in terms[1:]:
            total = total + term[...].astype(F32)
        mirror[j] = total[:, 0] * scale
        kernel[j] = total[:, 1] * scale


def quick(n_kp, n_ga, densities, screened, coulomb, block_rows):
    held, _, g_local, t = densities.shape
    transfers, g_total = screened.shape[0], screened.shape[3]
    count = block_rows.shape[1]
    chips = n_ga // 2
    half = g_local // 2
    shape = jax.ShapeDtypeStruct
    tie = lax.optimization_barrier

    def across(x, bit):
        return lax.ppermute(x, "kp", [(i, i ^ bit) for i in range(n_kp)])

    def other_core(x):
        return lax.ppermute(x, "ga", [(i, i ^ 1) for i in range(n_ga)])

    def along(x, chips_on):
        return lax.ppermute(x, "ga", [(i, 2 * chips_on[i // 2] + i % 2) for i in range(n_ga)])

    message = shape((2 * held * half + LABELS, t), BF16)

    sums = shape((transfers, g_local, 2 * count * t), F32)

    def product(body, terms, *args):
        return run(
            body,
            sums,
            screened,
            *args,
            scratch=[pltpu.VMEM((terms * g_local, 2 * count * t), BF16)] * 2,
            aliases={} if terms == 1 else {3: 0},
            name="product",
            mib=24,
        )

    def pick(packed, came):
        sends = run(
            functools.partial(pick_kernel, held),
            [shape((count, 2, half, t), BF16)] * 2,
            *packed,
            *came,
            name="pick",
        )
        return [across(sends[h], BITS[h][1]) for h in range(2)]

    slices = shape((count, 2, g_local, t), BF16)

    def near_of(packed, came, picked, apart=False):
        kernel = functools.partial(near_kernel, held)
        outs = [slices] + [shape(slices.shape[1:], BF16)] * (count if apart else 0)
        near, *each = run(kernel, outs, *packed, *came, *picked, name="near")
        return (near, each) if apart else near

    packed = run(
        pack_kernel, [message] * 2, block_rows, densities, specs=[SMEM, VMEM], name="pack", mib=53
    )
    packed_before = [along(x, FORTH) for x in packed]
    came = [across(packed[h], BITS[h][0]) for h in range(2)]
    source, packed = tie((screened, packed))
    screened = run(
        load_kernel,
        shape(screened.shape, screened.dtype),
        source,
        specs=[HBM],
        scratch=[pltpu.SemaphoreType.DMA((2 * transfers,))],
        name="load",
        mib=40,
    )
    came, screened = tie((came, screened))
    picked = pick(packed, came)
    rest_sends = run(
        functools.partial(rest_kernel, held, transfers, count),
        [shape((room, 2, half, t), BF16) for room in left_over(n_kp, held, transfers, count)],
        *packed,
        *came,
        name="rest",
    )
    picked = list(tie((picked, (packed_before, rest_sends)))[0])
    near = near_of(packed, came, picked)
    ahead = along(near, BACK)
    total = product(first_kernel, 1, near, coulomb[None, :])

    came_before = [across(packed_before[h], BITS[h][0]) for h in range(2)]
    picked_before, sent = [None, None], total
    for h in range(2):
        came_h, _ = tie((came_before[h], sent))
        sent = run(
            functools.partial(pick_half_kernel, held, count, h),
            shape((count, 2, half, t) if h else (2 * count * half + LABELS, t), BF16),
            packed_before[h],
            came_h,
            came[1 - h],
            name="pick_half",
        )
        picked_before[h] = across(sent, BITS[h][1])
    near_before, before_each = near_of(packed_before, came_before, picked_before, True)
    behind = [along(x, FORTH) for x in before_each]

    rest_sends, ahead, _ = tie((rest_sends, ahead, near_before))
    rest = [across(rest_sends[h], BITS[h][1]) for h in range(2)]

    stack, _ = tie(((near, near_before), ahead))
    both = run(stack_kernel, shape((2, *slices.shape), BF16), *stack, name="stack")
    total = product(
        functools.partial(step_kernel, 1), 2, ahead, other_core(ahead), total
    )
    total = product(
        functools.partial(second_kernel, -1), 3, near_before, other_core(both), total
    )
    behind[0], _ = tie((behind[0], total))
    parts = shape((chips, transfers, 2, 2, t // n_ga, t), F32)
    part = parts.shape[1:]
    stages = []
    done = total
    for j in range(count):
        total, _ = tie((total, done))
        image = run(
            functools.partial(image_kernel, -2, j),
            shape((transfers, g_local, 2 * t), BF16),
            screened,
            behind[j],
            *[other_core(behind[j][part]) for part in range(2)],
            total,
            scratch=[pltpu.VMEM((2 * g_local, 2 * t), BF16)] * 2,
            name="image",
            mib=24,
        )
        rest, _ = tie((rest, image if j == 0 else done))
        far = run(
            functools.partial(far_kernel, held, j, count),
            shape((transfers, 2, g_local, t), BF16),
            *packed,
            *came,
            *picked,
            *rest,
            name="far",
        )
        keep, *gives = run(
            functools.partial(mirror_kernel, chips),
            [parts] + [shape((chips, 2, t // n_ga, t), BF16)] * (2 * transfers),
            image,
            far,
            name="mirror",
            mib=24,
        )
        near_z = 1 if j % 2 else 2
        own, cross, *sends = run(
            functools.partial(split_kernel, near_z),
            [shape(part, F32)] * 2 + ([shape(part, BF16)] * 2 if j else [shape((8 * transfers * part[3] + 16, t), BF16)]),
            keep,
            *[other_core(x) for x in gives],
            name="split",
        )
        done = own
        came_j = [lax.ppermute(x, "ga", [(i, i ^ (2 * near_z)) for i in range(n_ga)]) for x in sends]
        stages.append((own, cross, came_j, 3 - near_z))
    groups = []
    for own, cross, came_j, far_z in stages:
        if groups:
            came_j, _ = tie((came_j, sends))
        own, sends = run(
            merge_kernel, [shape(part, F32), shape(part, BF16)], own, cross, *came_j, name="merge"
        )
        groups += [own, lax.ppermute(sends, "ga", [(i, i ^ (2 * far_z)) for i in range(n_ga)])]
    result = shape((count, transfers, 2, t // n_ga, t), F32)
    return tuple(
        run(
            functools.partial(finish_kernel, count, 2, -1.0 / math.sqrt(g_total)),
            [result] * 2,
            *groups,
            name="finish",
        )
    )


def plain(densities, screened, coulomb, block_rows):
    owner = lax.axis_index("kp")
    g_slot = lax.axis_index("ga")
    k_held = densities.shape[0]
    g_local = densities.shape[2]
    g_total = screened.shape[3]
    rows = block_rows[0]
    transfers = owner * k_held + jnp.arange(k_held, dtype=jnp.int32)
    far_rows = rows[:, None] + transfers[None, :]
    piece = lax.all_gather(densities, "kp", axis=0, tiled=True)
    labels = jnp.arange(piece.shape[0], dtype=jnp.int32)
    pick_near = (rows[:, None] == labels[None, :]).astype(jnp.bfloat16)
    pick_far = (far_rows[:, :, None] == labels[None, None, :]).astype(jnp.bfloat16)
    near_acc = jnp.einsum(
        "jp,pcgt->jcgt", pick_near, piece, preferred_element_type=jnp.float32
    ).astype(jnp.bfloat16)
    far_acc = jnp.einsum(
        "jsp,pcgt->jscgt", pick_far, piece, preferred_element_type=jnp.float32
    ).astype(jnp.bfloat16)
    columns = jnp.arange(g_total, dtype=jnp.int32)
    own_rows = g_slot * g_local + jnp.arange(g_local, dtype=jnp.int32)
    diag_mask = own_rows[:, None] == columns[None, :]
    coulomb_diag = jnp.where(diag_mask, 2.0 * coulomb[:, None], 0.0)
    screen_real = (coulomb_diag[None] - screened[:, 0].astype(jnp.float32)).astype(jnp.bfloat16)
    screen_imag = -screened[:, 1]
    near_all = lax.all_gather(near_acc, "ga", axis=2, tiled=True)
    piece_real = near_all[:, 0]
    piece_imag = near_all[:, 1]
    real_term = jnp.einsum(
        "sgh,jht->jsgt", screen_real, piece_real, preferred_element_type=jnp.float32
    ) - jnp.einsum("sgh,jht->jsgt", screen_imag, piece_imag, preferred_element_type=jnp.float32)
    imag_term = jnp.einsum(
        "sgh,jht->jsgt", screen_real, piece_imag, preferred_element_type=jnp.float32
    ) + jnp.einsum("sgh,jht->jsgt", screen_imag, piece_real, preferred_element_type=jnp.float32)
    image = jnp.stack([real_term, imag_term], 2)
    image = image.astype(jnp.bfloat16)
    image_real = image[:, :, 0]
    image_imag = image[:, :, 1]
    far_real = far_acc[:, :, 0]
    far_imag = far_acc[:, :, 1]
    lower_real = jnp.einsum(
        "jsga,jsgb->jsab", far_real, image_real, preferred_element_type=jnp.float32
    ) + jnp.einsum("jsga,jsgb->jsab", far_imag, image_imag, preferred_element_type=jnp.float32)
    lower_imag = jnp.einsum(
        "jsga,jsgb->jsab", far_real, image_imag, preferred_element_type=jnp.float32
    ) - jnp.einsum("jsga,jsgb->jsab", far_imag, image_real, preferred_element_type=jnp.float32)
    partial_lower = jnp.stack([lower_real, lower_imag], 2)
    inverse = 1.0 / math.sqrt(g_total)
    mirror = lax.psum_scatter(partial_lower, "ga", scatter_dimension=3, tiled=True) * inverse
    partial_upper = jnp.stack([jnp.swapaxes(lower_real, 2, 3), -jnp.swapaxes(lower_imag, 2, 3)], 2)
    kernel = lax.psum_scatter(partial_upper, "ga", scatter_dimension=3, tiled=True) * inverse
    return (kernel, mirror)


def solution(mesh):
    placed = (P("kp", None, "ga", None), P("kp", None, "ga", None), P("ga"), P("kp", None))
    n_kp, n_ga = mesh.shape["kp"], mesh.shape["ga"]

    def shards(densities, screened, coulomb, block_rows):
        g_local, t = densities.shape[2], densities.shape[3]
        fits = n_kp == 2 * 2 and n_ga == 4 * 2
        fits = fits and g_local % 128 == 0 and t % (8 * n_ga) == 0
        fits = fits and n_kp * densities.shape[0] <= 256
        if fits:
            return quick(n_kp, n_ga, densities, screened, coulomb, block_rows)
        return plain(densities, screened, coulomb, block_rows)

    return jax.shard_map(
        shards,
        mesh=mesh,
        in_specs=placed,
        out_specs=(P("kp", None, None, "ga", None), P("kp", None, None, "ga", None)),
        check_vma=False,
    )
```

```python
import functools
import itertools
import math

import jax
import jax.numpy as jnp
from jax import lax
from jax.experimental import pallas as pl
from jax.experimental.pallas import tpu as pltpu
from jax.sharding import PartitionSpec as P

F32 = jnp.float32
BF16 = jnp.bfloat16
LABELS = 16
VMEM = pl.BlockSpec(memory_space=pltpu.VMEM)
SMEM = pl.BlockSpec(memory_space=pltpu.SMEM)
HBM = pl.BlockSpec(memory_space=pltpu.HBM)


def dot(a, b):
    return jnp.dot(a, b, preferred_element_type=F32)


def tdot(a, b):
    return lax.dot_general(a, b, (((0,), (0,)), ((), ())), preferred_element_type=F32)


def run(body, out, *args, specs=None, scratch=(), name=None, aliases=None, mib=16):
    outs = out if isinstance(out, (list, tuple)) else [out]
    result = pl.pallas_call(
        body,
        in_specs=specs or [VMEM] * len(args),
        out_specs=[VMEM] * len(outs),
        out_shape=list(outs),
        scratch_shapes=list(scratch),
        input_output_aliases=aliases or {},
        compiler_params=pltpu.CompilerParams(vmem_limit_bytes=mib * 2**20),
        cost_estimate=pl.CostEstimate(flops=0, bytes_accessed=0, transcendentals=0),
        name=name,
    )(*args)
    return list(result) if isinstance(out, (list, tuple)) else result[0]


BITS = ((1, 2), (2, 1))


def pack_kernel(rows, densities, *sends):
    held, _, g_local, t = densities.shape
    half = g_local // 2
    for h in range(2):
        for k in range(held):
            for part in range(2):
                at = (2 * k + part) * half
                sends[h][at : at + half] = densities[k, part, h * half : (h + 1) * half]
        line = lax.broadcasted_iota(jnp.int32, (LABELS, t), 0)
        tile = jnp.zeros((LABELS, t), F32)
        for j in range(rows.shape[1]):
            tile = jnp.where(line == j, rows[0, j].astype(F32), tile)
        sends[h][2 * held * half :] = tile.astype(BF16)


def label_of(message, held, half, j):
    tail = message[2 * held * half :].astype(F32)
    return jnp.max(tail[j : j + 1]).astype(jnp.int32)


def entries(message, owner, held, half):
    return [(owner * held + k, message, 2 * k * half, (2 * k + 1) * half) for k in range(held)]


def copy_if(label, found, out):
    half = out.shape[1]
    hit = None
    for name, message, real, imag in found:
        match = label == name
        hit = match if hit is None else hit | match

        @pl.when(match)
        def _(message=message, real=real, imag=imag):
            out[0] = message[real : real + half]
            out[1] = message[imag : imag + half]

    return hit


def pick_kernel(held, packed_0, packed_1, came_0, came_1, *sends):
    owner = lax.axis_index("kp")
    packed, came = (packed_0, packed_1), (came_0, came_1)
    half = sends[0].shape[2]
    for j in range(sends[0].shape[0]):
        for h in range(2):
            found = entries(packed[h], owner, held, half)
            found += entries(came[h], owner ^ BITS[h][0], held, half)
            copy_if(label_of(came[1 - h], held, half, j), found, sends[h].at[j])


def pick_half_kernel(held, count, h, packed, came, labels, send):
    owner = lax.axis_index("kp")
    half = (packed.shape[0] - LABELS) // (2 * held)
    found = entries(packed, owner, held, half)
    found += entries(came, owner ^ BITS[h][0], held, half)
    if len(send.shape) == 2:
        send[2 * count * half :] = jnp.zeros((LABELS, send.shape[1]), BF16)
    for j in range(count):
        label = label_of(labels, held, half, j)
        if len(send.shape) == 4:
            copy_if(label, found, send.at[j])
            continue
        for name, message, real, imag in found:

            @pl.when(label == name)
            def _(j=j, message=message, real=real, imag=imag):
                send[2 * j * half : (2 * j + 1) * half] = message[real : real + half]
                send[(2 * j + 1) * half : (2 * j + 2) * half] = message[imag : imag + half]


def near_kernel(held, packed_0, packed_1, came_0, came_1, picked_0, picked_1, near, *each):
    owner = lax.axis_index("kp")
    packed, came, picked = (packed_0, packed_1), (came_0, came_1), (picked_0, picked_1)
    half = picked_1.shape[2]
    for j in range(near.shape[0]):
        label = label_of(packed_0, held, half, j)
        for h in range(2):
            out = near.at[j, :, h * half : (h + 1) * half]
            found = entries(packed[h], owner, held, half)
            found += entries(came[h], owner ^ BITS[h][0], held, half)
            hit = copy_if(label, found, out)

            @pl.when(jnp.logical_not(hit))
            def _(h=h, j=j, out=out):
                if len(picked[h].shape) == 4:
                    out[...] = picked[h][j]
                else:
                    out[0] = picked[h][2 * j * half : (2 * j + 1) * half]
                    out[1] = picked[h][(2 * j + 1) * half : (2 * j + 2) * half]

    for j, out in enumerate(each):
        out[...] = near[j]


def stack_kernel(*refs):
    for i, ref in enumerate(refs[:-1]):
        refs[-1][i] = ref[...]


def left_over(n_kp, held, transfers, count):
    most = []
    for first, second in BITS:
        worst = 0
        for owner in range(n_kp):
            side = {who * held + k for who in (owner ^ second, owner ^ second ^ first) for k in range(held)}
            rows = range(n_kp * held - transfers * (owner + 1) + 1)
            for chosen in itertools.product(rows, repeat=count):
                need = {r + owner * transfers + s for r in chosen for s in range(transfers)}
                worst = max(worst, len((need & side) - set(chosen)))
        most.append(max(worst, 1))
    return most


def slots(labels, rows, owner, transfers):
    found, place = [], jnp.int32(0)
    for label in labels:
        need, sent = jnp.bool_(False), jnp.bool_(False)
        for row in rows:
            first = row + owner * transfers
            need = need | ((label >= first) & (label < first + transfers))
            sent = sent | (label == row)
        need = need & jnp.logical_not(sent)
        found.append((need, place))
        place = place + need.astype(jnp.int32)
    return found


def rest_kernel(held, transfers, count, packed_0, packed_1, came_0, came_1, *sends):
    owner = lax.axis_index("kp")
    packed, came = (packed_0, packed_1), (came_0, came_1)
    for h in range(2):
        first, second = BITS[h]
        room, _, half, _ = sends[h].shape
        found = entries(packed[h], owner, held, half)
        found += entries(came[h], owner ^ first, held, half)
        rows = [label_of(came[1 - h], held, half, j) for j in range(count)]
        places = slots([label for label, *_ in found], rows, owner ^ second, transfers)
        for (_, message, real, imag), (need, place) in zip(found, places):
            for i in range(room):

                @pl.when(need & (place == i))
                def _(h=h, i=i, message=message, real=real, imag=imag, half=half):
                    sends[h][i, 0] = message[real : real + half]
                    sends[h][i, 1] = message[imag : imag + half]


def far_kernel(
    held, j, count, packed_0, packed_1, came_0, came_1, picked_0, picked_1, rest_0, rest_1, far
):
    owner = lax.axis_index("kp")
    packed, came = (packed_0, packed_1), (came_0, came_1)
    picked, rest = (picked_0, picked_1), (rest_0, rest_1)
    transfers, _, g_local, _ = far.shape
    half = g_local // 2
    rows = [label_of(packed_0, held, half, j) for j in range(count)]
    for h in range(2):
        first, second = BITS[h]
        found = entries(packed[h], owner, held, half)
        found += entries(came[h], owner ^ first, held, half)
        side = [
            who * held + k for who in (owner ^ second, owner ^ second ^ first) for k in range(held)
        ]
        places = slots(side, rows, owner, transfers)
        for s in range(transfers):
            label = rows[j] + owner * transfers + s
            out = far.at[s, :, h * half : (h + 1) * half]
            hit = copy_if(label, found, out)
            for i in range(count):
                match = (label == rows[i]) & jnp.logical_not(hit)
                hit = hit | match

                @pl.when(match)
                def _(h=h, i=i, out=out):
                    out[...] = picked[h][i]

            for name, (need, place) in zip(side, places):
                for i in range(rest[h].shape[0]):

                    @pl.when((label == name) & need & (place == i))
                    def _(h=h, i=i, out=out):
                        out[...] = rest[h][i]


def load_kernel(source, panels, sems):
    copies = []
    for s in range(source.shape[0]):
        for part in range(2):
            copy = pltpu.make_async_copy(source.at[s, part], panels.at[s, part], sems.at[2 * s + part])
            copy.start()
            copies.append(copy)
    for copy in copies:
        copy.wait()


FORTH = (1, 3, 0, 2)
BACK = (2, 0, 3, 1)


def chip_at(z, steps):
    if steps == 1:
        return jnp.where(z < 2, 2 * z + 1, 2 * z - 4)
    if steps == -1:
        return jnp.where(lax.rem(z, 2) == 0, 2 + z // 2, z // 2)
    return z if steps == 0 else 3 - z


def lay(terms, near):
    for ref, first in terms:
        *count, _, g_local, t = ref.shape
        rows = pl.ds(first if isinstance(first, int) else pl.multiple_of(first, 128), g_local)
        for j, panel in enumerate([ref.at[j] for j in range(count[0])] if count else [ref]):
            near[rows, 2 * j * t : (2 * j + 1) * t] = panel[0]
            near[rows, (2 * j + 1) * t : (2 * j + 2) * t] = panel[1]


def place():
    slot = lax.axis_index("ga")
    return slot // 2, lax.rem(slot, 2)


def combine(by_real, by_imag, t):
    parts = []
    for real in range(0, by_real.shape[1], 2 * t):
        imag = real + t
        parts.append(by_real[:, real:imag] - by_imag[:, imag : imag + t])
        parts.append(by_real[:, imag : imag + t] + by_imag[:, real:imag])
    return jnp.concatenate(parts, axis=1)


def multiply(screened, s, span, width, near, t, first=0):
    span = pl.ds(pl.multiple_of(span, 128), width)
    rows = slice(first, first + width)
    by_real, by_imag = dot(screened[s, 0, :, span], near[rows]), dot(screened[s, 1, :, span], near[rows])
    return combine(by_real, by_imag, t)


def first_kernel(screened, own, coulomb, total, near):
    z, core = place()
    g, t = own.shape[2:]
    lay([(own, 0)], near)
    span = pl.ds(pl.multiple_of((2 * z + core) * g, 128), g)
    line = lax.broadcasted_iota(jnp.int32, (g, g), 0)
    on = line == lax.broadcasted_iota(jnp.int32, (g, g), 1)
    for s in range(screened.shape[0]):
        real = screened[s, 0, :, span]
        real = jnp.where(on, (real.astype(F32) - 2.0 * coulomb[...]).astype(BF16), real)
        total[s] = combine(dot(real, near[...]), dot(screened[s, 1, :, span], near[...]), t)


def step_kernel(steps, screened, own, pair, before, total, near):
    z, core = place()
    g, t = own.shape[2:]
    lay([(own, core * g), (pair, (1 - core) * g)], near)
    span = 2 * chip_at(z, steps) * g
    for s in range(screened.shape[0]):
        total[s] = before[s] + multiply(screened, s, span, 2 * g, near, t)


def second_kernel(steps, screened, own, pairs, before, total, near):
    z, core = place()
    g, t = own.shape[2:]
    lay([(own, core * g), (pairs.at[1], (1 - core) * g), (pairs.at[0], 2 * g)], near)
    span = 2 * chip_at(z, steps) * g
    left = (2 * z + 1 - core) * g
    for s in range(screened.shape[0]):
        value = before[s] + multiply(screened, s, span, 2 * g, near, t)
        total[s] = value + multiply(screened, s, left, g, near, t, 2 * g)


def image_kernel(steps, j, screened, own, pair_real, pair_imag, before, image, near):
    z, core = place()
    g = screened.shape[2]
    t = own.shape[2]
    lay([(own, core * g)], near)
    rows = pl.ds(pl.multiple_of((1 - core) * g, 128), g)
    near[rows, :t] = pair_real[...]
    near[rows, t:] = pair_imag[...]
    span = 2 * chip_at(z, steps) * g
    for s in range(screened.shape[0]):
        value = before[s, :, 2 * j * t : 2 * (j + 1) * t]
        image[s] = (value + multiply(screened, s, span, 2 * g, near, t)).astype(BF16)


def mirror_kernel(chips, image, far, keep, *gives):
    first = lax.rem(lax.axis_index("ga"), 2) == 0
    t = far.shape[-1]
    for s in range(image.shape[0]):
        by_real, by_imag = tdot(far[s, 0], image[s]), tdot(far[s, 1], image[s])
        real = by_real[:, :t] + by_imag[:, t:]
        imag = by_real[:, t:] - by_imag[:, :t]
        parts = ((real, imag), (real.T, -imag.T))
        for which in range(2):
            for part in range(2):
                block = parts[which][part]
                block = block.reshape(chips, 2, t // (2 * chips), t)
                keep[:, s, which, part] = jnp.where(first, block[:, 0], block[:, 1])
                give = jnp.where(first, block[:, 1], block[:, 0])
                gives[2 * s + which][:, part] = give.astype(BF16)


def split_kernel(keep, *refs):
    *came, own, cross, sends = refs
    z = lax.axis_index("ga") // 2
    for s in range(keep.shape[1]):
        for which in range(2):

            def chip(at):
                return keep[at, s, which] + came[2 * s + which][at].astype(F32)

            own[s, which] = chip(z)
            cross[s, which] = chip(z ^ 2)
            for i, at in enumerate((z ^ 1, z ^ 3)):
                sends[i, s, which] = chip(at).astype(BF16)


def merge_kernel(own, cross, came, total, sends):
    total[...] = own[...] + came[0].astype(F32)
    sends[...] = (cross[...] + came[1].astype(F32)).astype(BF16)


def finish_kernel(count, chips, scale, *refs):
    kernel, mirror = refs[-2:]
    for j in range(count):
        terms = refs[j * chips : (j + 1) * chips]
        total = terms[0][...]
        for term in terms[1:]:
            total = total + term[...].astype(F32)
        mirror[j] = total[:, 0] * scale
        kernel[j] = total[:, 1] * scale


def quick(n_kp, n_ga, densities, screened, coulomb, block_rows):
    held, _, g_local, t = densities.shape
    transfers, g_total = screened.shape[0], screened.shape[3]
    count = block_rows.shape[1]
    chips = n_ga // 2
    half = g_local // 2
    shape = jax.ShapeDtypeStruct
    tie = lax.optimization_barrier

    def across(x, bit):
        return lax.ppermute(x, "kp", [(i, i ^ bit) for i in range(n_kp)])

    def other_core(x):
        return lax.ppermute(x, "ga", [(i, i ^ 1) for i in range(n_ga)])

    def along(x, chips_on):
        return lax.ppermute(x, "ga", [(i, 2 * chips_on[i // 2] + i % 2) for i in range(n_ga)])

    message = shape((2 * held * half + LABELS, t), BF16)

    sums = shape((transfers, g_local, 2 * count * t), F32)

    def product(body, terms, *args):
        return run(
            body,
            sums,
            screened,
            *args,
            scratch=[pltpu.VMEM((terms * g_local, 2 * count * t), BF16)],
            aliases={} if terms == 1 else {3: 0},
            name="product",
            mib=24,
        )

    def pick(packed, came):
        sends = run(
            functools.partial(pick_kernel, held),
            [shape((count, 2, half, t), BF16)] * 2,
            *packed,
            *came,
            name="pick",
        )
        return [across(sends[h], BITS[h][1]) for h in range(2)]

    slices = shape((count, 2, g_local, t), BF16)

    def near_of(packed, came, picked, apart=False):
        kernel = functools.partial(near_kernel, held)
        outs = [slices] + [shape(slices.shape[1:], BF16)] * (count if apart else 0)
        near, *each = run(kernel, outs, *packed, *came, *picked, name="near")
        return (near, each) if apart else near

    packed = run(
        pack_kernel, [message] * 2, block_rows, densities, specs=[SMEM, VMEM], name="pack", mib=53
    )
    packed_before = [along(x, FORTH) for x in packed]
    came = [across(packed[h], BITS[h][0]) for h in range(2)]
    source, packed = tie((screened, packed))
    screened = run(
        load_kernel,
        shape(screened.shape, screened.dtype),
        source,
        specs=[HBM],
        scratch=[pltpu.SemaphoreType.DMA((2 * transfers,))],
        name="load",
        mib=40,
    )
    came, screened = tie((came, screened))
    picked = pick(packed, came)
    rest_sends = run(
        functools.partial(rest_kernel, held, transfers, count),
        [shape((room, 2, half, t), BF16) for room in left_over(n_kp, held, transfers, count)],
        *packed,
        *came,
        name="rest",
    )
    picked = list(tie((picked, (packed_before, rest_sends)))[0])
    near = near_of(packed, came, picked)
    ahead = along(near, BACK)
    total = product(first_kernel, 1, near, coulomb[None, :])

    came_before = [across(packed_before[h], BITS[h][0]) for h in range(2)]
    picked_before, sent = [None, None], total
    for h in range(2):
        came_h, _ = tie((came_before[h], sent))
        sent = run(
            functools.partial(pick_half_kernel, held, count, h),
            shape((count, 2, half, t) if h else (2 * count * half + LABELS, t), BF16),
            packed_before[h],
            came_h,
            came[1 - h],
            name="pick_half",
        )
        picked_before[h] = across(sent, BITS[h][1])
    near_before, before_each = near_of(packed_before, came_before, picked_before, True)
    behind = [along(x, FORTH) for x in before_each]

    rest_sends, ahead, _ = tie((rest_sends, ahead, near_before))
    rest = [across(rest_sends[h], BITS[h][1]) for h in range(2)]

    stack, _ = tie(((near, near_before), ahead))
    both = run(stack_kernel, shape((2, *slices.shape), BF16), *stack, name="stack")
    total = product(
        functools.partial(step_kernel, 1), 2, ahead, other_core(ahead), total
    )
    total = product(
        functools.partial(second_kernel, -1), 3, near_before, other_core(both), total
    )
    behind[0], _ = tie((behind[0], total))
    parts = shape((chips, transfers, 2, 2, t // n_ga, t), F32)
    part = parts.shape[1:]
    stages = []
    done = total
    for j in range(count):
        total, _ = tie((total, done))
        image = run(
            functools.partial(image_kernel, -2, j),
            shape((transfers, g_local, 2 * t), BF16),
            screened,
            behind[j],
            *[other_core(behind[j][part]) for part in range(2)],
            total,
            scratch=[pltpu.VMEM((2 * g_local, 2 * t), BF16)],
            name="image",
            mib=24,
        )
        rest, _ = tie((rest, image if j == 0 else done))
        far = run(
            functools.partial(far_kernel, held, j, count),
            shape((transfers, 2, g_local, t), BF16),
            *packed,
            *came,
            *picked,
            *rest,
            name="far",
        )
        keep, *gives = run(
            functools.partial(mirror_kernel, chips),
            [parts] + [shape((chips, 2, t // n_ga, t), BF16)] * (2 * transfers),
            image,
            far,
            name="mirror",
            mib=24,
        )
        own, cross, sends = run(
            split_kernel,
            [shape(part, F32), shape(part, F32), shape((2, *part), BF16)],
            keep,
            *[other_core(x) for x in gives],
            name="split",
        )
        if j + 1 < count:
            behind[j + 1], _ = tie((behind[j + 1], keep))
        if stages:
            sends, _ = tie((sends, stages[-1][2]))
        done = own
        came_j = lax.ppermute(sends, "ga", [(i, i ^ 2) for i in range(n_ga)])
        stages.append((own, cross, came_j))
    groups = []
    for own, cross, came_j in stages:
        own, sends = run(
            merge_kernel, [shape(part, F32), shape(part, BF16)], own, cross, came_j, name="merge"
        )
        groups += [own, lax.ppermute(sends, "ga", [(i, i ^ 4) for i in range(n_ga)])]
    result = shape((count, transfers, 2, t // n_ga, t), F32)
    return tuple(
        run(
            functools.partial(finish_kernel, count, 2, -1.0 / math.sqrt(g_total)),
            [result] * 2,
            *groups,
            name="finish",
        )
    )


def plain(densities, screened, coulomb, block_rows):
    owner = lax.axis_index("kp")
    g_slot = lax.axis_index("ga")
    k_held = densities.shape[0]
    g_local = densities.shape[2]
    g_total = screened.shape[3]
    rows = block_rows[0]
    transfers = owner * k_held + jnp.arange(k_held, dtype=jnp.int32)
    far_rows = rows[:, None] + transfers[None, :]
    piece = lax.all_gather(densities, "kp", axis=0, tiled=True)
    labels = jnp.arange(piece.shape[0], dtype=jnp.int32)
    pick_near = (rows[:, None] == labels[None, :]).astype(jnp.bfloat16)
    pick_far = (far_rows[:, :, None] == labels[None, None, :]).astype(jnp.bfloat16)
    near_acc = jnp.einsum(
        "jp,pcgt->jcgt", pick_near, piece, preferred_element_type=jnp.float32
    ).astype(jnp.bfloat16)
    far_acc = jnp.einsum(
        "jsp,pcgt->jscgt", pick_far, piece, preferred_element_type=jnp.float32
    ).astype(jnp.bfloat16)
    columns = jnp.arange(g_total, dtype=jnp.int32)
    own_rows = g_slot * g_local + jnp.arange(g_local, dtype=jnp.int32)
    diag_mask = own_rows[:, None] == columns[None, :]
    coulomb_diag = jnp.where(diag_mask, 2.0 * coulomb[:, None], 0.0)
    screen_real = (coulomb_diag[None] - screened[:, 0].astype(jnp.float32)).astype(jnp.bfloat16)
    screen_imag = -screened[:, 1]
    near_all = lax.all_gather(near_acc, "ga", axis=2, tiled=True)
    piece_real = near_all[:, 0]
    piece_imag = near_all[:, 1]
    real_term = jnp.einsum(
        "sgh,jht->jsgt", screen_real, piece_real, preferred_element_type=jnp.float32
    ) - jnp.einsum("sgh,jht->jsgt", screen_imag, piece_imag, preferred_element_type=jnp.float32)
    imag_term = jnp.einsum(
        "sgh,jht->jsgt", screen_real, piece_imag, preferred_element_type=jnp.float32
    ) + jnp.einsum("sgh,jht->jsgt", screen_imag, piece_real, preferred_element_type=jnp.float32)
    image = jnp.stack([real_term, imag_term], 2)
    image = image.astype(jnp.bfloat16)
    image_real = image[:, :, 0]
    image_imag = image[:, :, 1]
    far_real = far_acc[:, :, 0]
    far_imag = far_acc[:, :, 1]
    lower_real = jnp.einsum(
        "jsga,jsgb->jsab", far_real, image_real, preferred_element_type=jnp.float32
    ) + jnp.einsum("jsga,jsgb->jsab", far_imag, image_imag, preferred_element_type=jnp.float32)
    lower_imag = jnp.einsum(
        "jsga,jsgb->jsab", far_real, image_imag, preferred_element_type=jnp.float32
    ) - jnp.einsum("jsga,jsgb->jsab", far_imag, image_real, preferred_element_type=jnp.float32)
    partial_lower = jnp.stack([lower_real, lower_imag], 2)
    inverse = 1.0 / math.sqrt(g_total)
    mirror = lax.psum_scatter(partial_lower, "ga", scatter_dimension=3, tiled=True) * inverse
    partial_upper = jnp.stack([jnp.swapaxes(lower_real, 2, 3), -jnp.swapaxes(lower_imag, 2, 3)], 2)
    kernel = lax.psum_scatter(partial_upper, "ga", scatter_dimension=3, tiled=True) * inverse
    return (kernel, mirror)


def solution(mesh):
    placed = (P("kp", None, "ga", None), P("kp", None, "ga", None), P("ga"), P("kp", None))
    n_kp, n_ga = mesh.shape["kp"], mesh.shape["ga"]

    def shards(densities, screened, coulomb, block_rows):
        g_local, t = densities.shape[2], densities.shape[3]
        fits = n_kp == 2 * 2 and n_ga == 4 * 2
        fits = fits and g_local % 128 == 0 and t % (8 * n_ga) == 0
        fits = fits and n_kp * densities.shape[0] <= 256
        if fits:
            return quick(n_kp, n_ga, densities, screened, coulomb, block_rows)
        return plain(densities, screened, coulomb, block_rows)

    return jax.shard_map(
        shards,
        mesh=mesh,
        in_specs=placed,
        out_specs=(P("kp", None, None, "ga", None), P("kp", None, None, "ga", None)),
        check_vma=False,
    )
```

```python
import functools
import itertools
import math

import jax
import jax.numpy as jnp
from jax import lax
from jax.experimental import pallas as pl
from jax.experimental.pallas import tpu as pltpu
from jax.sharding import PartitionSpec as P

F32 = jnp.float32
BF16 = jnp.bfloat16
LABELS = 16
VMEM = pl.BlockSpec(memory_space=pltpu.VMEM)
SMEM = pl.BlockSpec(memory_space=pltpu.SMEM)
HBM = pl.BlockSpec(memory_space=pltpu.HBM)


def dot(a, b):
    return jnp.dot(a, b, preferred_element_type=F32)


def tdot(a, b):
    return lax.dot_general(a, b, (((0,), (0,)), ((), ())), preferred_element_type=F32)


def run(body, out, *args, specs=None, scratch=(), name=None, aliases=None, mib=16):
    outs = out if isinstance(out, (list, tuple)) else [out]
    result = pl.pallas_call(
        body,
        in_specs=specs or [VMEM] * len(args),
        out_specs=[VMEM] * len(outs),
        out_shape=list(outs),
        scratch_shapes=list(scratch),
        input_output_aliases=aliases or {},
        compiler_params=pltpu.CompilerParams(vmem_limit_bytes=mib * 2**20),
        cost_estimate=pl.CostEstimate(flops=0, bytes_accessed=0, transcendentals=0),
        name=name,
    )(*args)
    return list(result) if isinstance(out, (list, tuple)) else result[0]


BITS = ((1, 2), (2, 1))


def pack_kernel(rows, densities, *sends):
    held, _, g_local, t = densities.shape
    half = g_local // 2
    for h in range(2):
        for k in range(held):
            for part in range(2):
                at = (2 * k + part) * half
                sends[h][at : at + half] = densities[k, part, h * half : (h + 1) * half]
        line = lax.broadcasted_iota(jnp.int32, (LABELS, t), 0)
        tile = jnp.zeros((LABELS, t), F32)
        for j in range(rows.shape[1]):
            tile = jnp.where(line == j, rows[0, j].astype(F32), tile)
        sends[h][2 * held * half :] = tile.astype(BF16)


def label_of(message, held, half, j):
    tail = message[2 * held * half :].astype(F32)
    return jnp.max(tail[j : j + 1]).astype(jnp.int32)


def entries(message, owner, held, half):
    return [(owner * held + k, message, 2 * k * half, (2 * k + 1) * half) for k in range(held)]


def copy_if(label, found, out):
    half = out.shape[1]
    hit = None
    for name, message, real, imag in found:
        match = label == name
        hit = match if hit is None else hit | match

        @pl.when(match)
        def _(message=message, real=real, imag=imag):
            out[0] = message[real : real + half]
            out[1] = message[imag : imag + half]

    return hit


def pick_kernel(held, packed_0, packed_1, came_0, came_1, *sends):
    owner = lax.axis_index("kp")
    packed, came = (packed_0, packed_1), (came_0, came_1)
    half = sends[0].shape[2]
    for j in range(sends[0].shape[0]):
        for h in range(2):
            found = entries(packed[h], owner, held, half)
            found += entries(came[h], owner ^ BITS[h][0], held, half)
            copy_if(label_of(came[1 - h], held, half, j), found, sends[h].at[j])


def pick_half_kernel(held, count, h, packed, came, labels, send):
    owner = lax.axis_index("kp")
    half = (packed.shape[0] - LABELS) // (2 * held)
    found = entries(packed, owner, held, half)
    found += entries(came, owner ^ BITS[h][0], held, half)
    if len(send.shape) == 2:
        send[2 * count * half :] = jnp.zeros((LABELS, send.shape[1]), BF16)
    for j in range(count):
        label = label_of(labels, held, half, j)
        if len(send.shape) == 4:
            copy_if(label, found, send.at[j])
            continue
        for name, message, real, imag in found:

            @pl.when(label == name)
            def _(j=j, message=message, real=real, imag=imag):
                send[2 * j * half : (2 * j + 1) * half] = message[real : real + half]
                send[(2 * j + 1) * half : (2 * j + 2) * half] = message[imag : imag + half]


def near_kernel(held, packed_0, packed_1, came_0, came_1, picked_0, picked_1, near, *each):
    owner = lax.axis_index("kp")
    packed, came, picked = (packed_0, packed_1), (came_0, came_1), (picked_0, picked_1)
    half = picked_1.shape[2]
    for j in range(near.shape[0]):
        label = label_of(packed_0, held, half, j)
        for h in range(2):
            out = near.at[j, :, h * half : (h + 1) * half]
            found = entries(packed[h], owner, held, half)
            found += entries(came[h], owner ^ BITS[h][0], held, half)
            hit = copy_if(label, found, out)

            @pl.when(jnp.logical_not(hit))
            def _(h=h, j=j, out=out):
                if len(picked[h].shape) == 4:
                    out[...] = picked[h][j]
                else:
                    out[0] = picked[h][2 * j * half : (2 * j + 1) * half]
                    out[1] = picked[h][(2 * j + 1) * half : (2 * j + 2) * half]

    for j, out in enumerate(each):
        out[...] = near[j]


def stack_kernel(*refs):
    for i, ref in enumerate(refs[:-1]):
        refs[-1][i] = ref[...]


def left_over(n_kp, held, transfers, count):
    most = []
    for first, second in BITS:
        worst = 0
        for owner in range(n_kp):
            side = {who * held + k for who in (owner ^ second, owner ^ second ^ first) for k in range(held)}
            rows = range(n_kp * held - transfers * (owner + 1) + 1)
            for chosen in itertools.product(rows, repeat=count):
                need = {r + owner * transfers + s for r in chosen for s in range(transfers)}
                worst = max(worst, len((need & side) - set(chosen)))
        most.append(max(worst, 1))
    return most


def slots(labels, rows, owner, transfers):
    found, place = [], jnp.int32(0)
    for label in labels:
        need, sent = jnp.bool_(False), jnp.bool_(False)
        for row in rows:
            first = row + owner * transfers
            need = need | ((label >= first) & (label < first + transfers))
            sent = sent | (label == row)
        need = need & jnp.logical_not(sent)
        found.append((need, place))
        place = place + need.astype(jnp.int32)
    return found


def rest_kernel(held, transfers, count, packed_0, packed_1, came_0, came_1, *sends):
    owner = lax.axis_index("kp")
    packed, came = (packed_0, packed_1), (came_0, came_1)
    for h in range(2):
        first, second = BITS[h]
        room, _, half, _ = sends[h].shape
        found = entries(packed[h], owner, held, half)
        found += entries(came[h], owner ^ first, held, half)
        rows = [label_of(came[1 - h], held, half, j) for j in range(count)]
        places = slots([label for label, *_ in found], rows, owner ^ second, transfers)
        for (_, message, real, imag), (need, place) in zip(found, places):
            for i in range(room):

                @pl.when(need & (place == i))
                def _(h=h, i=i, message=message, real=real, imag=imag, half=half):
                    sends[h][i, 0] = message[real : real + half]
                    sends[h][i, 1] = message[imag : imag + half]


def far_kernel(
    held, j, count, packed_0, packed_1, came_0, came_1, picked_0, picked_1, rest_0, rest_1, far
):
    owner = lax.axis_index("kp")
    packed, came = (packed_0, packed_1), (came_0, came_1)
    picked, rest = (picked_0, picked_1), (rest_0, rest_1)
    transfers, _, g_local, _ = far.shape
    half = g_local // 2
    rows = [label_of(packed_0, held, half, j) for j in range(count)]
    for h in range(2):
        first, second = BITS[h]
        found = entries(packed[h], owner, held, half)
        found += entries(came[h], owner ^ first, held, half)
        side = [
            who * held + k for who in (owner ^ second, owner ^ second ^ first) for k in range(held)
        ]
        places = slots(side, rows, owner, transfers)
        for s in range(transfers):
            label = rows[j] + owner * transfers + s
            out = far.at[s, :, h * half : (h + 1) * half]
            hit = copy_if(label, found, out)
            for i in range(count):
                match = (label == rows[i]) & jnp.logical_not(hit)
                hit = hit | match

                @pl.when(match)
                def _(h=h, i=i, out=out):
                    out[...] = picked[h][i]

            for name, (need, place) in zip(side, places):
                for i in range(rest[h].shape[0]):

                    @pl.when((label == name) & need & (place == i))
                    def _(h=h, i=i, out=out):
                        out[...] = rest[h][i]


def load_kernel(source, panels, sems):
    copies = []
    for s in range(source.shape[0]):
        for part in range(2):
            copy = pltpu.make_async_copy(source.at[s, part], panels.at[s, part], sems.at[2 * s + part])
            copy.start()
            copies.append(copy)
    for copy in copies:
        copy.wait()


FORTH = (1, 3, 0, 2)
BACK = (2, 0, 3, 1)


def chip_at(z, steps):
    if steps == 1:
        return jnp.where(z < 2, 2 * z + 1, 2 * z - 4)
    if steps == -1:
        return jnp.where(lax.rem(z, 2) == 0, 2 + z // 2, z // 2)
    return z if steps == 0 else 3 - z


def lay(terms, upper, lower):
    for ref, first in terms:
        *count, _, g_local, t = ref.shape
        rows = pl.ds(first if isinstance(first, int) else pl.multiple_of(first, 128), g_local)
        for j, panel in enumerate([ref.at[j] for j in range(count[0])] if count else [ref]):
            real, imag = slice(2 * j * t, (2 * j + 1) * t), slice((2 * j + 1) * t, (2 * j + 2) * t)
            upper[rows, real] = panel[0]
            upper[rows, imag] = panel[1]
            lower[rows, real] = -panel[1]
            lower[rows, imag] = panel[0]


def place():
    slot = lax.axis_index("ga")
    return slot // 2, lax.rem(slot, 2)


def multiply(screened, s, span, width, upper, lower, first=0):
    span = pl.ds(pl.multiple_of(span, 128), width)
    rows = slice(first, first + width)
    return dot(screened[s, 0, :, span], upper[rows]) + dot(screened[s, 1, :, span], lower[rows])


def first_kernel(screened, own, coulomb, total, upper, lower):
    z, core = place()
    g = screened.shape[2]
    lay([(own, 0)], upper, lower)
    span = pl.ds(pl.multiple_of((2 * z + core) * g, 128), g)
    line = lax.broadcasted_iota(jnp.int32, (g, g), 0)
    on = line == lax.broadcasted_iota(jnp.int32, (g, g), 1)
    for s in range(screened.shape[0]):
        real = screened[s, 0, :, span]
        real = jnp.where(on, (real.astype(F32) - 2.0 * coulomb[...]).astype(BF16), real)
        total[s] = dot(real, upper[...]) + dot(screened[s, 1, :, span], lower[...])


def step_kernel(steps, screened, own, pair, before, total, upper, lower):
    z, core = place()
    g = screened.shape[2]
    lay([(own, core * g), (pair, (1 - core) * g)], upper, lower)
    span = 2 * chip_at(z, steps) * g
    for s in range(screened.shape[0]):
        total[s] = before[s] + multiply(screened, s, span, 2 * g, upper, lower)


def second_kernel(steps, screened, own, pairs, before, total, upper, lower):
    z, core = place()
    g = screened.shape[2]
    lay([(own, core * g), (pairs.at[1], (1 - core) * g), (pairs.at[0], 2 * g)], upper, lower)
    span = 2 * chip_at(z, steps) * g
    left = (2 * z + 1 - core) * g
    for s in range(screened.shape[0]):
        value = before[s] + multiply(screened, s, span, 2 * g, upper, lower)
        total[s] = value + multiply(screened, s, left, g, upper, lower, 2 * g)


def image_kernel(steps, j, screened, own, pair_real, pair_imag, before, image, upper, lower):
    z, core = place()
    g = screened.shape[2]
    t = own.shape[2]
    lay([(own, core * g)], upper, lower)
    rows = pl.ds(pl.multiple_of((1 - core) * g, 128), g)
    upper[rows, :t] = pair_real[...]
    upper[rows, t:] = pair_imag[...]
    lower[rows, :t] = -pair_imag[...]
    lower[rows, t:] = pair_real[...]
    span = 2 * chip_at(z, steps) * g
    for s in range(screened.shape[0]):
        value = before[s, :, 2 * j * t : 2 * (j + 1) * t]
        image[s] = (value + multiply(screened, s, span, 2 * g, upper, lower)).astype(BF16)


def mirror_kernel(chips, image, far, keep, *gives):
    first = lax.rem(lax.axis_index("ga"), 2) == 0
    t = far.shape[-1]
    for s in range(image.shape[0]):
        by_real, by_imag = tdot(far[s, 0], image[s]), tdot(far[s, 1], image[s])
        real = by_real[:, :t] + by_imag[:, t:]
        imag = by_real[:, t:] - by_imag[:, :t]
        parts = ((real, imag), (real.T, -imag.T))
        for which in range(2):
            for part in range(2):
                block = parts[which][part]
                block = block.reshape(chips, 2, t // (2 * chips), t)
                keep[:, s, which, part] = jnp.where(first, block[:, 0], block[:, 1])
                give = jnp.where(first, block[:, 1], block[:, 0])
                gives[2 * s + which][:, part] = give.astype(BF16)


def split_kernel(near, keep, *refs):
    transfers, _, _, rows, t = keep.shape[1:]
    came, (own, cross, *sends) = refs[: 2 * transfers], refs[2 * transfers :]
    z = lax.axis_index("ga") // 2
    for s in range(transfers):
        for which in range(2):

            def chip(at):
                return keep[at, s, which] + came[2 * s + which][at].astype(F32)

            own[s, which] = chip(z)
            cross[s, which] = chip(z ^ 3 ^ near)
            for i, at in enumerate((z ^ near, z ^ 3)):
                share = chip(at).astype(BF16)
                if len(sends) == 2:
                    sends[i][s, which] = share
                else:
                    first = ((i * transfers + s) * 2 + which) * 2 * rows
                    sends[0][first : first + 2 * rows] = share.reshape(2 * rows, t)
    if len(sends) == 1:
        rest = sends[0].shape[0] - 8 * transfers * rows
        sends[0][8 * transfers * rows :] = jnp.zeros((rest, t), BF16)


def merge_kernel(own, cross, *refs):
    *came, total, sends = refs
    transfers, _, _, rows, t = own.shape
    for s in range(transfers):
        for which in range(2):
            shares = []
            for i in range(2):
                if len(came) == 2:
                    share = came[i][s, which]
                else:
                    first = ((i * transfers + s) * 2 + which) * 2 * rows
                    share = came[0][first : first + 2 * rows].reshape(2, rows, t)
                shares.append(share.astype(F32))
            total[s, which] = own[s, which] + shares[0]
            share = (cross[s, which] + shares[1]).astype(BF16)
            if len(sends.shape) > 2:
                sends[s, which] = share
            else:
                first = (2 * s + which) * 2 * rows
                sends[first : first + 2 * rows] = share.reshape(2 * rows, t)
    if len(sends.shape) == 2:
        rest = sends.shape[0] - 4 * transfers * rows
        sends[4 * transfers * rows :] = jnp.zeros((rest, t), BF16)


def finish_kernel(count, scale, *refs):
    kernel, mirror = refs[-2:]
    for j in range(count):
        own, came = refs[2 * j : 2 * j + 2]
        transfers, _, _, rows, t = own.shape
        for s in range(transfers):
            for which, out in enumerate((mirror, kernel)):
                first = (2 * s + which) * 2 * rows
                if len(came.shape) > 2:
                    share = came[s, which]
                else:
                    share = came[first : first + 2 * rows].reshape(2, rows, t)
                out[j, s] = (own[s, which] + share.astype(F32)) * scale


def quick(n_kp, n_ga, densities, screened, coulomb, block_rows):
    held, _, g_local, t = densities.shape
    transfers, g_total = screened.shape[0], screened.shape[3]
    count = block_rows.shape[1]
    chips = n_ga // 2
    half = g_local // 2
    shape = jax.ShapeDtypeStruct
    tie = lax.optimization_barrier

    def across(x, bit):
        return lax.ppermute(x, "kp", [(i, i ^ bit) for i in range(n_kp)])

    def other_core(x):
        return lax.ppermute(x, "ga", [(i, i ^ 1) for i in range(n_ga)])

    def along(x, chips_on):
        return lax.ppermute(x, "ga", [(i, 2 * chips_on[i // 2] + i % 2) for i in range(n_ga)])

    message = shape((2 * held * half + LABELS, t), BF16)

    sums = shape((transfers, g_local, 2 * count * t), F32)

    def product(body, terms, *args):
        return run(
            body,
            sums,
            screened,
            *args,
            scratch=[pltpu.VMEM((terms * g_local, 2 * count * t), BF16)] * 2,
            aliases={} if terms == 1 else {3: 0},
            name="product",
            mib=24,
        )

    def pick(packed, came):
        sends = run(
            functools.partial(pick_kernel, held),
            [shape((count, 2, half, t), BF16)] * 2,
            *packed,
            *came,
            name="pick",
        )
        return [across(sends[h], BITS[h][1]) for h in range(2)]

    slices = shape((count, 2, g_local, t), BF16)

    def near_of(packed, came, picked, apart=False):
        kernel = functools.partial(near_kernel, held)
        outs = [slices] + [shape(slices.shape[1:], BF16)] * (count if apart else 0)
        near, *each = run(kernel, outs, *packed, *came, *picked, name="near")
        return (near, each) if apart else near

    packed = run(
        pack_kernel, [message] * 2, block_rows, densities, specs=[SMEM, VMEM], name="pack", mib=53
    )
    packed_before = [along(x, FORTH) for x in packed]
    came = [across(packed[h], BITS[h][0]) for h in range(2)]
    source, packed = tie((screened, packed))
    screened = run(
        load_kernel,
        shape(screened.shape, screened.dtype),
        source,
        specs=[HBM],
        scratch=[pltpu.SemaphoreType.DMA((2 * transfers,))],
        name="load",
        mib=40,
    )
    came, screened = tie((came, screened))
    picked = pick(packed, came)
    rest_sends = run(
        functools.partial(rest_kernel, held, transfers, count),
        [shape((room, 2, half, t), BF16) for room in left_over(n_kp, held, transfers, count)],
        *packed,
        *came,
        name="rest",
    )
    picked = list(tie((picked, (packed_before, rest_sends)))[0])
    near = near_of(packed, came, picked)
    ahead = along(near, BACK)
    total = product(first_kernel, 1, near, coulomb[None, :])

    came_before = [across(packed_before[h], BITS[h][0]) for h in range(2)]
    picked_before, sent = [None, None], total
    for h in range(2):
        came_h, _ = tie((came_before[h], sent))
        sent = run(
            functools.partial(pick_half_kernel, held, count, h),
            shape((count, 2, half, t) if h else (2 * count * half + LABELS, t), BF16),
            packed_before[h],
            came_h,
            came[1 - h],
            name="pick_half",
        )
        picked_before[h] = across(sent, BITS[h][1])
    near_before, before_each = near_of(packed_before, came_before, picked_before, True)
    behind = [along(x, FORTH) for x in before_each]

    rest_sends, ahead, _ = tie((rest_sends, ahead, near_before))
    rest = [across(rest_sends[h], BITS[h][1]) for h in range(2)]

    stack, _ = tie(((near, near_before), ahead))
    both = run(stack_kernel, shape((2, *slices.shape), BF16), *stack, name="stack")
    total = product(
        functools.partial(step_kernel, 1), 2, ahead, other_core(ahead), total
    )
    total = product(
        functools.partial(second_kernel, -1), 3, near_before, other_core(both), total
    )
    behind[0], _ = tie((behind[0], total))
    parts = shape((chips, transfers, 2, 2, t // n_ga, t), F32)
    part = parts.shape[1:]
    stages = []
    done = total
    for j in range(count):
        total, _ = tie((total, done))
        image = run(
            functools.partial(image_kernel, -2, j),
            shape((transfers, g_local, 2 * t), BF16),
            screened,
            behind[j],
            *[other_core(behind[j][part]) for part in range(2)],
            total,
            scratch=[pltpu.VMEM((2 * g_local, 2 * t), BF16)] * 2,
            name="image",
            mib=24,
        )
        rest, _ = tie((rest, image if j == 0 else done))
        far = run(
            functools.partial(far_kernel, held, j, count),
            shape((transfers, 2, g_local, t), BF16),
            *packed,
            *came,
            *picked,
            *rest,
            name="far",
        )
        keep, *gives = run(
            functools.partial(mirror_kernel, chips),
            [parts] + [shape((chips, 2, t // n_ga, t), BF16)] * (2 * transfers),
            image,
            far,
            name="mirror",
            mib=24,
        )
        near_z = 1
        own, cross, *sends = run(
            functools.partial(split_kernel, near_z),
            [shape(part, F32)] * 2 + ([shape(part, BF16)] * 2 if j else [shape((8 * transfers * part[3] + 16, t), BF16)]),
            keep,
            *[other_core(x) for x in gives],
            name="split",
        )
        done = own
        came_j = [lax.ppermute(x, "ga", [(i, i ^ (2 * near_z)) for i in range(n_ga)]) for x in sends]
        stages.append((own, cross, came_j, 3 - near_z))
    groups = []
    for own, cross, came_j, far_z in stages:
        if groups:
            came_j, _ = tie((came_j, sends))
        own, sends = run(
            merge_kernel,
            [
                shape(part, F32),
                shape(part, BF16) if groups else shape((4 * transfers * part[3] + 16, t), BF16),
            ],
            own,
            cross,
            *came_j,
            name="merge",
        )
        groups += [own, lax.ppermute(sends, "ga", [(i, i ^ (2 * far_z)) for i in range(n_ga)])]
    result = shape((count, transfers, 2, t // n_ga, t), F32)
    return tuple(
        run(
            functools.partial(finish_kernel, count, -1.0 / math.sqrt(g_total)),
            [result] * 2,
            *groups,
            name="finish",
        )
    )


def plain(densities, screened, coulomb, block_rows):
    owner = lax.axis_index("kp")
    g_slot = lax.axis_index("ga")
    k_held = densities.shape[0]
    g_local = densities.shape[2]
    g_total = screened.shape[3]
    rows = block_rows[0]
    transfers = owner * k_held + jnp.arange(k_held, dtype=jnp.int32)
    far_rows = rows[:, None] + transfers[None, :]
    piece = lax.all_gather(densities, "kp", axis=0, tiled=True)
    labels = jnp.arange(piece.shape[0], dtype=jnp.int32)
    pick_near = (rows[:, None] == labels[None, :]).astype(jnp.bfloat16)
    pick_far = (far_rows[:, :, None] == labels[None, None, :]).astype(jnp.bfloat16)
    near_acc = jnp.einsum(
        "jp,pcgt->jcgt", pick_near, piece, preferred_element_type=jnp.float32
    ).astype(jnp.bfloat16)
    far_acc = jnp.einsum(
        "jsp,pcgt->jscgt", pick_far, piece, preferred_element_type=jnp.float32
    ).astype(jnp.bfloat16)
    columns = jnp.arange(g_total, dtype=jnp.int32)
    own_rows = g_slot * g_local + jnp.arange(g_local, dtype=jnp.int32)
    diag_mask = own_rows[:, None] == columns[None, :]
    coulomb_diag = jnp.where(diag_mask, 2.0 * coulomb[:, None], 0.0)
    screen_real = (coulomb_diag[None] - screened[:, 0].astype(jnp.float32)).astype(jnp.bfloat16)
    screen_imag = -screened[:, 1]
    near_all = lax.all_gather(near_acc, "ga", axis=2, tiled=True)
    piece_real = near_all[:, 0]
    piece_imag = near_all[:, 1]
    real_term = jnp.einsum(
        "sgh,jht->jsgt", screen_real, piece_real, preferred_element_type=jnp.float32
    ) - jnp.einsum("sgh,jht->jsgt", screen_imag, piece_imag, preferred_element_type=jnp.float32)
    imag_term = jnp.einsum(
        "sgh,jht->jsgt", screen_real, piece_imag, preferred_element_type=jnp.float32
    ) + jnp.einsum("sgh,jht->jsgt", screen_imag, piece_real, preferred_element_type=jnp.float32)
    image = jnp.stack([real_term, imag_term], 2)
    image = image.astype(jnp.bfloat16)
    image_real = image[:, :, 0]
    image_imag = image[:, :, 1]
    far_real = far_acc[:, :, 0]
    far_imag = far_acc[:, :, 1]
    lower_real = jnp.einsum(
        "jsga,jsgb->jsab", far_real, image_real, preferred_element_type=jnp.float32
    ) + jnp.einsum("jsga,jsgb->jsab", far_imag, image_imag, preferred_element_type=jnp.float32)
    lower_imag = jnp.einsum(
        "jsga,jsgb->jsab", far_real, image_imag, preferred_element_type=jnp.float32
    ) - jnp.einsum("jsga,jsgb->jsab", far_imag, image_real, preferred_element_type=jnp.float32)
    partial_lower = jnp.stack([lower_real, lower_imag], 2)
    inverse = 1.0 / math.sqrt(g_total)
    mirror = lax.psum_scatter(partial_lower, "ga", scatter_dimension=3, tiled=True) * inverse
    partial_upper = jnp.stack([jnp.swapaxes(lower_real, 2, 3), -jnp.swapaxes(lower_imag, 2, 3)], 2)
    kernel = lax.psum_scatter(partial_upper, "ga", scatter_dimension=3, tiled=True) * inverse
    return (kernel, mirror)


def solution(mesh):
    placed = (P("kp", None, "ga", None), P("kp", None, "ga", None), P("ga"), P("kp", None))
    n_kp, n_ga = mesh.shape["kp"], mesh.shape["ga"]

    def shards(densities, screened, coulomb, block_rows):
        g_local, t = densities.shape[2], densities.shape[3]
        fits = n_kp == 2 * 2 and n_ga == 4 * 2
        fits = fits and g_local % 128 == 0 and t % (8 * n_ga) == 0
        fits = fits and n_kp * densities.shape[0] <= 256
        if fits:
            return quick(n_kp, n_ga, densities, screened, coulomb, block_rows)
        return plain(densities, screened, coulomb, block_rows)

    return jax.shard_map(
        shards,
        mesh=mesh,
        in_specs=placed,
        out_specs=(P("kp", None, None, "ga", None), P("kp", None, None, "ga", None)),
        check_vma=False,
    )
```

```python
import functools
import itertools
import math

import jax
import jax.numpy as jnp
from jax import lax
from jax.experimental import pallas as pl
from jax.experimental.pallas import tpu as pltpu
from jax.sharding import PartitionSpec as P

F32 = jnp.float32
BF16 = jnp.bfloat16
LABELS = 16
VMEM = pl.BlockSpec(memory_space=pltpu.VMEM)
SMEM = pl.BlockSpec(memory_space=pltpu.SMEM)
HBM = pl.BlockSpec(memory_space=pltpu.HBM)


def dot(a, b):
    return jnp.dot(a, b, preferred_element_type=F32)


def tdot(a, b):
    return lax.dot_general(a, b, (((0,), (0,)), ((), ())), preferred_element_type=F32)


def run(body, out, *args, specs=None, scratch=(), name=None, aliases=None, mib=16):
    outs = out if isinstance(out, (list, tuple)) else [out]
    result = pl.pallas_call(
        body,
        in_specs=specs or [VMEM] * len(args),
        out_specs=[VMEM] * len(outs),
        out_shape=list(outs),
        scratch_shapes=list(scratch),
        input_output_aliases=aliases or {},
        compiler_params=pltpu.CompilerParams(vmem_limit_bytes=mib * 2**20),
        cost_estimate=pl.CostEstimate(flops=0, bytes_accessed=0, transcendentals=0),
        name=name,
    )(*args)
    return list(result) if isinstance(out, (list, tuple)) else result[0]


BITS = ((1, 2), (2, 1))


def pack_kernel(rows, densities, *sends):
    held, _, g_local, t = densities.shape
    half = g_local // 2
    for h in range(2):
        for k in range(held):
            for part in range(2):
                at = (2 * k + part) * half
                sends[h][at : at + half] = densities[k, part, h * half : (h + 1) * half]
        line = lax.broadcasted_iota(jnp.int32, (LABELS, t), 0)
        tile = jnp.zeros((LABELS, t), F32)
        for j in range(rows.shape[1]):
            tile = jnp.where(line == j, rows[0, j].astype(F32), tile)
        sends[h][2 * held * half :] = tile.astype(BF16)


def label_of(message, held, half, j):
    tail = message[2 * held * half :].astype(F32)
    return jnp.max(tail[j : j + 1]).astype(jnp.int32)


def entries(message, owner, held, half):
    return [(owner * held + k, message, 2 * k * half, (2 * k + 1) * half) for k in range(held)]


def copy_if(label, found, out):
    half = out.shape[1]
    hit = None
    for name, message, real, imag in found:
        match = label == name
        hit = match if hit is None else hit | match

        @pl.when(match)
        def _(message=message, real=real, imag=imag):
            out[0] = message[real : real + half]
            out[1] = message[imag : imag + half]

    return hit


def pick_kernel(held, packed_0, packed_1, came_0, came_1, *sends):
    owner = lax.axis_index("kp")
    packed, came = (packed_0, packed_1), (came_0, came_1)
    half = sends[0].shape[2]
    for j in range(sends[0].shape[0]):
        for h in range(2):
            found = entries(packed[h], owner, held, half)
            found += entries(came[h], owner ^ BITS[h][0], held, half)
            copy_if(label_of(came[1 - h], held, half, j), found, sends[h].at[j])


def pick_half_kernel(held, count, h, packed, came, labels, send):
    owner = lax.axis_index("kp")
    half = (packed.shape[0] - LABELS) // (2 * held)
    found = entries(packed, owner, held, half)
    found += entries(came, owner ^ BITS[h][0], held, half)
    if len(send.shape) == 2:
        send[2 * count * half :] = jnp.zeros((LABELS, send.shape[1]), BF16)
    for j in range(count):
        label = label_of(labels, held, half, j)
        if len(send.shape) == 4:
            copy_if(label, found, send.at[j])
            continue
        for name, message, real, imag in found:

            @pl.when(label == name)
            def _(j=j, message=message, real=real, imag=imag):
                send[2 * j * half : (2 * j + 1) * half] = message[real : real + half]
                send[(2 * j + 1) * half : (2 * j + 2) * half] = message[imag : imag + half]


def near_kernel(held, packed_0, packed_1, came_0, came_1, picked_0, picked_1, near, *each):
    owner = lax.axis_index("kp")
    packed, came, picked = (packed_0, packed_1), (came_0, came_1), (picked_0, picked_1)
    half = picked_1.shape[2]
    for j in range(near.shape[0]):
        label = label_of(packed_0, held, half, j)
        for h in range(2):
            out = near.at[j, :, h * half : (h + 1) * half]
            found = entries(packed[h], owner, held, half)
            found += entries(came[h], owner ^ BITS[h][0], held, half)
            hit = copy_if(label, found, out)

            @pl.when(jnp.logical_not(hit))
            def _(h=h, j=j, out=out):
                if len(picked[h].shape) == 4:
                    out[...] = picked[h][j]
                else:
                    out[0] = picked[h][2 * j * half : (2 * j + 1) * half]
                    out[1] = picked[h][(2 * j + 1) * half : (2 * j + 2) * half]

    for j, out in enumerate(each):
        out[...] = near[j]


def stack_kernel(*refs):
    for i, ref in enumerate(refs[:-1]):
        refs[-1][i] = ref[...]


def left_over(n_kp, held, transfers, count):
    most = []
    for first, second in BITS:
        worst = 0
        for owner in range(n_kp):
            side = {who * held + k for who in (owner ^ second, owner ^ second ^ first) for k in range(held)}
            rows = range(n_kp * held - transfers * (owner + 1) + 1)
            for chosen in itertools.product(rows, repeat=count):
                need = {r + owner * transfers + s for r in chosen for s in range(transfers)}
                worst = max(worst, len((need & side) - set(chosen)))
        most.append(max(worst, 1))
    return most


def slots(labels, rows, owner, transfers):
    found, place = [], jnp.int32(0)
    for label in labels:
        need, sent = jnp.bool_(False), jnp.bool_(False)
        for row in rows:
            first = row + owner * transfers
            need = need | ((label >= first) & (label < first + transfers))
            sent = sent | (label == row)
        need = need & jnp.logical_not(sent)
        found.append((need, place))
        place = place + need.astype(jnp.int32)
    return found


def rest_kernel(held, transfers, count, packed_0, packed_1, came_0, came_1, *sends):
    owner = lax.axis_index("kp")
    packed, came = (packed_0, packed_1), (came_0, came_1)
    for h in range(2):
        first, second = BITS[h]
        room, _, half, _ = sends[h].shape
        found = entries(packed[h], owner, held, half)
        found += entries(came[h], owner ^ first, held, half)
        rows = [label_of(came[1 - h], held, half, j) for j in range(count)]
        places = slots([label for label, *_ in found], rows, owner ^ second, transfers)
        for (_, message, real, imag), (need, place) in zip(found, places):
            for i in range(room):

                @pl.when(need & (place == i))
                def _(h=h, i=i, message=message, real=real, imag=imag, half=half):
                    sends[h][i, 0] = message[real : real + half]
                    sends[h][i, 1] = message[imag : imag + half]


def far_kernel(
    held, j, count, packed_0, packed_1, came_0, came_1, picked_0, picked_1, rest_0, rest_1, far
):
    owner = lax.axis_index("kp")
    packed, came = (packed_0, packed_1), (came_0, came_1)
    picked, rest = (picked_0, picked_1), (rest_0, rest_1)
    transfers, _, g_local, _ = far.shape
    half = g_local // 2
    rows = [label_of(packed_0, held, half, j) for j in range(count)]
    for h in range(2):
        first, second = BITS[h]
        found = entries(packed[h], owner, held, half)
        found += entries(came[h], owner ^ first, held, half)
        side = [
            who * held + k for who in (owner ^ second, owner ^ second ^ first) for k in range(held)
        ]
        places = slots(side, rows, owner, transfers)
        for s in range(transfers):
            label = rows[j] + owner * transfers + s
            out = far.at[s, :, h * half : (h + 1) * half]
            hit = copy_if(label, found, out)
            for i in range(count):
                match = (label == rows[i]) & jnp.logical_not(hit)
                hit = hit | match

                @pl.when(match)
                def _(h=h, i=i, out=out):
                    out[...] = picked[h][i]

            for name, (need, place) in zip(side, places):
                for i in range(rest[h].shape[0]):

                    @pl.when((label == name) & need & (place == i))
                    def _(h=h, i=i, out=out):
                        out[...] = rest[h][i]


def load_kernel(source, panels, sems):
    copies = []
    for s in range(source.shape[0]):
        for part in range(2):
            copy = pltpu.make_async_copy(source.at[s, part], panels.at[s, part], sems.at[2 * s + part])
            copy.start()
            copies.append(copy)
    for copy in copies:
        copy.wait()


FORTH = (1, 3, 0, 2)
BACK = (2, 0, 3, 1)


def chip_at(z, steps):
    if steps == 1:
        return jnp.where(z < 2, 2 * z + 1, 2 * z - 4)
    if steps == -1:
        return jnp.where(lax.rem(z, 2) == 0, 2 + z // 2, z // 2)
    return z if steps == 0 else 3 - z


def lay(terms, upper, lower):
    for ref, first in terms:
        *count, _, g_local, t = ref.shape
        rows = pl.ds(first if isinstance(first, int) else pl.multiple_of(first, 128), g_local)
        for j, panel in enumerate([ref.at[j] for j in range(count[0])] if count else [ref]):
            real, imag = slice(2 * j * t, (2 * j + 1) * t), slice((2 * j + 1) * t, (2 * j + 2) * t)
            upper[rows, real] = panel[0]
            upper[rows, imag] = panel[1]
            lower[rows, real] = -panel[1]
            lower[rows, imag] = panel[0]


def place():
    slot = lax.axis_index("ga")
    return slot // 2, lax.rem(slot, 2)


def multiply(screened, s, span, width, upper, lower, first=0):
    span = pl.ds(pl.multiple_of(span, 128), width)
    rows = slice(first, first + width)
    return dot(screened[s, 0, :, span], upper[rows]) + dot(screened[s, 1, :, span], lower[rows])


def first_kernel(screened, own, coulomb, total, upper, lower):
    z, core = place()
    g = screened.shape[2]
    lay([(own, 0)], upper, lower)
    span = pl.ds(pl.multiple_of((2 * z + core) * g, 128), g)
    line = lax.broadcasted_iota(jnp.int32, (g, g), 0)
    on = line == lax.broadcasted_iota(jnp.int32, (g, g), 1)
    for s in range(screened.shape[0]):
        real = screened[s, 0, :, span]
        real = jnp.where(on, (real.astype(F32) - 2.0 * coulomb[...]).astype(BF16), real)
        total[s] = dot(real, upper[...]) + dot(screened[s, 1, :, span], lower[...])


def step_kernel(steps, screened, own, pair, before, total, upper, lower):
    z, core = place()
    g = screened.shape[2]
    lay([(own, core * g), (pair, (1 - core) * g)], upper, lower)
    span = 2 * chip_at(z, steps) * g
    for s in range(screened.shape[0]):
        total[s] = before[s] + multiply(screened, s, span, 2 * g, upper, lower)


def second_kernel(steps, screened, own, pairs, before, total, upper, lower):
    z, core = place()
    g = screened.shape[2]
    lay([(own, core * g), (pairs.at[1], (1 - core) * g), (pairs.at[0], 2 * g)], upper, lower)
    span = 2 * chip_at(z, steps) * g
    left = (2 * z + 1 - core) * g
    for s in range(screened.shape[0]):
        value = before[s] + multiply(screened, s, span, 2 * g, upper, lower)
        total[s] = value + multiply(screened, s, left, g, upper, lower, 2 * g)


def image_kernel(steps, j, screened, own, pair_real, pair_imag, before, image, upper, lower):
    z, core = place()
    g = screened.shape[2]
    t = own.shape[2]
    lay([(own, core * g)], upper, lower)
    rows = pl.ds(pl.multiple_of((1 - core) * g, 128), g)
    upper[rows, :t] = pair_real[...]
    upper[rows, t:] = pair_imag[...]
    lower[rows, :t] = -pair_imag[...]
    lower[rows, t:] = pair_real[...]
    span = 2 * chip_at(z, steps) * g
    for s in range(screened.shape[0]):
        value = before[s, :, 2 * j * t : 2 * (j + 1) * t]
        image[s] = (value + multiply(screened, s, span, 2 * g, upper, lower)).astype(BF16)


def mirror_kernel(chips, image, far, keep, *gives):
    first = lax.rem(lax.axis_index("ga"), 2) == 0
    t = far.shape[-1]
    for s in range(image.shape[0]):
        by_real, by_imag = tdot(far[s, 0], image[s]), tdot(far[s, 1], image[s])
        real = by_real[:, :t] + by_imag[:, t:]
        imag = by_real[:, t:] - by_imag[:, :t]
        parts = ((real, imag), (real.T, -imag.T))
        for which in range(2):
            for part in range(2):
                block = parts[which][part]
                block = block.reshape(chips, 2, t // (2 * chips), t)
                keep[:, s, which, part] = jnp.where(first, block[:, 0], block[:, 1])
                give = jnp.where(first, block[:, 1], block[:, 0])
                if len(gives) == 2:
                    gives[which][:, s, part] = give.astype(BF16)
                else:
                    gives[2 * s + which][:, part] = give.astype(BF16)


def split_kernel(keep, *refs):
    *came, own, cross, sends = refs
    z = lax.axis_index("ga") // 2
    for s in range(keep.shape[1]):
        for which in range(2):

            def chip(at):
                if len(came) == 2:
                    return keep[at, s, which] + came[which][at, s].astype(F32)
                return keep[at, s, which] + came[2 * s + which][at].astype(F32)

            own[s, which] = chip(z)
            cross[s, which] = chip(z ^ 2)
            for i, at in enumerate((z ^ 1, z ^ 3)):
                sends[i, s, which] = chip(at).astype(BF16)


def merge_kernel(own, cross, came, total, sends):
    total[...] = own[...] + came[0].astype(F32)
    sends[...] = (cross[...] + came[1].astype(F32)).astype(BF16)


def finish_kernel(count, chips, scale, *refs):
    kernel, mirror = refs[-2:]
    for j in range(count):
        terms = refs[j * chips : (j + 1) * chips]
        total = terms[0][...]
        for term in terms[1:]:
            total = total + term[...].astype(F32)
        mirror[j] = total[:, 0] * scale
        kernel[j] = total[:, 1] * scale


def quick(n_kp, n_ga, densities, screened, coulomb, block_rows):
    held, _, g_local, t = densities.shape
    transfers, g_total = screened.shape[0], screened.shape[3]
    count = block_rows.shape[1]
    chips = n_ga // 2
    half = g_local // 2
    shape = jax.ShapeDtypeStruct
    tie = lax.optimization_barrier

    def across(x, bit):
        return lax.ppermute(x, "kp", [(i, i ^ bit) for i in range(n_kp)])

    def other_core(x):
        return lax.ppermute(x, "ga", [(i, i ^ 1) for i in range(n_ga)])

    def along(x, chips_on):
        return lax.ppermute(x, "ga", [(i, 2 * chips_on[i // 2] + i % 2) for i in range(n_ga)])

    message = shape((2 * held * half + LABELS, t), BF16)

    sums = shape((transfers, g_local, 2 * count * t), F32)

    def product(body, terms, *args):
        return run(
            body,
            sums,
            screened,
            *args,
            scratch=[pltpu.VMEM((terms * g_local, 2 * count * t), BF16)] * 2,
            aliases={} if terms == 1 else {3: 0},
            name="product",
            mib=24,
        )

    def pick(packed, came):
        sends = run(
            functools.partial(pick_kernel, held),
            [shape((count, 2, half, t), BF16)] * 2,
            *packed,
            *came,
            name="pick",
        )
        return [across(sends[h], BITS[h][1]) for h in range(2)]

    slices = shape((count, 2, g_local, t), BF16)

    def near_of(packed, came, picked, apart=False):
        kernel = functools.partial(near_kernel, held)
        outs = [slices] + [shape(slices.shape[1:], BF16)] * (count if apart else 0)
        near, *each = run(kernel, outs, *packed, *came, *picked, name="near")
        return (near, each) if apart else near

    packed = run(
        pack_kernel, [message] * 2, block_rows, densities, specs=[SMEM, VMEM], name="pack", mib=53
    )
    packed_before = [along(x, FORTH) for x in packed]
    came = [across(packed[h], BITS[h][0]) for h in range(2)]
    source, packed = tie((screened, packed))
    screened = run(
        load_kernel,
        shape(screened.shape, screened.dtype),
        source,
        specs=[HBM],
        scratch=[pltpu.SemaphoreType.DMA((2 * transfers,))],
        name="load",
        mib=40,
    )
    came, screened = tie((came, screened))
    picked = pick(packed, came)
    rest_sends = run(
        functools.partial(rest_kernel, held, transfers, count),
        [shape((room, 2, half, t), BF16) for room in left_over(n_kp, held, transfers, count)],
        *packed,
        *came,
        name="rest",
    )
    picked = list(tie((picked, (packed_before, rest_sends)))[0])
    near = near_of(packed, came, picked)
    ahead = along(near, BACK)
    total = product(first_kernel, 1, near, coulomb[None, :])

    came_before = [across(packed_before[h], BITS[h][0]) for h in range(2)]
    picked_before, sent = [None, None], total
    for h in range(2):
        came_h, _ = tie((came_before[h], sent))
        sent = run(
            functools.partial(pick_half_kernel, held, count, h),
            shape((count, 2, half, t) if h else (2 * count * half + LABELS, t), BF16),
            packed_before[h],
            came_h,
            came[1 - h],
            name="pick_half",
        )
        picked_before[h] = across(sent, BITS[h][1])
    near_before, before_each = near_of(packed_before, came_before, picked_before, True)
    behind = [along(x, FORTH) for x in before_each]

    rest_sends, ahead, _ = tie((rest_sends, ahead, near_before))
    rest = [across(rest_sends[h], BITS[h][1]) for h in range(2)]

    stack, _ = tie(((near, near_before), ahead))
    both = run(stack_kernel, shape((2, *slices.shape), BF16), *stack, name="stack")
    total = product(
        functools.partial(step_kernel, 1), 2, ahead, other_core(ahead), total
    )
    total = product(
        functools.partial(second_kernel, -1), 3, near_before, other_core(both), total
    )
    behind[0], _ = tie((behind[0], total))
    parts = shape((chips, transfers, 2, 2, t // n_ga, t), F32)
    part = parts.shape[1:]
    stages = []
    done = total
    for j in range(count):
        total, _ = tie((total, done))
        image = run(
            functools.partial(image_kernel, -2, j),
            shape((transfers, g_local, 2 * t), BF16),
            screened,
            behind[j],
            *[other_core(behind[j][part]) for part in range(2)],
            total,
            scratch=[pltpu.VMEM((2 * g_local, 2 * t), BF16)] * 2,
            name="image",
            mib=24,
        )
        rest, _ = tie((rest, image if j == 0 else done))
        far = run(
            functools.partial(far_kernel, held, j, count),
            shape((transfers, 2, g_local, t), BF16),
            *packed,
            *came,
            *picked,
            *rest,
            name="far",
        )
        keep, *gives = run(
            functools.partial(mirror_kernel, chips),
            [parts]
            + (
                [shape((chips, 2, t // n_ga, t), BF16)] * (2 * transfers)
                if j
                else [shape((chips, transfers, 2, t // n_ga, t), BF16)] * 2
            ),
            image,
            far,
            name="mirror",
            mib=24,
        )
        own, cross, sends = run(
            split_kernel,
            [shape(part, F32), shape(part, F32), shape((2, *part), BF16)],
            keep,
            *[other_core(x) for x in gives],
            name="split",
        )
        if j + 1 < count:
            behind[j + 1], _ = tie((behind[j + 1], keep))
        if stages:
            sends, _ = tie((sends, stages[-1][2]))
        done = own
        came_j = lax.ppermute(sends, "ga", [(i, i ^ 2) for i in range(n_ga)])
        stages.append((own, cross, came_j))
    groups = []
    for own, cross, came_j in stages:
        own, sends = run(
            merge_kernel, [shape(part, F32), shape(part, BF16)], own, cross, came_j, name="merge"
        )
        groups += [own, lax.ppermute(sends, "ga", [(i, i ^ 4) for i in range(n_ga)])]
    result = shape((count, transfers, 2, t // n_ga, t), F32)
    return tuple(
        run(
            functools.partial(finish_kernel, count, 2, -1.0 / math.sqrt(g_total)),
            [result] * 2,
            *groups,
            name="finish",
        )
    )


def plain(densities, screened, coulomb, block_rows):
    owner = lax.axis_index("kp")
    g_slot = lax.axis_index("ga")
    k_held = densities.shape[0]
    g_local = densities.shape[2]
    g_total = screened.shape[3]
    rows = block_rows[0]
    transfers = owner * k_held + jnp.arange(k_held, dtype=jnp.int32)
    far_rows = rows[:, None] + transfers[None, :]
    piece = lax.all_gather(densities, "kp", axis=0, tiled=True)
    labels = jnp.arange(piece.shape[0], dtype=jnp.int32)
    pick_near = (rows[:, None] == labels[None, :]).astype(jnp.bfloat16)
    pick_far = (far_rows[:, :, None] == labels[None, None, :]).astype(jnp.bfloat16)
    near_acc = jnp.einsum(
        "jp,pcgt->jcgt", pick_near, piece, preferred_element_type=jnp.float32
    ).astype(jnp.bfloat16)
    far_acc = jnp.einsum(
        "jsp,pcgt->jscgt", pick_far, piece, preferred_element_type=jnp.float32
    ).astype(jnp.bfloat16)
    columns = jnp.arange(g_total, dtype=jnp.int32)
    own_rows = g_slot * g_local + jnp.arange(g_local, dtype=jnp.int32)
    diag_mask = own_rows[:, None] == columns[None, :]
    coulomb_diag = jnp.where(diag_mask, 2.0 * coulomb[:, None], 0.0)
    screen_real = (coulomb_diag[None] - screened[:, 0].astype(jnp.float32)).astype(jnp.bfloat16)
    screen_imag = -screened[:, 1]
    near_all = lax.all_gather(near_acc, "ga", axis=2, tiled=True)
    piece_real = near_all[:, 0]
    piece_imag = near_all[:, 1]
    real_term = jnp.einsum(
        "sgh,jht->jsgt", screen_real, piece_real, preferred_element_type=jnp.float32
    ) - jnp.einsum("sgh,jht->jsgt", screen_imag, piece_imag, preferred_element_type=jnp.float32)
    imag_term = jnp.einsum(
        "sgh,jht->jsgt", screen_real, piece_imag, preferred_element_type=jnp.float32
    ) + jnp.einsum("sgh,jht->jsgt", screen_imag, piece_real, preferred_element_type=jnp.float32)
    image = jnp.stack([real_term, imag_term], 2)
    image = image.astype(jnp.bfloat16)
    image_real = image[:, :, 0]
    image_imag = image[:, :, 1]
    far_real = far_acc[:, :, 0]
    far_imag = far_acc[:, :, 1]
    lower_real = jnp.einsum(
        "jsga,jsgb->jsab", far_real, image_real, preferred_element_type=jnp.float32
    ) + jnp.einsum("jsga,jsgb->jsab", far_imag, image_imag, preferred_element_type=jnp.float32)
    lower_imag = jnp.einsum(
        "jsga,jsgb->jsab", far_real, image_imag, preferred_element_type=jnp.float32
    ) - jnp.einsum("jsga,jsgb->jsab", far_imag, image_real, preferred_element_type=jnp.float32)
    partial_lower = jnp.stack([lower_real, lower_imag], 2)
    inverse = 1.0 / math.sqrt(g_total)
    mirror = lax.psum_scatter(partial_lower, "ga", scatter_dimension=3, tiled=True) * inverse
    partial_upper = jnp.stack([jnp.swapaxes(lower_real, 2, 3), -jnp.swapaxes(lower_imag, 2, 3)], 2)
    kernel = lax.psum_scatter(partial_upper, "ga", scatter_dimension=3, tiled=True) * inverse
    return (kernel, mirror)


def solution(mesh):
    placed = (P("kp", None, "ga", None), P("kp", None, "ga", None), P("ga"), P("kp", None))
    n_kp, n_ga = mesh.shape["kp"], mesh.shape["ga"]

    def shards(densities, screened, coulomb, block_rows):
        g_local, t = densities.shape[2], densities.shape[3]
        fits = n_kp == 2 * 2 and n_ga == 4 * 2
        fits = fits and g_local % 128 == 0 and t % (8 * n_ga) == 0
        fits = fits and n_kp * densities.shape[0] <= 256
        if fits:
            return quick(n_kp, n_ga, densities, screened, coulomb, block_rows)
        return plain(densities, screened, coulomb, block_rows)

    return jax.shard_map(
        shards,
        mesh=mesh,
        in_specs=placed,
        out_specs=(P("kp", None, None, "ga", None), P("kp", None, None, "ga", None)),
        check_vma=False,
    )
```
